32 devices in a mesh: tile: 8 (over y, x, core), sub: 4 (over z).
Axes of the slice: x: 2, y: 2, z: 4, core: 2. Of those that a mesh axis runs over, the one named last changes fastest.
Arguments:
- right_side: float32 [8, 131072], P(None, ('tile', 'sub')), may hold values from -6 to 6
- point_order: int32 [32, 4096], P(('tile', 'sub')), may hold values from 0 to 4095, each once within a row
- noise_var: float32 [131072], P(('tile', 'sub')), may hold values from 0.1 to 1
- block_pairs: int32 [3072, 2], P(('tile', 'sub')), may hold values from -1 to 511, as said below
- pair_blocks: bfloat16 [3072, 256, 256], P(('tile', 'sub')), as said below
- diag_blocks: bfloat16 [512, 256, 256], P(('tile', 'sub')), as said below
Outputs:
- solution: float32 [8, 131072], P(None, ('tile', 'sub'))
- residual: float32 [8, 131072], P(None, ('tile', 'sub'))
The draws below stay inside these ranges and needn't reach their ends.
Inputs may be any that keep to these rules, and one draw needn't show every extreme that they name: `block_pairs`: the blocks form a grid of rows of 16 blocks in row-major order; device d (tile slowest, then sub) owns blocks 16 d to 16 d + 15, one grid row. A slot holds (r, c) with c the right, lower-left, lower or lower-right grid neighbour of r, or (-1, -1) when empty; every such neighbouring pair is held exactly once, by a device of the tile that owns r. On each device the live slots come first, and in every tile some device has all 96 slots live. pair_blocks[p] has the rows of block r and the columns of block c of block_pairs[p], and is zero for an empty slot; with diag_blocks these are the bfloat16 values of all nonzero blocks of a kernel matrix that is positive semi-definite before rounding. Each diag_blocks[q] is symmetric.
All inputs are finite; a program needn't handle non-finite values.
Results may differ from the reference program's by a relative error of at most 0.0075.
Values may be sent and summed in bfloat16 or wider, within the bound.
No kernel may reach another device: no remote copies, remote signals or barrier semaphores. Data moves between devices by JAX's collectives and lax.ppermute only.
A program may use at most 64 MiB of HBM per device.

```python
import math
import jax
import jax.numpy as jnp
from jax import lax

RHS = 8
BLOCK = 256
BLK_DEV = 16
ITERS = 3
PAIR_DEV = 96
GRID_W = 16
BLOCKS = 512
POINTS = 131072
PTS_DEV = 4096
N_SUB = 4
DEVICES = 32


AMPLITUDE = 0.0625


def point_coords(key):
    spread = jax.random.uniform(key, (BLOCKS, BLOCK, 2), jnp.float32)
    block_ids = jnp.arange(BLOCKS, dtype=jnp.int32)
    across = (block_ids % GRID_W).astype(jnp.float32)[:, None]
    downward = (block_ids // GRID_W).astype(jnp.float32)[:, None]
    return (spread[:, :, 0] + across, spread[:, :, 1] + downward)


def wendland(first_x, first_y, second_x, second_y):
    delta_x = first_x[:, None] - second_x[None, :]
    delta_y = first_y[:, None] - second_y[None, :]
    radius = jnp.sqrt(delta_x * delta_x + delta_y * delta_y)
    inside = jnp.maximum(1.0 - radius, 0.0)
    return AMPLITUDE * inside * inside * inside * inside * (4.0 * radius + 1.0)


def pair_table(key):
    tile_count = DEVICES // N_SUB
    tile_blocks = N_SUB * BLK_DEV
    slot_count = 4 * tile_blocks
    slot_ids = jnp.arange(slot_count, dtype=jnp.int32)
    kind_ids = slot_ids % 4
    row_block = jnp.arange(tile_count, dtype=jnp.int32)[:, None] * tile_blocks + (slot_ids // 4)[None, :]
    grid_row = row_block // GRID_W
    grid_col = row_block % GRID_W
    step_row = jnp.where(kind_ids == 0, 0, 1)[None, :]
    step_col = jnp.where(kind_ids == 0, 1, kind_ids - 2)[None, :]
    other_row = grid_row + step_row
    other_col = grid_col + step_col
    is_valid = (other_col >= 0) & (other_col < GRID_W) & (other_row < BLOCKS // GRID_W)
    partner = other_row * GRID_W + other_col
    score_key, rotation_key = jax.random.split(key)
    scores = jax.random.randint(score_key, (tile_count, slot_count), 0, 1 << 18)
    sort_keys = jnp.where(is_valid, scores * slot_count + slot_ids[None, :], (1 << 29) + slot_ids[None, :])
    ranked = jnp.argsort(sort_keys, axis=1).astype(jnp.int32)
    live_count = jnp.sum(is_valid.astype(jnp.int32), axis=1)
    capacity = jnp.array([12, 8, 7, 5], jnp.int32) * BLK_DEV // 2
    offsets = jnp.array([0, 12, 20, 27], jnp.int32) * BLK_DEV // 2
    rotation = jax.random.randint(rotation_key, (tile_count, 1), 0, 4)
    position = (jnp.arange(N_SUB, dtype=jnp.int32)[None, :] + rotation) % 4
    held_cap = capacity[position]
    held_start = offsets[position]
    slot_pos = jnp.arange(PAIR_DEV, dtype=jnp.int32)
    deal_index = held_start[:, :, None] + slot_pos[None, None, :]
    is_used = (slot_pos[None, None, :] < held_cap[:, :, None]) & (deal_index < live_count[:, None, None])
    picked = jnp.take_along_axis(ranked, jnp.minimum(deal_index, slot_count - 1).reshape(tile_count, -1), axis=1)
    row_ids = jnp.take_along_axis(row_block, picked, axis=1).reshape(tile_count, N_SUB, PAIR_DEV)
    col_ids = jnp.take_along_axis(partner, picked, axis=1).reshape(tile_count, N_SUB, PAIR_DEV)
    row_ids = jnp.where(is_used, row_ids, -1)
    col_ids = jnp.where(is_used, col_ids, -1)
    return jnp.stack([row_ids, col_ids], axis=-1).reshape(DEVICES * PAIR_DEV, 2).astype(jnp.int32)


def draw_block_pairs(key, part):
    return pair_table(jax.random.fold_in(key, 3))


def draw_pair_blocks(key, part):
    table = pair_table(jax.random.fold_in(key, 3))
    across, downward = point_coords(jax.random.fold_in(key, 5))
    live_flag = (table[:, 0] >= 0).astype(jnp.float32)
    first_id = jnp.maximum(table[:, 0], 0)
    second = jnp.maximum(table[:, 1], 0)

    def one_block(entry_data):
        row_id, col_id, flag_value = entry_data
        values = wendland(across[row_id], downward[row_id], across[col_id], downward[col_id])
        return (values * flag_value).astype(jnp.bfloat16)
    return lax.map(one_block, (first_id, second, live_flag))


def draw_diag_blocks(key, part):
    across, downward = point_coords(jax.random.fold_in(key, 5))

    def one_block(entry_data):
        block_x, block_y = entry_data
        return wendland(block_x, block_y, block_x, block_y).astype(jnp.bfloat16)
    return lax.map(one_block, (across, downward))


def block_scale(stream_key, shape, cuts, smallest, high):
    loudness = 1.0
    for axis_at, shards_of in cuts:
        heights = jax.random.uniform(jax.random.fold_in(jax.random.fold_in(stream_key, 6), axis_at), (shards_of,), jnp.float32, smallest / len(cuts), high / len(cuts))
        loudness = loudness * jnp.repeat(jnp.exp(heights), shape[axis_at] // shards_of).reshape((-1,) + (1,) * (len(shape) - 1 - axis_at))
    return loudness


def gaussian(key, dims, deviation, limit, shards=(), kind=jnp.bfloat16):
    loudness = block_scale(key, dims, shards, -0.22, 0.18) if shards else 1.0
    result = jax.random.normal(key, dims, jnp.float32) * deviation * loudness
    return jnp.minimum(jnp.maximum(result, -limit), limit).astype(kind)


def setup_inputs(seed: int = 0) -> dict:
    streams_of = jax.random.split(jax.random.key(seed), 7)
    return {
        "right_side": gaussian(streams_of[0], (RHS, POINTS), 1.0, 6.0, ((1, 32),), jnp.float32),
        "point_order": jax.vmap(lambda own: jax.random.permutation(own, PTS_DEV))(jax.random.split(streams_of[1], DEVICES)).reshape((DEVICES, PTS_DEV)).astype(jnp.int32),
        "noise_var": jnp.clip(jnp.exp(math.log(1.0) - 2.3025851 * jax.random.uniform(streams_of[2], (POINTS,), jnp.float32) ** block_scale(streams_of[2], (POINTS,), ((0, 32),), -0.2, 0.2)), 0.1, 1.0),
        "block_pairs": draw_block_pairs(jax.random.fold_in(streams_of[6], 71), 0),
        "pair_blocks": draw_pair_blocks(jax.random.fold_in(streams_of[6], 71), 0),
        "diag_blocks": draw_diag_blocks(jax.random.fold_in(streams_of[6], 71), 0),
    }


def apply_operator(vector, noise_var, block_pairs, pair_blocks, diag_blocks):
    rounded = lax.optimization_barrier(vector.astype(jnp.bfloat16)).astype(jnp.float32)
    by_block = rounded.reshape(RHS, BLOCKS, BLOCK)
    diag_part = jnp.einsum("bij,rbj->rbi", diag_blocks.astype(jnp.float32), by_block)
    row_ids = block_pairs[:, 0].reshape(DEVICES, PAIR_DEV)
    col_ids = block_pairs[:, 1].reshape(DEVICES, PAIR_DEV)
    kernels = pair_blocks.reshape(DEVICES, PAIR_DEV, BLOCK, BLOCK)

    def add_group(carried, group_data):
        rows_here, cols_here, kernel_here = group_data
        live_weight = (rows_here >= 0).astype(jnp.float32)[None, :, None]
        row_safe = jnp.maximum(rows_here, 0).astype(jnp.int32)
        col_safe = jnp.maximum(cols_here, 0).astype(jnp.int32)
        kernel_float = kernel_here.astype(jnp.float32)
        to_rows = jnp.einsum("pij,rpj->rpi", kernel_float, by_block[:, col_safe]) * live_weight
        to_cols = jnp.einsum("pij,rpi->rpj", kernel_float, by_block[:, row_safe]) * live_weight
        carried = carried.at[:, row_safe].add(to_rows).at[:, col_safe].add(to_cols)
        return carried, None

    start_sum = jnp.zeros((RHS, BLOCKS, BLOCK), jnp.float32)
    pair_part, unused = lax.scan(add_group, start_sum, (row_ids, col_ids, kernels))
    return (diag_part + pair_part).reshape(RHS, POINTS) + noise_var[None, :] * vector


def reference(right_side, point_order, noise_var, block_pairs, pair_blocks, diag_blocks):
    shaped = right_side.reshape(RHS, DEVICES, PTS_DEV)
    curve_rhs = jnp.take_along_axis(shaped, point_order[None, :, :], axis=2).reshape(RHS, POINTS)
    solution = jnp.zeros_like(curve_rhs)
    residual = curve_rhs
    direction = curve_rhs
    norm_now = jnp.sum(residual * residual, axis=1)
    for iteration in range(ITERS):
        image_vec = apply_operator(direction, noise_var, block_pairs, pair_blocks, diag_blocks)
        step_size = norm_now / jnp.sum(direction * image_vec, axis=1)
        solution = solution + step_size[:, None] * direction
        residual = residual - step_size[:, None] * image_vec
        if iteration + 1 < ITERS:
            norm_next = jnp.sum(residual * residual, axis=1)
            direction = residual + (norm_next / norm_now)[:, None] * direction
            norm_now = norm_next
    return solution, residual
```

```python
import functools

import jax
import jax.numpy as jnp
from jax import lax
from jax.experimental import pallas as pl
from jax.experimental.pallas import tpu as pltpu
from jax.sharding import PartitionSpec as P

ITERS = 3
LANES = 128
GROUP = 16
F32 = jnp.float32
BF16 = jnp.bfloat16
VMEM = pl.BlockSpec(memory_space=pltpu.VMEM)
SMEM = pl.BlockSpec(memory_space=pltpu.SMEM)
PARAMS = pltpu.CompilerParams(vmem_limit_bytes=16 * 1024 * 1024)


def times(field, block):
    return lax.dot_general(field, block, (((1,), (0,)), ((), ())), preferred_element_type=F32)


def times_transposed(field, block):
    return lax.dot_general(field, block, (((1,), (1,)), ((), ())), preferred_element_type=F32)


def order_kernel(right_ref, order_ref, curve_ref, rounded_ref):
    rhs_count, points = right_ref.shape
    for start in range(0, points, LANES):
        at = jnp.broadcast_to(order_ref[:, start : start + LANES], (rhs_count, LANES))
        chunk = at // LANES
        lane = at % LANES
        result = jnp.zeros((rhs_count, LANES), F32)
        for source in range(points // LANES):
            values = right_ref[:, source * LANES : (source + 1) * LANES]
            picked = jnp.take_along_axis(values, lane, axis=1)
            result = jnp.where(chunk == source, picked, result)
        curve_ref[:, start : start + LANES] = result
        rounded_ref[:, start : start + LANES] = result.astype(BF16)


def ahead_kernel(sub_count, where_ref, pairs_ref, blocks_ref, *refs):
    row_refs = refs[:sub_count]
    even_ref, odd_ref, field_ref, total = refs[sub_count:]
    sub_index, parity, live = where_ref[0], where_ref[1], where_ref[2]
    rhs_count, points_dev = even_ref.shape
    block_len = blocks_ref.shape[1]
    blocks_dev = points_dev // block_len
    tile_blocks = sub_count * blocks_dev
    for step, row_ref in enumerate(row_refs):
        first = (sub_index ^ step) * blocks_dev
        for block in range(blocks_dev):
            piece = row_ref[:, block * block_len : (block + 1) * block_len]
            field_ref[first + block] = piece.astype(F32)
    for block in range(blocks_dev):
        total[block] = jnp.zeros((rhs_count, block_len), F32)

    def one_slot(slot, carry):
        row, col = pairs_ref[2 * slot], pairs_ref[2 * slot + 1]

        @pl.when(col >= tile_blocks)
        def _():
            at = col - tile_blocks
            total[at] += times(field_ref[row].astype(BF16), blocks_ref[slot])

        return carry

    lax.fori_loop(0, live, one_slot, 0)
    is_odd = parity == 1
    for block in range(blocks_dev):
        span = slice(block * block_len, (block + 1) * block_len)
        products = total[block].astype(BF16)
        first_row = field_ref[block].astype(BF16)
        even_ref[:, span] = jnp.where(is_odd, first_row, products)
        odd_ref[:, span] = jnp.where(is_odd, products, first_row)


def product_kernel(
    sub_count, where_ref, pairs_ref, blocks_ref, diag_ref, noise_ref, own_ref, field_ref, even_ref,
    odd_ref, *refs
):
    part_refs = refs[:sub_count]
    total, ahead = refs[sub_count:]
    sub_index, parity, live = where_ref[0], where_ref[1], where_ref[2]
    rhs_count, points_dev = own_ref.shape
    block_len = blocks_ref.shape[1]
    blocks_dev = points_dev // block_len
    tile_blocks = sub_count * blocks_dev
    is_odd = parity == 1
    for block in range(tile_blocks):
        ahead[block] = field_ref[block].astype(BF16).astype(F32)
        if block >= blocks_dev:
            total[block] = jnp.zeros((rhs_count, block_len), F32)
    for block in range(blocks_dev):
        span = slice(block * block_len, (block + 1) * block_len)
        even = even_ref[:, span].astype(F32)
        odd = odd_ref[:, span].astype(F32)
        ahead[tile_blocks + block] = jnp.where(is_odd, odd, even)
        total[block] = jnp.where(is_odd, even, odd)
        total[tile_blocks + block] = jnp.zeros((rhs_count, block_len), F32)

    def one_group(group, carry):
        results = []
        for step in range(GROUP):
            slot = group * GROUP + step
            row, col = pairs_ref[2 * slot], pairs_ref[2 * slot + 1]
            block = blocks_ref[slot]
            results.append((row, times_transposed(ahead[col].astype(BF16), block)))
            results.append((col, times(ahead[row].astype(BF16), block)))
        for at, value in results:
            total[at] += value
        return carry

    lax.fori_loop(0, (live + GROUP - 1) // GROUP, one_group, 0)
    own_first = sub_index * blocks_dev
    for block in range(blocks_dev):
        span = slice(block * block_len, (block + 1) * block_len)
        value = total[own_first + block] + noise_ref[:, span] * own_ref[:, span]
        value += times(ahead[own_first + block].astype(BF16), diag_ref[block])
        part_refs[0][:, span] = value
        for step in range(1, sub_count):
            first = (sub_index ^ step) * blocks_dev
            part_refs[step][:, span] = total[first + block].astype(part_refs[step].dtype)


def join_kernel(index, own_ref, old_ref, moments_in_ref, *refs):
    part_refs = refs[:-3]
    next_ref, rounded_ref, moments_ref = refs[-3:]
    value = own_ref[...]
    for part_ref in part_refs:
        value += part_ref[...].astype(F32)
    next_ref[...] = value
    rounded_ref[...] = value.astype(BF16)
    old = old_ref[...]
    lane = lax.broadcasted_iota(jnp.int32, moments_ref.shape, 1)
    moments = moments_in_ref[...]
    found = {2 * index + 1: old * value}
    if index == 0:
        found[0] = old * old
    if index + 1 < ITERS:
        found[2 * index + 2] = value * value
    for order, product in found.items():
        moments = jnp.where(lane == order, jnp.sum(product, axis=1, keepdims=True), moments)
    moments_ref[...] = moments


def finish_kernel(moments_ref, *refs):
    basis_refs = refs[: ITERS + 1]
    solution_ref, residual_ref = refs[ITERS + 1 :]
    moments = [moments_ref[:, order : order + 1] for order in range(2 * ITERS)]

    def inner(first, second, shift):
        value = 0.0
        for i, a in enumerate(first):
            for j, b in enumerate(second):
                value = value + a * b * moments[i + j + shift]
        return value

    one = jnp.ones_like(moments[0])
    zero = jnp.zeros_like(one)
    direction, residual = [one], [one]
    answer = [zero] * ITERS
    norm_now = moments[0]
    for iteration in range(ITERS):
        step_size = norm_now / inner(direction, direction, 1)
        for power, weight in enumerate(direction):
            answer[power] = answer[power] + step_size * weight
        residual = residual + [zero]
        for power, weight in enumerate(direction):
            residual[power + 1] = residual[power + 1] - step_size * weight
        if iteration + 1 < ITERS:
            norm_next = inner(residual, residual, 0)
            direction = [
                value + (norm_next / norm_now) * old
                for value, old in zip(residual, direction + [zero])
            ]
            norm_now = norm_next
    fields = [basis_ref[...] for basis_ref in basis_refs]
    solution_ref[...] = sum(weight * field for weight, field in zip(answer, fields))
    residual_ref[...] = sum(weight * field for weight, field in zip(residual, fields))


def shape(rows, columns, kind):
    return jax.ShapeDtypeStruct((rows, columns), kind)


def exchange(block, axis, step):
    count = lax.axis_size(axis)
    return lax.ppermute(block, axis, [(i, i ^ step) for i in range(count)])


def swap(block, axis, first):
    count = lax.axis_size(axis)
    route = []
    for i in range(first, count - 1, 2):
        route += [(i, i + 1), (i + 1, i)]
    return lax.ppermute(block, axis, route)


def on_device(right_side, point_order, noise_var, block_pairs, pair_blocks, diag_blocks):
    sub_count = lax.axis_size("sub")
    tile_count = lax.axis_size("tile")
    sub_index = lax.axis_index("sub")
    tile_index = lax.axis_index("tile")
    rhs_count, points_dev = right_side.shape
    blocks_dev, block_len = diag_blocks.shape[:2]
    extended = (sub_count + 1) * blocks_dev
    live = jnp.sum((block_pairs[:, 0] >= 0).astype(jnp.int32))
    first_block = tile_index * (blocks_dev * sub_count)
    pairs = jnp.where(block_pairs >= 0, block_pairs - first_block, 0).reshape(-1)
    where = jnp.stack([sub_index, tile_index % 2, live]).astype(jnp.int32)
    blocks = pltpu.with_memory_space_constraint(pair_blocks, pltpu.VMEM)
    noise = noise_var[None, :]
    full = shape(rhs_count, points_dev, F32)
    half = shape(rhs_count, points_dev, BF16)
    field, rounded = pl.pallas_call(
        order_kernel,
        out_shape=(full, half),
        in_specs=[VMEM, VMEM],
        out_specs=(VMEM, VMEM),
        compiler_params=PARAMS,
        name="curve_order",
    )(right_side, point_order)
    basis = [field]
    moments = jnp.zeros((rhs_count, LANES), F32)
    for index in range(ITERS):
        rows = [rounded] + [exchange(rounded, "sub", step) for step in range(1, sub_count)]
        by_block = (extended, rhs_count, block_len)
        even, odd, tile_field = pl.pallas_call(
            functools.partial(ahead_kernel, sub_count),
            out_shape=(half, half, jax.ShapeDtypeStruct(by_block, F32)),
            in_specs=[SMEM, SMEM, VMEM] + [VMEM] * sub_count,
            out_specs=(VMEM, VMEM, VMEM),
            scratch_shapes=[pltpu.VMEM((blocks_dev, rhs_count, block_len), F32)],
            compiler_params=PARAMS,
            name="ahead",
        )(where, pairs, blocks, *rows)
        even = swap(even, "tile", 0)
        odd = swap(odd, "tile", 1)
        sent = F32 if index + 1 == ITERS else BF16
        part = shape(rhs_count, points_dev, sent)
        parts = pl.pallas_call(
            functools.partial(product_kernel, sub_count),
            out_shape=(full,) + (part,) * (sub_count - 1),
            in_specs=[SMEM, SMEM] + [VMEM] * 7,
            out_specs=(VMEM,) * sub_count,
            scratch_shapes=[pltpu.VMEM(by_block, F32), pltpu.VMEM(by_block, F32)],
            compiler_params=PARAMS,
            name="products",
        )(where, pairs, blocks, diag_blocks, noise, field, tile_field, even, odd)
        arrived = [exchange(parts[step], "sub", step) for step in range(1, sub_count)]
        field, rounded, moments = pl.pallas_call(
            functools.partial(join_kernel, index),
            out_shape=(full, half, shape(rhs_count, LANES, F32)),
            in_specs=[VMEM] * (3 + len(arrived)),
            out_specs=(VMEM, VMEM, VMEM),
            compiler_params=PARAMS,
            name="join",
        )(parts[0], field, moments, *arrived)
        basis.append(field)
    for axis, count in (("sub", sub_count), ("tile", tile_count)):
        step = 1
        while step < count:
            moments = moments + exchange(moments, axis, step)
            step *= 2
    return pl.pallas_call(
        finish_kernel,
        out_shape=(full, full),
        in_specs=[VMEM] * (ITERS + 2),
        out_specs=(VMEM, VMEM),
        compiler_params=PARAMS,
        name="finish",
    )(moments, *basis)


def solution(mesh):
    placed = (
        P(None, ("tile", "sub")),
        P(("tile", "sub"), None),
        P(("tile", "sub")),
        P(("tile", "sub"), None),
        P(("tile", "sub"), None, None),
        P(("tile", "sub"), None, None),
    )
    return jax.shard_map(
        on_device,
        mesh=mesh,
        in_specs=placed,
        out_specs=(P(None, ("tile", "sub")), P(None, ("tile", "sub"))),
        check_vma=False,
    )
```

```python
import functools

import jax
import jax.numpy as jnp
from jax import lax
from jax.experimental import pallas as pl
from jax.experimental.pallas import tpu as pltpu
from jax.sharding import PartitionSpec as P

ITERS = 3
LANES = 128
GROUP = 8
CHUNKS = 8
F32 = jnp.float32
BF16 = jnp.bfloat16
VMEM = pl.BlockSpec(memory_space=pltpu.VMEM)
SMEM = pl.BlockSpec(memory_space=pltpu.SMEM)
SLOTS = 128
EARLY_ROWS, EARLY_COLS, AHEAD_COLS, LATE_ROWS, LATE_COLS, FROM_AHEAD = range(6)
PARAMS = pltpu.CompilerParams(vmem_limit_bytes=16 * 1024 * 1024)


def times(field, block):
    return lax.dot_general(field, block, (((1,), (0,)), ((), ())), preferred_element_type=F32)


def times_transposed(field, block):
    return lax.dot_general(field, block, (((1,), (1,)), ((), ())), preferred_element_type=F32)


def order_kernel(right_ref, order_ref, curve_ref, rounded_ref):
    rhs_count, points = right_ref.shape
    for start in range(0, points, LANES):
        at = jnp.broadcast_to(order_ref[:, start : start + LANES], (rhs_count, LANES))
        chunk = at // LANES
        lane = at % LANES
        result = jnp.zeros((rhs_count, LANES), F32)
        for source in range(points // LANES):
            values = right_ref[:, source * LANES : (source + 1) * LANES]
            picked = jnp.take_along_axis(values, lane, axis=1)
            result = jnp.where(chunk == source, picked, result)
        curve_ref[:, start : start + LANES] = result
        rounded_ref[:, start : start + LANES] = result.astype(BF16)


def device_place(block_len, field_ref, sub_count):
    blocks_dev = field_ref.shape[1] // block_len
    sub_index = lax.axis_index("sub")
    return sub_index, blocks_dev, sub_index * blocks_dev, blocks_dev * sub_count


def load_kernel(sub_count, blocks_dev, pairs_ref, blocks_in, diag_in, blocks_ref, diag_ref, lists_ref, sems):
    slot_count = pairs_ref.shape[1]
    size = slot_count // CHUNKS
    copies = [
        pltpu.make_async_copy(
            blocks_in.at[pl.ds(part * size, size)], blocks_ref.at[pl.ds(part * size, size)], sems.at[part]
        )
        for part in range(CHUNKS)
    ]
    copies.append(pltpu.make_async_copy(diag_in, diag_ref, sems.at[CHUNKS]))
    for copy in copies:
        copy.start()
    sub_index = lax.axis_index("sub")
    tile_blocks = blocks_dev * sub_count
    own_first = sub_index * blocks_dev
    first_block = lax.axis_index("tile") * tile_blocks
    idle = (tile_blocks + blocks_dev) * 65536
    idle_source = {
        EARLY_ROWS: own_first,
        EARLY_COLS: own_first,
        AHEAD_COLS: tile_blocks - blocks_dev,
        LATE_ROWS: 0,
        LATE_COLS: 0,
        FROM_AHEAD: tile_blocks,
    }
    for index, source in idle_source.items():
        entry = idle + 256 * source

        def clear(at, carry, index=index, entry=entry):
            lists_ref[index * SLOTS + at] = entry
            return carry

        lax.fori_loop(0, SLOTS, clear, 0, unroll=8)

    def one_slot(slot, counts):
        row, col = pairs_ref[0, slot], pairs_ref[1, slot]
        live = row >= 0
        row, col = row - first_block, col - first_block

        def append(counts, source, target, kinds):
            early = (source // blocks_dev) // 2 == sub_index // 2
            entry = slot + 256 * source + 65536 * target
            for index, chosen in kinds(early):
                chosen = chosen & live
                count = counts[index]

                @pl.when(chosen)
                def _():
                    lists_ref[index * SLOTS + count] = entry

                counts[index] = count + chosen.astype(jnp.int32)

        counts = list(counts)
        outside = col >= tile_blocks
        append(
            counts, col, row,
            lambda early: (
                (EARLY_ROWS, early & ~outside), (LATE_ROWS, ~early & ~outside), (FROM_AHEAD, outside)
            ),
        )
        append(
            counts, row, col,
            lambda early: (
                (EARLY_COLS, early), (LATE_COLS, ~early & ~outside), (AHEAD_COLS, ~early & outside)
            ),
        )
        return tuple(counts)

    counts = lax.fori_loop(0, slot_count, one_slot, (jnp.int32(0),) * 6)
    for index, count in enumerate(counts):
        lists_ref[6 * SLOTS + index] = count
    for copy in copies:
        copy.wait()


def add_products(lists_ref, blocks_ref, field, total, row_list, col_list, source_from=0, target_from=0):
    kinds = [(index, kind) for index, kind in ((row_list, times_transposed), (col_list, times)) if index is not None]
    longest = functools.reduce(jnp.maximum, [lists_ref[6 * SLOTS + index] for index, _ in kinds])

    def one_group(group, carry):
        results = []
        for step in range(GROUP):
            for index, kind in kinds:
                entry = lists_ref[index * SLOTS + group * GROUP + step]
                slot, source, target = entry & 255, (entry >> 8) & 255, entry >> 16
                value = kind(field[source - source_from].astype(BF16), blocks_ref[slot])
                results.append((target - target_from, value))
        for at, value in results:
            total[at] += value
        return carry

    lax.fori_loop(0, (longest + GROUP - 1) // GROUP, one_group, 0)


def lay_out(row_ref, field, first, block_len):
    for block in range(row_ref.shape[1] // block_len):
        piece = row_ref[:, block * block_len : (block + 1) * block_len]
        field[first + block] = piece.astype(F32)


def early_kernel(sub_count, lists_ref, blocks_ref, diag_ref, noise_ref, own_ref, *refs):
    row_refs, (total, field) = refs[:-2], refs[-2:]
    block_len = blocks_ref.shape[1]
    sub_index, blocks_dev, own_first, _ = device_place(block_len, own_ref, sub_count)
    for step, row_ref in enumerate(row_refs):
        lay_out(row_ref, field, (sub_index ^ step) * blocks_dev, block_len)
    for block in range(total.shape[0]):
        total[block] = jnp.zeros(total.shape[1:], F32)
    for block in range(blocks_dev):
        span = slice(block * block_len, (block + 1) * block_len)
        value = noise_ref[:, span] * own_ref[:, span]
        total[own_first + block] = value + times(field[own_first + block].astype(BF16), diag_ref[block])
    add_products(lists_ref, blocks_ref, field, total, EARLY_ROWS, EARLY_COLS)


def ahead_kernel(sub_count, lists_ref, blocks_ref, begun_ref, *refs):
    row_refs = refs[:sub_count]
    even_ref, odd_ref, field_ref, total = refs[sub_count:]
    block_len = blocks_ref.shape[1]
    sub_index, blocks_dev, _, tile_blocks = device_place(block_len, even_ref, sub_count)
    for step, row_ref in enumerate(row_refs):
        lay_out(row_ref, field_ref, (sub_index ^ step) * blocks_dev, block_len)
    for block in range(blocks_dev):
        total[block] = begun_ref[tile_blocks + block]
    total[blocks_dev] = jnp.zeros(total.shape[1:], F32)
    add_products(lists_ref, blocks_ref, field_ref, total, None, AHEAD_COLS, 0, tile_blocks)
    is_odd = lax.axis_index("tile") % 2 == 1
    for block in range(blocks_dev):
        span = slice(block * block_len, (block + 1) * block_len)
        products = total[block]
        first_row = field_ref[block]
        even_ref[:, span] = jnp.where(is_odd, first_row, products).astype(BF16)
        odd_ref[:, span] = jnp.where(is_odd, products, first_row).astype(BF16)


def late_kernel(lists_ref, blocks_ref, begun_ref, field_ref, total):
    total[...] = begun_ref[...]
    add_products(lists_ref, blocks_ref, field_ref, total, LATE_ROWS, LATE_COLS)


def part_kernel(sub_count, is_last, lists_ref, blocks_ref, begun_ref, field_ref, even_ref, odd_ref, moments_in_ref, *refs):
    part_refs = refs[:sub_count]
    moments_ref, total, ahead = refs[sub_count:]
    block_len = blocks_ref.shape[1]
    sub_index, blocks_dev, own_first, tile_blocks = device_place(block_len, even_ref, sub_count)
    is_odd = lax.axis_index("tile") % 2 == 1
    for block in range(blocks_dev):
        span = slice(block * block_len, (block + 1) * block_len)
        even = even_ref[:, span].astype(F32)
        odd = odd_ref[:, span].astype(F32)
        ahead[block] = jnp.where(is_odd, odd, even)
        total[block] = begun_ref[block] + jnp.where(is_odd, even, odd)
    for block in range(blocks_dev, tile_blocks):
        total[block] = begun_ref[block]
    total[begun_ref.shape[0] - 1] = jnp.zeros(total.shape[1:], F32)
    add_products(lists_ref, blocks_ref, ahead, total, FROM_AHEAD, None, tile_blocks, 0)
    for step in range(sub_count):
        first = (sub_index ^ step) * blocks_dev
        for block in range(blocks_dev):
            span = slice(block * block_len, (block + 1) * block_len)
            part_refs[step][:, span] = total[first + block].astype(part_refs[step].dtype)
    moments = moments_in_ref[...]
    if is_last:
        product = jnp.zeros(total.shape[1:], F32)
        for block in range(tile_blocks):
            product += field_ref[block] * total[block]
        lane = lax.broadcasted_iota(jnp.int32, moments.shape, 1)
        moments = jnp.where(lane == 2 * ITERS - 1, jnp.sum(product, axis=1, keepdims=True), moments)
    moments_ref[...] = moments


def join_kernel(index, own_ref, old_ref, moments_in_ref, *refs):
    part_refs = refs[:-3]
    next_ref, rounded_ref, moments_ref = refs[-3:]
    value = own_ref[...]
    for part_ref in part_refs:
        value += part_ref[...].astype(F32)
    next_ref[...] = value
    rounded_ref[...] = value.astype(BF16)
    old = old_ref[...]
    lane = lax.broadcasted_iota(jnp.int32, moments_ref.shape, 1)
    moments = moments_in_ref[...] if index else jnp.zeros(moments_ref.shape, F32)
    found = {2 * index + 1: old * value, 2 * index + 2: value * value}
    if index == 0:
        found[0] = old * old
    for order, product in found.items():
        moments = jnp.where(lane == order, jnp.sum(product, axis=1, keepdims=True), moments)
    moments_ref[...] = moments


def finish_kernel(sub_count, moments_ref, *refs):
    part_refs, basis_refs = refs[:sub_count], refs[sub_count:-2]
    solution_ref, residual_ref = refs[-2:]
    moments = [moments_ref[:, order : order + 1] for order in range(2 * ITERS)]

    def inner(first, second, shift):
        value = 0.0
        for i, a in enumerate(first):
            for j, b in enumerate(second):
                value = value + a * b * moments[i + j + shift]
        return value

    one = jnp.ones_like(moments[0])
    zero = jnp.zeros_like(one)
    direction, residual = [one], [one]
    answer = [zero] * ITERS
    norm_now = moments[0]
    for iteration in range(ITERS):
        step_size = norm_now / inner(direction, direction, 1)
        for power, weight in enumerate(direction):
            answer[power] = answer[power] + step_size * weight
        residual = residual + [zero]
        for power, weight in enumerate(direction):
            residual[power + 1] = residual[power + 1] - step_size * weight
        if iteration + 1 < ITERS:
            norm_next = inner(residual, residual, 0)
            direction = [
                value + (norm_next / norm_now) * old
                for value, old in zip(residual, direction + [zero])
            ]
            norm_now = norm_next
    fields = [basis_ref[...] for basis_ref in basis_refs]
    fields.append(sum(part_ref[...].astype(F32) for part_ref in part_refs))
    solution_ref[...] = sum(weight * field for weight, field in zip(answer, fields))
    residual_ref[...] = sum(weight * field for weight, field in zip(residual, fields))


def shape(rows, columns, kind):
    return jax.ShapeDtypeStruct((rows, columns), kind)


def exchange(block, axis, step):
    count = lax.axis_size(axis)
    return lax.ppermute(block, axis, [(i, i ^ step) for i in range(count)])


def swap(block, axis, first):
    count = lax.axis_size(axis)
    route = []
    for i in range(first, count - 1, 2):
        route += [(i, i + 1), (i + 1, i)]
    return lax.ppermute(block, axis, route)


def call(kernel, outs, ins, name, cost=0, **options):
    single = not isinstance(outs, tuple)
    specs = [SMEM if getattr(value, "dtype", None) == jnp.int32 and value.ndim == 1 else VMEM for value in ins]
    options.setdefault("in_specs", specs)
    options.setdefault("out_specs", VMEM if single else (VMEM,) * len(outs))
    return pl.pallas_call(
        kernel,
        out_shape=outs,
        compiler_params=PARAMS,
        name=name,
        cost_estimate=pl.CostEstimate(flops=int(cost * 1e9), bytes_accessed=0, transcendentals=0),
        **options,
    )(*ins)


def on_device(right_side, point_order, noise_var, block_pairs, pair_blocks, diag_blocks):
    sub_count = lax.axis_size("sub")
    tile_count = lax.axis_size("tile")
    rhs_count, points_dev = right_side.shape
    blocks_dev, block_len = diag_blocks.shape[:2]
    extended = (sub_count + 1) * blocks_dev
    noise = noise_var[None, :]
    full = shape(rhs_count, points_dev, F32)
    half = shape(rhs_count, points_dev, BF16)
    scalars = shape(rhs_count, LANES, F32)
    sums = jax.ShapeDtypeStruct((extended + 1, rhs_count, block_len), F32)

    def scratch(blocks):
        return pltpu.VMEM((blocks, rhs_count, block_len), F32)

    any_space = pl.BlockSpec(memory_space=pl.ANY)
    blocks, diag, lists = call(
        functools.partial(load_kernel, sub_count, blocks_dev),
        (
            pltpu.VMEM(pair_blocks.shape, BF16),
            pltpu.VMEM(diag_blocks.shape, BF16),
            jax.ShapeDtypeStruct((8 * SLOTS,), jnp.int32),
        ),
        (block_pairs.T, pair_blocks, diag_blocks),
        "load",
        4,
        in_specs=[SMEM, any_space, any_space],
        out_specs=(VMEM, VMEM, SMEM),
        scratch_shapes=[pltpu.SemaphoreType.DMA((CHUNKS + 1,))],
    )
    field, rounded = call(order_kernel, (full, half), (right_side, point_order), "curve_order", 1, in_specs=[VMEM, VMEM])
    basis = [field]
    moments = jnp.zeros(scalars.shape, F32)
    for index in range(ITERS):
        is_last = index + 1 == ITERS
        rows = [rounded] + [exchange(rounded, "sub", step) for step in range(1, sub_count)]
        begun = call(
            functools.partial(early_kernel, sub_count),
            sums,
            (lists, blocks, diag, noise, field, *rows[:2]),
            "early",
            3,
            scratch_shapes=[scratch(extended)],
        )
        even, odd, tile_field = call(
            functools.partial(ahead_kernel, sub_count),
            (half, half, jax.ShapeDtypeStruct((sub_count * blocks_dev, rhs_count, block_len), F32)),
            (lists, blocks, begun, *rows),
            "ahead",
            1,
            scratch_shapes=[scratch(blocks_dev + 1)],
        )
        even = swap(even, "tile", 0)
        odd = swap(odd, "tile", 1)
        begun = call(late_kernel, sums, (lists, blocks, begun, tile_field), "late", 3)
        part = shape(rhs_count, points_dev, F32 if is_last else BF16)
        *parts, moments = call(
            functools.partial(part_kernel, sub_count, is_last),
            (full,) + (part,) * (sub_count - 1) + (scalars,),
            (lists, blocks, begun, tile_field, even, odd, moments),
            "parts",
            1,
            scratch_shapes=[scratch(extended + 1), scratch(blocks_dev)],
        )
        arrived = [exchange(parts[step], "sub", step) for step in range(1, sub_count)]
        if not is_last:
            field, rounded, moments = call(
                functools.partial(join_kernel, index),
                (full, half, scalars),
                (parts[0], field, moments, *arrived),
                "join",
            )
            basis.append(field)
    for axis, count in (("sub", sub_count), ("tile", tile_count)):
        step = 1
        while step < count:
            moments = moments + exchange(moments, axis, step)
            step *= 2
    return call(
        functools.partial(finish_kernel, sub_count),
        (full, full),
        (moments, parts[0], *arrived, *basis),
        "finish",
    )


def solution(mesh):
    placed = (
        P(None, ("tile", "sub")),
        P(("tile", "sub"), None),
        P(("tile", "sub")),
        P(("tile", "sub"), None),
        P(("tile", "sub"), None, None),
        P(("tile", "sub"), None, None),
    )
    return jax.shard_map(
        on_device,
        mesh=mesh,
        in_specs=placed,
        out_specs=(P(None, ("tile", "sub")), P(None, ("tile", "sub"))),
        check_vma=False,
    )
```

```python
import functools

import jax
import jax.numpy as jnp
from jax import lax
from jax.experimental import pallas as pl
from jax.experimental.pallas import tpu as pltpu
from jax.sharding import PartitionSpec as P

ITERS = 3
LANES = 128
LONG_GROUP = 16
SHORT_GROUP = 8
TURN_GROUP = 4
F32 = jnp.float32
BF16 = jnp.bfloat16
VMEM = pl.BlockSpec(memory_space=pltpu.VMEM)
SMEM = pl.BlockSpec(memory_space=pltpu.SMEM)
EARLY, AHEAD, LATE, FROM_AHEAD = KINDS = range(4)
PARAMS = pltpu.CompilerParams(vmem_limit_bytes=4 * 1024 * 1024)


def times(field, block):
    return lax.dot_general(field, block, (((1,), (0,)), ((), ())), preferred_element_type=F32)


def order_kernel(right_ref, order_ref, curve_ref, rounded_ref):
    rhs_count, points = right_ref.shape
    for start in range(0, points, LANES):
        at = jnp.broadcast_to(order_ref[:, start : start + LANES], (rhs_count, LANES))
        chunk = at // LANES
        lane = at % LANES
        result = jnp.zeros((rhs_count, LANES), F32)
        for source in range(points // LANES):
            values = right_ref[:, source * LANES : (source + 1) * LANES]
            picked = jnp.take_along_axis(values, lane, axis=1)
            result = jnp.where(chunk == source, picked, result)
        curve_ref[:, start : start + LANES] = result
        rounded_ref[:, start : start + LANES] = result.astype(BF16)


def device_place(block_len, field_ref, sub_count):
    blocks_dev = field_ref.shape[1] // block_len
    sub_index = lax.axis_index("sub")
    return sub_index, blocks_dev, sub_index * blocks_dev, blocks_dev * sub_count


def list_stride(slot_count):
    return -(-(2 * slot_count + LONG_GROUP) // LANES) * LANES


def lists_kernel(sub_count, blocks_dev, slot_count, pairs_ref, lists_ref, padded):
    width = padded.shape[1]
    stride = list_stride(slot_count)
    sub_index = lax.axis_index("sub")
    tile_blocks = blocks_dev * sub_count
    first_block = lax.axis_index("tile") * tile_blocks
    padded[...] = jnp.full(padded.shape, -1.0, F32)
    padded[0:2, 0:slot_count] = pairs_ref[...].astype(F32)
    by_lane = padded[...]
    by_row = jnp.transpose(by_lane)

    def sides(row, col, axis):
        live = jnp.concatenate([row, row], axis) >= 0.0
        row = row.astype(jnp.int32) - first_block
        col = col.astype(jnp.int32) - first_block
        source = jnp.concatenate([row, col], axis)
        target = jnp.concatenate([col, row], axis)
        return live, source, target

    live, source, target = sides(by_row[:, 0:1], by_row[:, 1:2], 0)
    kind = jnp.where(target >= tile_blocks, AHEAD, LATE)
    first_row = (sub_index // 2) * (2 * blocks_dev)
    is_early = (source >= first_row) & (source < first_row + 2 * blocks_dev) & (source < tile_blocks)
    kind = jnp.where(is_early, EARLY, kind)
    kind = jnp.where(source >= tile_blocks, FROM_AHEAD, kind)
    kind = jnp.where(live, kind, -1)
    hot = (kind == lax.broadcasted_iota(jnp.int32, (2 * width, LANES), 1)).astype(F32)
    below = lax.broadcasted_iota(jnp.int32, (2 * width, 2 * width), 0) > lax.broadcasted_iota(
        jnp.int32, (2 * width, 2 * width), 1
    )
    ranks = times(below.astype(F32).astype(BF16), hot.astype(BF16))
    rank = jnp.sum(ranks * hot, axis=1, keepdims=True).astype(jnp.int32)
    counts = jnp.sum(hot, axis=0, keepdims=True)
    at = jnp.where(live, kind * stride + rank, -1)
    spread = at == lax.broadcasted_iota(jnp.int32, (2 * width, len(KINDS) * stride), 1)
    live, source, target = sides(by_lane[0:1, :], by_lane[1:2, :], 1)
    lane = lax.broadcasted_iota(jnp.int32, (1, 2 * width), 1)
    block = jnp.where(lane < width, lane, lane - width + slot_count)
    fields = jnp.concatenate(
        [jnp.where(live, value, 0).astype(F32) for value in (block, source, target)]
        + [jnp.zeros((5, 2 * width), F32)],
        0,
    )
    found = times(fields.astype(BF16), spread.astype(F32).astype(BF16))
    entries = found[0:1] + 256.0 * found[1:2] + 65536.0 * found[2:3]
    entries = entries.astype(jnp.int32)
    idle = (tile_blocks + blocks_dev) * 65536
    idle_source = {
        EARLY: sub_index * blocks_dev,
        AHEAD: tile_blocks - blocks_dev,
        LATE: 0,
        FROM_AHEAD: tile_blocks,
    }
    place = lax.broadcasted_iota(jnp.int32, (1, stride), 1)
    for index in KINDS:
        span = slice(index * stride, (index + 1) * stride)
        count = counts[:, index : index + 1].astype(jnp.int32)
        lists_ref[:, span] = jnp.where(place < count, entries[:, span], idle + 256 * idle_source[index])
    lists_ref[:, len(KINDS) * stride :] = counts.astype(jnp.int32)


def turn_kernel(pairs_blocks_ref, blocks_ref, sem):
    slot_count = pairs_blocks_ref.shape[0]
    copy = pltpu.make_async_copy(pairs_blocks_ref, blocks_ref.at[pl.ds(0, slot_count)], sem)
    copy.start()

    def one_group(group, carry):
        for step in range(TURN_GROUP):
            slot = group * TURN_GROUP + step
            blocks_ref[slot_count + slot] = jnp.transpose(pairs_blocks_ref[slot])
        return carry

    lax.fori_loop(0, slot_count // TURN_GROUP, one_group, 0)
    copy.wait()


def add_products(lists_ref, blocks_ref, field, total, index, size, source_from=0, target_from=0):
    stride = list_stride(blocks_ref.shape[0] // 2)
    count = lists_ref[0, len(KINDS) * stride + index]

    def one_group(group, carry):
        results = []
        for step in range(size):
            entry = lists_ref[0, index * stride + group * size + step]
            block, source, target = entry & 255, (entry >> 8) & 255, entry >> 16
            value = times(field[source - source_from].astype(BF16), blocks_ref[block])
            results.append((target - target_from, value))
        for at, value in results:
            total[at] += value
        return carry

    lax.fori_loop(0, (count + size - 1) // size, one_group, 0)


def lay_out(row_ref, field, first, block_len):
    for block in range(row_ref.shape[1] // block_len):
        piece = row_ref[:, block * block_len : (block + 1) * block_len]
        field[first + block] = piece.astype(F32)


def early_kernel(sub_count, lists_ref, blocks_ref, diag_ref, noise_ref, own_ref, *refs):
    row_refs, (total, field) = refs[:-2], refs[-2:]
    block_len = blocks_ref.shape[1]
    sub_index, blocks_dev, own_first, _ = device_place(block_len, own_ref, sub_count)
    for step, row_ref in enumerate(row_refs):
        lay_out(row_ref, field, (sub_index ^ step) * blocks_dev, block_len)
    for block in range(total.shape[0]):
        total[block] = jnp.zeros(total.shape[1:], F32)
    for block in range(blocks_dev):
        span = slice(block * block_len, (block + 1) * block_len)
        value = noise_ref[:, span] * own_ref[:, span]
        total[own_first + block] = value + times(field[own_first + block].astype(BF16), diag_ref[block])
    add_products(lists_ref, blocks_ref, field, total, EARLY, LONG_GROUP)


def ahead_kernel(sub_count, lists_ref, blocks_ref, begun_ref, *refs):
    row_refs = refs[:sub_count]
    even_ref, odd_ref, field_ref, total = refs[sub_count:]
    block_len = blocks_ref.shape[1]
    sub_index, blocks_dev, _, tile_blocks = device_place(block_len, even_ref, sub_count)
    for step, row_ref in enumerate(row_refs):
        lay_out(row_ref, field_ref, (sub_index ^ step) * blocks_dev, block_len)
    for block in range(blocks_dev):
        total[block] = begun_ref[tile_blocks + block]
    total[blocks_dev] = jnp.zeros(total.shape[1:], F32)
    add_products(lists_ref, blocks_ref, field_ref, total, AHEAD, SHORT_GROUP, 0, tile_blocks)
    is_odd = lax.axis_index("tile") % 2 == 1
    for block in range(blocks_dev):
        span = slice(block * block_len, (block + 1) * block_len)
        products = total[block]
        first_row = field_ref[block]
        even_ref[:, span] = jnp.where(is_odd, first_row, products).astype(BF16)
        odd_ref[:, span] = jnp.where(is_odd, products, first_row).astype(BF16)


def late_kernel(lists_ref, blocks_ref, begun_ref, field_ref, total):
    total[...] = begun_ref[...]
    add_products(lists_ref, blocks_ref, field_ref, total, LATE, LONG_GROUP)


def part_kernel(sub_count, is_last, lists_ref, blocks_ref, begun_ref, field_ref, even_ref, odd_ref, moments_in_ref, *refs):
    part_refs = refs[:sub_count]
    moments_ref, total, ahead = refs[sub_count:]
    block_len = blocks_ref.shape[1]
    sub_index, blocks_dev, own_first, tile_blocks = device_place(block_len, even_ref, sub_count)
    is_odd = lax.axis_index("tile") % 2 == 1
    for block in range(blocks_dev):
        span = slice(block * block_len, (block + 1) * block_len)
        even = even_ref[:, span].astype(F32)
        odd = odd_ref[:, span].astype(F32)
        ahead[block] = jnp.where(is_odd, odd, even)
        total[block] = begun_ref[block] + jnp.where(is_odd, even, odd)
    for block in range(blocks_dev, tile_blocks):
        total[block] = begun_ref[block]
    total[begun_ref.shape[0] - 1] = jnp.zeros(total.shape[1:], F32)
    add_products(lists_ref, blocks_ref, ahead, total, FROM_AHEAD, SHORT_GROUP, tile_blocks, 0)
    for step in range(sub_count):
        first = (sub_index ^ step) * blocks_dev
        for block in range(blocks_dev):
            span = slice(block * block_len, (block + 1) * block_len)
            part_refs[step][:, span] = total[first + block].astype(part_refs[step].dtype)
    moments = moments_in_ref[...]
    if is_last:
        product = jnp.zeros(total.shape[1:], F32)
        for block in range(tile_blocks):
            product += field_ref[block] * total[block]
        lane = lax.broadcasted_iota(jnp.int32, moments.shape, 1)
        moments = jnp.where(lane == 2 * ITERS - 1, jnp.sum(product, axis=1, keepdims=True), moments)
    moments_ref[...] = moments


def join_kernel(index, own_ref, old_ref, moments_in_ref, *refs):
    part_refs = refs[:-3]
    next_ref, rounded_ref, moments_ref = refs[-3:]
    value = own_ref[...]
    for part_ref in part_refs:
        value += part_ref[...].astype(F32)
    next_ref[...] = value
    rounded_ref[...] = value.astype(BF16)
    old = old_ref[...]
    lane = lax.broadcasted_iota(jnp.int32, moments_ref.shape, 1)
    moments = moments_in_ref[...] if index else jnp.zeros(moments_ref.shape, F32)
    found = {2 * index + 1: old * value, 2 * index + 2: value * value}
    if index == 0:
        found[0] = old * old
    for order, product in found.items():
        moments = jnp.where(lane == order, jnp.sum(product, axis=1, keepdims=True), moments)
    moments_ref[...] = moments


def finish_kernel(sub_count, moments_ref, *refs):
    part_refs, basis_refs = refs[:sub_count], refs[sub_count:-2]
    solution_ref, residual_ref = refs[-2:]
    moments = [moments_ref[:, order : order + 1] for order in range(2 * ITERS)]

    def inner(first, second, shift):
        value = 0.0
        for i, a in enumerate(first):
            for j, b in enumerate(second):
                value = value + a * b * moments[i + j + shift]
        return value

    one = jnp.ones_like(moments[0])
    zero = jnp.zeros_like(one)
    direction, residual = [one], [one]
    answer = [zero] * ITERS
    norm_now = moments[0]
    for iteration in range(ITERS):
        step_size = norm_now / inner(direction, direction, 1)
        for power, weight in enumerate(direction):
            answer[power] = answer[power] + step_size * weight
        residual = residual + [zero]
        for power, weight in enumerate(direction):
            residual[power + 1] = residual[power + 1] - step_size * weight
        if iteration + 1 < ITERS:
            norm_next = inner(residual, residual, 0)
            direction = [
                value + (norm_next / norm_now) * old
                for value, old in zip(residual, direction + [zero])
            ]
            norm_now = norm_next
    fields = [basis_ref[...] for basis_ref in basis_refs]
    fields.append(sum(part_ref[...].astype(F32) for part_ref in part_refs))
    solution_ref[...] = sum(weight * field for weight, field in zip(answer, fields))
    residual_ref[...] = sum(weight * field for weight, field in zip(residual, fields))


def shape(rows, columns, kind):
    return jax.ShapeDtypeStruct((rows, columns), kind)


def exchange(block, axis, step):
    count = lax.axis_size(axis)
    return lax.ppermute(block, axis, [(i, i ^ step) for i in range(count)])


def swap(block, axis, first):
    count = lax.axis_size(axis)
    route = []
    for i in range(first, count - 1, 2):
        route += [(i, i + 1), (i + 1, i)]
    return lax.ppermute(block, axis, route)


def call(kernel, outs, ins, name, cost=0, **options):
    single = not isinstance(outs, tuple)
    specs = [SMEM if value.dtype == jnp.int32 else VMEM for value in ins]
    options.setdefault("in_specs", specs)
    options.setdefault("out_specs", VMEM if single else (VMEM,) * len(outs))
    return pl.pallas_call(
        kernel,
        out_shape=outs,
        compiler_params=PARAMS,
        name=name,
        cost_estimate=pl.CostEstimate(flops=int(cost * 1e9), bytes_accessed=0, transcendentals=0),
        **options,
    )(*ins)


def on_device(right_side, point_order, noise_var, block_pairs, pair_blocks, diag_blocks):
    sub_count = lax.axis_size("sub")
    tile_count = lax.axis_size("tile")
    rhs_count, points_dev = right_side.shape
    blocks_dev, block_len = diag_blocks.shape[:2]
    extended = (sub_count + 1) * blocks_dev
    noise = noise_var[None, :]
    full = shape(rhs_count, points_dev, F32)
    half = shape(rhs_count, points_dev, BF16)
    scalars = shape(rhs_count, LANES, F32)
    sums = jax.ShapeDtypeStruct((extended + 1, rhs_count, block_len), F32)

    def scratch(blocks):
        return pltpu.VMEM((blocks, rhs_count, block_len), F32)

    slot_count = pair_blocks.shape[0]
    width = -(-slot_count // LANES) * LANES
    assert 2 * width <= 256 and extended < 256 and slot_count % TURN_GROUP == 0
    lists = call(
        functools.partial(lists_kernel, sub_count, blocks_dev, slot_count),
        jax.ShapeDtypeStruct((1, len(KINDS) * list_stride(slot_count) + LANES), jnp.int32),
        (block_pairs.T,),
        "lists",
        1,
        in_specs=[VMEM],
        scratch_shapes=[pltpu.VMEM((8, width), F32)],
    )
    blocks = call(
        turn_kernel,
        pltpu.VMEM((2 * slot_count, block_len, block_len), BF16),
        (pair_blocks,),
        "turn",
        4,
        scratch_shapes=[pltpu.SemaphoreType.DMA(())],
    )
    field, rounded = call(order_kernel, (full, half), (right_side, point_order), "curve_order", 10, in_specs=[VMEM, VMEM])
    basis = [field]
    moments = jnp.zeros(scalars.shape, F32)
    for index in range(ITERS):
        is_last = index + 1 == ITERS
        rows = [rounded] + [exchange(rounded, "sub", step) for step in range(1, sub_count)]
        begun = call(
            functools.partial(early_kernel, sub_count),
            sums,
            (lists, blocks, diag_blocks, noise, field, *rows[:2]),
            "early",
            3,
            scratch_shapes=[scratch(extended)],
        )
        even, odd, tile_field = call(
            functools.partial(ahead_kernel, sub_count),
            (half, half, jax.ShapeDtypeStruct((sub_count * blocks_dev, rhs_count, block_len), F32)),
            (lists, blocks, begun, *rows),
            "ahead",
            1,
            scratch_shapes=[scratch(blocks_dev + 1)],
        )
        even = swap(even, "tile", 0)
        odd = swap(odd, "tile", 1)
        begun = call(late_kernel, sums, (lists, blocks, begun, tile_field), "late", 3)
        part = shape(rhs_count, points_dev, F32 if is_last else BF16)
        *parts, moments = call(
            functools.partial(part_kernel, sub_count, is_last),
            (full,) + (part,) * (sub_count - 1) + (scalars,),
            (lists, blocks, begun, tile_field, even, odd, moments),
            "parts",
            1,
            scratch_shapes=[scratch(extended + 1), scratch(blocks_dev)],
        )
        if is_last:
            break
        arrived = [exchange(parts[step], "sub", step) for step in range(1, sub_count)]
        field, rounded, moments = call(
            functools.partial(join_kernel, index),
            (full, half, scalars),
            (parts[0], field, moments, *arrived),
            "join",
        )
        basis.append(field)
    arrived = []
    for axis, count in (("sub", sub_count), ("tile", tile_count)):
        step = 1
        while step < count:
            moments = moments + exchange(moments, axis, step)
            if len(arrived) < sub_count - 1:
                far = sub_count - 1 - len(arrived)
                arrived.append(exchange(parts[far], "sub", far))
                moments, *parts = lax.optimization_barrier((moments, *parts))
            step *= 2
    for far in range(sub_count - 1 - len(arrived), 0, -1):
        arrived.append(exchange(parts[far], "sub", far))
    return call(
        functools.partial(finish_kernel, sub_count),
        (full, full),
        (moments, parts[0], *arrived, *basis),
        "finish",
    )


def solution(mesh):
    placed = (
        P(None, ("tile", "sub")),
        P(("tile", "sub"), None),
        P(("tile", "sub")),
        P(("tile", "sub"), None),
        P(("tile", "sub"), None, None),
        P(("tile", "sub"), None, None),
    )
    return jax.shard_map(
        on_device,
        mesh=mesh,
        in_specs=placed,
        out_specs=(P(None, ("tile", "sub")), P(None, ("tile", "sub"))),
        check_vma=False,
    )
```

```python
import functools

import jax
import jax.numpy as jnp
from jax import lax
from jax.experimental import pallas as pl
from jax.experimental.pallas import tpu as pltpu
from jax.sharding import PartitionSpec as P

ITERS = 3
LANES = 128
LONG_GROUP = 16
SHORT_GROUP = 8
TURN_GROUP = 4
F32 = jnp.float32
BF16 = jnp.bfloat16
VMEM = pl.BlockSpec(memory_space=pltpu.VMEM)
SMEM = pl.BlockSpec(memory_space=pltpu.SMEM)
EARLY, AHEAD, LATE, FROM_AHEAD = KINDS = range(4)
PARAMS = pltpu.CompilerParams(vmem_limit_bytes=4 * 1024 * 1024)


def times(field, block):
    return lax.dot_general(field, block, (((1,), (0,)), ((), ())), preferred_element_type=F32)


def times_transposed(field, block):
    return lax.dot_general(field, block, (((1,), (1,)), ((), ())), preferred_element_type=F32)


def order_kernel(right_ref, order_ref, curve_ref, rounded_ref):
    rhs_count, points = right_ref.shape
    for start in range(0, points, LANES):
        at = jnp.broadcast_to(order_ref[:, start : start + LANES], (rhs_count, LANES))
        chunk = at // LANES
        lane = at % LANES
        result = jnp.zeros((rhs_count, LANES), F32)
        for source in range(points // LANES):
            values = right_ref[:, source * LANES : (source + 1) * LANES]
            picked = jnp.take_along_axis(values, lane, axis=1)
            result = jnp.where(chunk == source, picked, result)
        curve_ref[:, start : start + LANES] = result
        rounded_ref[:, start : start + LANES] = result.astype(BF16)


def device_place(block_len, field_ref, sub_count):
    blocks_dev = field_ref.shape[1] // block_len
    sub_index = lax.axis_index("sub")
    return sub_index, blocks_dev, sub_index * blocks_dev, blocks_dev * sub_count


def list_stride(slot_count):
    return -(-(2 * slot_count + LONG_GROUP) // LANES) * LANES


def lists_kernel(sub_count, blocks_dev, slot_count, pairs_ref, out_ref, padded, lists_ref, sem):
    width = padded.shape[1]
    stride = list_stride(slot_count)
    sub_index = lax.axis_index("sub")
    tile_blocks = blocks_dev * sub_count
    first_block = lax.axis_index("tile") * tile_blocks
    padded[...] = jnp.full(padded.shape, -1.0, F32)
    padded[0:2, 0:slot_count] = pairs_ref[...].astype(F32)
    by_lane = padded[...]
    by_row = jnp.transpose(by_lane)

    def sides(row, col, axis):
        live = jnp.concatenate([row, row], axis) >= 0.0
        row = row.astype(jnp.int32) - first_block
        col = col.astype(jnp.int32) - first_block
        source = jnp.concatenate([row, col], axis)
        target = jnp.concatenate([col, row], axis)
        return live, source, target

    live, source, target = sides(by_row[:, 0:1], by_row[:, 1:2], 0)
    kind = jnp.where(target >= tile_blocks, AHEAD, LATE)
    first_row = (sub_index // 2) * (2 * blocks_dev)
    is_early = (source >= first_row) & (source < first_row + 2 * blocks_dev) & (source < tile_blocks)
    kind = jnp.where(is_early, EARLY, kind)
    kind = jnp.where(source >= tile_blocks, FROM_AHEAD, kind)
    kind = jnp.where(live, kind, -1)
    hot = (kind == lax.broadcasted_iota(jnp.int32, (2 * width, LANES), 1)).astype(F32)
    below = lax.broadcasted_iota(jnp.int32, (2 * width, 2 * width), 0) > lax.broadcasted_iota(
        jnp.int32, (2 * width, 2 * width), 1
    )
    ranks = times(below.astype(F32).astype(BF16), hot.astype(BF16))
    rank = jnp.sum(ranks * hot, axis=1, keepdims=True).astype(jnp.int32)
    counts = jnp.sum(hot, axis=0, keepdims=True)
    at = jnp.where(live, kind * stride + rank, -1)
    spread = at == lax.broadcasted_iota(jnp.int32, (2 * width, len(KINDS) * stride), 1)
    live, source, target = sides(by_lane[0:1, :], by_lane[1:2, :], 1)
    lane = lax.broadcasted_iota(jnp.int32, (1, 2 * width), 1)
    block = jnp.where(lane < width, lane, lane - width + slot_count)
    fields = jnp.concatenate(
        [jnp.where(live, value, 0).astype(F32) for value in (block, source, target)]
        + [jnp.zeros((5, 2 * width), F32)],
        0,
    )
    found = times(fields.astype(BF16), spread.astype(F32).astype(BF16))
    entries = found[0:1] + 256.0 * found[1:2] + 65536.0 * found[2:3]
    entries = entries.astype(jnp.int32)
    idle = (tile_blocks + blocks_dev) * 65536
    idle_source = {
        EARLY: sub_index * blocks_dev,
        AHEAD: tile_blocks - blocks_dev,
        LATE: 0,
        FROM_AHEAD: tile_blocks,
    }
    place = lax.broadcasted_iota(jnp.int32, (1, stride), 1)
    for index in KINDS:
        span = slice(index * stride, (index + 1) * stride)
        count = counts[:, index : index + 1].astype(jnp.int32)
        lists_ref[:, span] = jnp.where(place < count, entries[:, span], idle + 256 * idle_source[index])
    lists_ref[:, len(KINDS) * stride : len(KINDS) * stride + LANES] = counts.astype(jnp.int32)
    by_column = jnp.sum(hot[:width], axis=0, keepdims=True)
    lists_ref[:, len(KINDS) * stride + LANES :] = by_column.astype(jnp.int32)
    copy = pltpu.make_async_copy(lists_ref, out_ref, sem)
    copy.start()
    copy.wait()


def turn_kernel(pairs_blocks_ref, moments_in_ref, blocks_ref, moments_ref, sem):
    moments_ref[...] = moments_in_ref[...]
    slot_count = pairs_blocks_ref.shape[0]
    copy = pltpu.make_async_copy(pairs_blocks_ref, blocks_ref.at[pl.ds(0, slot_count)], sem)
    copy.start()

    def one_group(group, carry):
        for step in range(TURN_GROUP):
            slot = group * TURN_GROUP + step
            blocks_ref[slot_count + slot] = jnp.transpose(pairs_blocks_ref[slot])
        return carry

    lax.fori_loop(0, slot_count // TURN_GROUP, one_group, 0)
    copy.wait()


def add_products(lists_ref, blocks_ref, slot_count, field, total, index, size, source_from=0, target_from=0):
    stride = list_stride(slot_count)
    idle = lists_ref[0, index * stride + stride - 1] >> 16
    count = lists_ref[0, len(KINDS) * stride + index]
    column_count = lists_ref[0, len(KINDS) * stride + LANES + index]

    def add_part(first, end, kind, plain, cuts):
        def one_group(group, carry):
            results = []
            for step in range(size):
                place = first + group * size + step
                entry = lists_ref[0, index * stride + place]
                block, source, target = entry & 255, (entry >> 8) & 255, entry >> 16
                if plain:
                    block = jnp.where(block >= slot_count, block - slot_count, block)
                if cuts:
                    target = jnp.where(place < end, target, idle)
                value = kind(field[source - source_from].astype(BF16), blocks_ref[block])
                results.append((target - target_from, value))
            for at, value in results:
                total[at] += value
            return carry

        lax.fori_loop(0, (end - first + size - 1) // size, one_group, 0)

    if blocks_ref.shape[0] > slot_count:
        add_part(0, count, times, False, False)
    else:
        add_part(0, column_count, times, True, True)
        add_part(column_count, count, times_transposed, True, False)


def lay_out(row_ref, field, first, block_len):
    for block in range(row_ref.shape[1] // block_len):
        piece = row_ref[:, block * block_len : (block + 1) * block_len]
        field[first + block] = piece.astype(F32)


def early_kernel(sub_count, slot_count, lists_ref, blocks_ref, diag_ref, noise_ref, own_ref, *refs):
    row_refs, (total, field) = refs[:-2], refs[-2:]
    block_len = blocks_ref.shape[1]
    sub_index, blocks_dev, own_first, _ = device_place(block_len, own_ref, sub_count)
    for step, row_ref in enumerate(row_refs):
        lay_out(row_ref, field, (sub_index ^ step) * blocks_dev, block_len)
    for block in range(total.shape[0]):
        total[block] = jnp.zeros(total.shape[1:], F32)
    for block in range(blocks_dev):
        span = slice(block * block_len, (block + 1) * block_len)
        value = noise_ref[:, span] * own_ref[:, span]
        total[own_first + block] = value + times(field[own_first + block].astype(BF16), diag_ref[block])
    add_products(lists_ref, blocks_ref, slot_count, field, total, EARLY, LONG_GROUP)


def ahead_kernel(sub_count, slot_count, lists_ref, blocks_ref, begun_ref, *refs):
    row_refs = refs[:sub_count]
    even_ref, odd_ref, field_ref, total = refs[sub_count:]
    block_len = blocks_ref.shape[1]
    sub_index, blocks_dev, _, tile_blocks = device_place(block_len, even_ref, sub_count)
    for step, row_ref in enumerate(row_refs):
        lay_out(row_ref, field_ref, (sub_index ^ step) * blocks_dev, block_len)
    for block in range(blocks_dev):
        total[block] = begun_ref[tile_blocks + block]
    total[blocks_dev] = jnp.zeros(total.shape[1:], F32)
    add_products(lists_ref, blocks_ref, slot_count, field_ref, total, AHEAD, SHORT_GROUP, 0, tile_blocks)
    is_odd = lax.axis_index("tile") % 2 == 1
    for block in range(blocks_dev):
        span = slice(block * block_len, (block + 1) * block_len)
        products = total[block]
        first_row = field_ref[block]
        even_ref[:, span] = jnp.where(is_odd, first_row, products).astype(BF16)
        odd_ref[:, span] = jnp.where(is_odd, products, first_row).astype(BF16)


def late_kernel(slot_count, lists_ref, blocks_ref, begun_ref, field_ref, total):
    total[...] = begun_ref[...]
    add_products(lists_ref, blocks_ref, slot_count, field_ref, total, LATE, LONG_GROUP)


def part_kernel(
    sub_count, slot_count, is_last, lists_ref, blocks_ref, begun_ref, field_ref, even_ref, odd_ref,
    moments_in_ref, *refs
):
    part_refs = refs[:sub_count]
    moments_ref, total, ahead = refs[sub_count:]
    block_len = blocks_ref.shape[1]
    sub_index, blocks_dev, own_first, tile_blocks = device_place(block_len, even_ref, sub_count)
    is_odd = lax.axis_index("tile") % 2 == 1
    for block in range(blocks_dev):
        span = slice(block * block_len, (block + 1) * block_len)
        even = even_ref[:, span].astype(F32)
        odd = odd_ref[:, span].astype(F32)
        ahead[block] = jnp.where(is_odd, odd, even)
        total[block] = begun_ref[block] + jnp.where(is_odd, even, odd)
    for block in range(blocks_dev, tile_blocks):
        total[block] = begun_ref[block]
    total[begun_ref.shape[0] - 1] = jnp.zeros(total.shape[1:], F32)
    add_products(lists_ref, blocks_ref, slot_count, ahead, total, FROM_AHEAD, SHORT_GROUP, tile_blocks, 0)
    for step in range(sub_count):
        first = (sub_index ^ step) * blocks_dev
        for block in range(blocks_dev):
            span = slice(block * block_len, (block + 1) * block_len)
            part_refs[step][:, span] = total[first + block].astype(part_refs[step].dtype)
    moments = moments_in_ref[...]
    if is_last:
        product = jnp.zeros(total.shape[1:], F32)
        for block in range(tile_blocks):
            product += field_ref[block] * total[block]
        lane = lax.broadcasted_iota(jnp.int32, moments.shape, 1)
        moments = jnp.where(lane == 2 * ITERS - 1, jnp.sum(product, axis=1, keepdims=True), moments)
    moments_ref[...] = moments


def join_kernel(index, own_ref, old_ref, moments_in_ref, *refs):
    part_refs = refs[:-3]
    next_ref, rounded_ref, moments_ref = refs[-3:]
    value = own_ref[...]
    for part_ref in part_refs:
        value += part_ref[...].astype(F32)
    next_ref[...] = value
    rounded_ref[...] = value.astype(BF16)
    old = old_ref[...]
    lane = lax.broadcasted_iota(jnp.int32, moments_ref.shape, 1)
    moments = moments_in_ref[...] if index else jnp.zeros(moments_ref.shape, F32)
    found = {2 * index + 1: old * value, 2 * index + 2: value * value}
    if index == 0:
        found[0] = old * old
    for order, product in found.items():
        moments = jnp.where(lane == order, jnp.sum(product, axis=1, keepdims=True), moments)
    moments_ref[...] = moments


def finish_kernel(sub_count, moments_ref, *refs):
    part_refs, basis_refs = refs[:sub_count], refs[sub_count:-2]
    solution_ref, residual_ref = refs[-2:]
    moments = [moments_ref[:, order : order + 1] for order in range(2 * ITERS)]

    def inner(first, second, shift):
        value = 0.0
        for i, a in enumerate(first):
            for j, b in enumerate(second):
                value = value + a * b * moments[i + j + shift]
        return value

    one = jnp.ones_like(moments[0])
    zero = jnp.zeros_like(one)
    direction, residual = [one], [one]
    answer = [zero] * ITERS
    norm_now = moments[0]
    for iteration in range(ITERS):
        step_size = norm_now / inner(direction, direction, 1)
        for power, weight in enumerate(direction):
            answer[power] = answer[power] + step_size * weight
        residual = residual + [zero]
        for power, weight in enumerate(direction):
            residual[power + 1] = residual[power + 1] - step_size * weight
        if iteration + 1 < ITERS:
            norm_next = inner(residual, residual, 0)
            direction = [
                value + (norm_next / norm_now) * old
                for value, old in zip(residual, direction + [zero])
            ]
            norm_now = norm_next
    fields = [basis_ref[...] for basis_ref in basis_refs]
    fields.append(sum(part_ref[...].astype(F32) for part_ref in part_refs))
    solution_ref[...] = sum(weight * field for weight, field in zip(answer, fields))
    residual_ref[...] = sum(weight * field for weight, field in zip(residual, fields))


def shape(rows, columns, kind):
    return jax.ShapeDtypeStruct((rows, columns), kind)


def exchange(block, axis, step):
    count = lax.axis_size(axis)
    return lax.ppermute(block, axis, [(i, i ^ step) for i in range(count)])


def swap(block, axis, first):
    count = lax.axis_size(axis)
    route = []
    for i in range(first, count - 1, 2):
        route += [(i, i + 1), (i + 1, i)]
    return lax.ppermute(block, axis, route)


def call(kernel, outs, ins, name, cost=0, **options):
    single = not isinstance(outs, tuple)
    specs = [SMEM if value.dtype == jnp.int32 else VMEM for value in ins]
    options.setdefault("in_specs", specs)
    options.setdefault("out_specs", VMEM if single else (VMEM,) * len(outs))
    return pl.pallas_call(
        kernel,
        out_shape=outs,
        compiler_params=PARAMS,
        name=name,
        cost_estimate=pl.CostEstimate(flops=int(cost * 1e9), bytes_accessed=0, transcendentals=0),
        **options,
    )(*ins)


def on_device(right_side, point_order, noise_var, block_pairs, pair_blocks, diag_blocks):
    sub_count = lax.axis_size("sub")
    tile_count = lax.axis_size("tile")
    rhs_count, points_dev = right_side.shape
    blocks_dev, block_len = diag_blocks.shape[:2]
    extended = (sub_count + 1) * blocks_dev
    noise = noise_var[None, :]
    full = shape(rhs_count, points_dev, F32)
    half = shape(rhs_count, points_dev, BF16)
    scalars = shape(rhs_count, LANES, F32)
    sums = jax.ShapeDtypeStruct((extended + 1, rhs_count, block_len), F32)

    def scratch(blocks):
        return pltpu.VMEM((blocks, rhs_count, block_len), F32)

    slot_count = pair_blocks.shape[0]
    width = -(-slot_count // LANES) * LANES
    assert 2 * width <= 256 and extended < 256 and slot_count % TURN_GROUP == 0
    lists_shape = (1, len(KINDS) * list_stride(slot_count) + 2 * LANES)
    lists = call(
        functools.partial(lists_kernel, sub_count, blocks_dev, slot_count),
        pltpu.SMEM(lists_shape, jnp.int32),
        (block_pairs.T,),
        "lists",
        1,
        in_specs=[VMEM],
        out_specs=SMEM,
        scratch_shapes=[
            pltpu.VMEM((8, width), F32),
            pltpu.VMEM(lists_shape, jnp.int32),
            pltpu.SemaphoreType.DMA(()),
        ],
    )
    blocks = pair_blocks
    field, rounded = call(order_kernel, (full, half), (right_side, point_order), "curve_order", 10, in_specs=[VMEM, VMEM])
    basis = [field]
    moments = jnp.zeros(scalars.shape, F32)
    for index in range(ITERS):
        is_last = index + 1 == ITERS
        rows = [rounded] + [exchange(rounded, "sub", step) for step in range(1, sub_count)]
        begun = call(
            functools.partial(early_kernel, sub_count, slot_count),
            sums,
            (lists, blocks, diag_blocks, noise, field, *rows[:2]),
            "early",
            3,
            scratch_shapes=[scratch(extended)],
        )
        even, odd, tile_field = call(
            functools.partial(ahead_kernel, sub_count, slot_count),
            (half, half, jax.ShapeDtypeStruct((sub_count * blocks_dev, rhs_count, block_len), F32)),
            (lists, blocks, begun, *rows),
            "ahead",
            1,
            scratch_shapes=[scratch(blocks_dev + 1)],
        )
        even = swap(even, "tile", 0)
        odd = swap(odd, "tile", 1)
        begun = call(functools.partial(late_kernel, slot_count), sums, (lists, blocks, begun, tile_field), "late", 3)
        part = shape(rhs_count, points_dev, F32 if is_last else BF16)
        *parts, moments = call(
            functools.partial(part_kernel, sub_count, slot_count, is_last),
            (full,) + (part,) * (sub_count - 1) + (scalars,),
            (lists, blocks, begun, tile_field, even, odd, moments),
            "parts",
            1,
            scratch_shapes=[scratch(extended + 1), scratch(blocks_dev)],
        )
        if is_last:
            break
        if index == 0:
            blocks, moments = call(
                turn_kernel,
                (pltpu.VMEM((2 * slot_count, block_len, block_len), BF16), scalars),
                (pair_blocks, moments),
                "turn",
                4,
                scratch_shapes=[pltpu.SemaphoreType.DMA(())],
            )
        arrived = [exchange(parts[step], "sub", step) for step in range(1, sub_count)]
        field, rounded, moments = call(
            functools.partial(join_kernel, index),
            (full, half, scalars),
            (parts[0], field, moments, *arrived),
            "join",
        )
        basis.append(field)
    arrived = []
    for axis, count in (("sub", sub_count), ("tile", tile_count)):
        step = 1
        while step < count:
            moments = moments + exchange(moments, axis, step)
            if len(arrived) < sub_count - 1:
                far = sub_count - 1 - len(arrived)
                arrived.append(exchange(parts[far], "sub", far))
                moments, *parts = lax.optimization_barrier((moments, *parts))
            step *= 2
    for far in range(sub_count - 1 - len(arrived), 0, -1):
        arrived.append(exchange(parts[far], "sub", far))
    return call(
        functools.partial(finish_kernel, sub_count),
        (full, full),
        (moments, parts[0], *arrived, *basis),
        "finish",
    )


def solution(mesh):
    placed = (
        P(None, ("tile", "sub")),
        P(("tile", "sub"), None),
        P(("tile", "sub")),
        P(("tile", "sub"), None),
        P(("tile", "sub"), None, None),
        P(("tile", "sub"), None, None),
    )
    return jax.shard_map(
        on_device,
        mesh=mesh,
        in_specs=placed,
        out_specs=(P(None, ("tile", "sub")), P(None, ("tile", "sub"))),
        check_vma=False,
    )
```

```python
import functools

import jax
import jax.numpy as jnp
from jax import lax
from jax.experimental import pallas as pl
from jax.experimental.pallas import tpu as pltpu
from jax.sharding import PartitionSpec as P

ITERS = 3
LANES = 128
LONG_GROUP = 16
SHORT_GROUP = 8
TURN_GROUP = 4
F32 = jnp.float32
BF16 = jnp.bfloat16
VMEM = pl.BlockSpec(memory_space=pltpu.VMEM)
SMEM = pl.BlockSpec(memory_space=pltpu.SMEM)
EARLY, AHEAD, LATE, FROM_AHEAD = KINDS = range(4)
PARAMS = pltpu.CompilerParams(vmem_limit_bytes=4 * 1024 * 1024)


def times(field, block):
    return lax.dot_general(field, block, (((1,), (0,)), ((), ())), preferred_element_type=F32)


def times_transposed(field, block):
    return lax.dot_general(field, block, (((1,), (1,)), ((), ())), preferred_element_type=F32)


def order_kernel(right_ref, order_ref, curve_ref, rounded_ref):
    rhs_count, points = right_ref.shape
    for start in range(0, points, LANES):
        at = jnp.broadcast_to(order_ref[:, start : start + LANES], (rhs_count, LANES))
        chunk = at // LANES
        lane = at % LANES
        result = jnp.zeros((rhs_count, LANES), F32)
        for source in range(points // LANES):
            values = right_ref[:, source * LANES : (source + 1) * LANES]
            picked = jnp.take_along_axis(values, lane, axis=1)
            result = jnp.where(chunk == source, picked, result)
        curve_ref[:, start : start + LANES] = result
        rounded_ref[:, start : start + LANES] = result.astype(BF16)


def device_place(block_len, field_ref, sub_count):
    blocks_dev = field_ref.shape[1] // block_len
    sub_index = lax.axis_index("sub")
    return sub_index, blocks_dev, sub_index * blocks_dev, blocks_dev * sub_count


def list_stride(slot_count):
    return -(-(2 * slot_count + LONG_GROUP) // LANES) * LANES


def lists_kernel(sub_count, blocks_dev, slot_count, pairs_ref, out_ref, padded, lists_ref, sem):
    width = padded.shape[1]
    stride = list_stride(slot_count)
    sub_index = lax.axis_index("sub")
    tile_blocks = blocks_dev * sub_count
    first_block = lax.axis_index("tile") * tile_blocks
    padded[...] = jnp.full(padded.shape, -1.0, F32)
    padded[0:2, 0:slot_count] = pairs_ref[...].astype(F32)
    by_lane = padded[...]
    by_row = jnp.transpose(by_lane)

    def sides(row, col, axis):
        live = jnp.concatenate([row, row], axis) >= 0.0
        row = row.astype(jnp.int32) - first_block
        col = col.astype(jnp.int32) - first_block
        source = jnp.concatenate([row, col], axis)
        target = jnp.concatenate([col, row], axis)
        return live, source, target

    live, source, target = sides(by_row[:, 0:1], by_row[:, 1:2], 0)
    kind = jnp.where(target >= tile_blocks, AHEAD, LATE)
    first_row = (sub_index // 2) * (2 * blocks_dev)
    is_early = (source >= first_row) & (source < first_row + 2 * blocks_dev) & (source < tile_blocks)
    kind = jnp.where(is_early, EARLY, kind)
    kind = jnp.where(source >= tile_blocks, FROM_AHEAD, kind)
    kind = jnp.where(live, kind, -1)
    hot = (kind == lax.broadcasted_iota(jnp.int32, (2 * width, LANES), 1)).astype(F32)
    below = lax.broadcasted_iota(jnp.int32, (2 * width, 2 * width), 0) > lax.broadcasted_iota(
        jnp.int32, (2 * width, 2 * width), 1
    )
    ranks = times(below.astype(F32).astype(BF16), hot.astype(BF16))
    rank = jnp.sum(ranks * hot, axis=1, keepdims=True).astype(jnp.int32)
    counts = jnp.sum(hot, axis=0, keepdims=True)
    at = jnp.where(live, kind * stride + rank, -1)
    spread = at == lax.broadcasted_iota(jnp.int32, (2 * width, len(KINDS) * stride), 1)
    live, source, target = sides(by_lane[0:1, :], by_lane[1:2, :], 1)
    lane = lax.broadcasted_iota(jnp.int32, (1, 2 * width), 1)
    block = jnp.where(lane < width, lane, lane - width + slot_count)
    fields = jnp.concatenate(
        [jnp.where(live, value, 0).astype(F32) for value in (block, source, target)]
        + [jnp.zeros((5, 2 * width), F32)],
        0,
    )
    found = times(fields.astype(BF16), spread.astype(F32).astype(BF16))
    entries = found[0:1] + 256.0 * found[1:2] + 65536.0 * found[2:3]
    entries = entries.astype(jnp.int32)
    idle = (tile_blocks + blocks_dev) * 65536
    idle_source = {
        EARLY: sub_index * blocks_dev,
        AHEAD: tile_blocks - blocks_dev,
        LATE: 0,
        FROM_AHEAD: tile_blocks,
    }
    place = lax.broadcasted_iota(jnp.int32, (1, stride), 1)
    for index in KINDS:
        span = slice(index * stride, (index + 1) * stride)
        count = counts[:, index : index + 1].astype(jnp.int32)
        lists_ref[:, span] = jnp.where(place < count, entries[:, span], idle + 256 * idle_source[index])
    lists_ref[:, len(KINDS) * stride : len(KINDS) * stride + LANES] = counts.astype(jnp.int32)
    by_column = jnp.sum(hot[:width], axis=0, keepdims=True)
    lists_ref[:, len(KINDS) * stride + LANES :] = by_column.astype(jnp.int32)
    copy = pltpu.make_async_copy(lists_ref, out_ref, sem)
    copy.start()
    copy.wait()


def turn_kernel(pairs_blocks_ref, after_ref, blocks_ref, sem):
    slot_count = pairs_blocks_ref.shape[0]
    copy = pltpu.make_async_copy(pairs_blocks_ref, blocks_ref.at[pl.ds(0, slot_count)], sem)
    copy.start()

    def one_group(group, carry):
        for step in range(TURN_GROUP):
            slot = group * TURN_GROUP + step
            blocks_ref[slot_count + slot] = jnp.transpose(pairs_blocks_ref[slot])
        return carry

    lax.fori_loop(0, slot_count // TURN_GROUP, one_group, 0)
    copy.wait()


def add_products(lists_ref, blocks_ref, slot_count, field, total, index, size, source_from=0, target_from=0):
    stride = list_stride(slot_count)
    idle = lists_ref[0, index * stride + stride - 1] >> 16
    count = lists_ref[0, len(KINDS) * stride + index]
    column_count = lists_ref[0, len(KINDS) * stride + LANES + index]

    def add_part(first, end, kind, plain, cuts):
        def one_group(group, carry):
            results = []
            for step in range(size):
                place = first + group * size + step
                entry = lists_ref[0, index * stride + place]
                block, source, target = entry & 255, (entry >> 8) & 255, entry >> 16
                if plain:
                    block = jnp.where(block >= slot_count, block - slot_count, block)
                if cuts:
                    target = jnp.where(place < end, target, idle)
                value = kind(field[source - source_from].astype(BF16), blocks_ref[block])
                results.append((target - target_from, value))
            for at, value in results:
                total[at] += value
            return carry

        lax.fori_loop(0, (end - first + size - 1) // size, one_group, 0)

    if blocks_ref.shape[0] > slot_count:
        add_part(0, count, times, False, False)
    else:
        add_part(0, column_count, times, True, True)
        add_part(column_count, count, times_transposed, True, False)


def lay_out(row_ref, field, first, block_len):
    for block in range(row_ref.shape[1] // block_len):
        piece = row_ref[:, block * block_len : (block + 1) * block_len]
        field[first + block] = piece.astype(F32)


def early_kernel(sub_count, slot_count, lists_ref, blocks_ref, diag_ref, noise_ref, own_ref, *refs):
    row_refs, (total, field) = refs[:-2], refs[-2:]
    block_len = blocks_ref.shape[1]
    sub_index, blocks_dev, own_first, _ = device_place(block_len, own_ref, sub_count)
    for step, row_ref in enumerate(row_refs):
        lay_out(row_ref, field, (sub_index ^ step) * blocks_dev, block_len)
    for block in range(total.shape[0]):
        total[block] = jnp.zeros(total.shape[1:], F32)
    for block in range(blocks_dev):
        span = slice(block * block_len, (block + 1) * block_len)
        value = noise_ref[:, span] * own_ref[:, span]
        total[own_first + block] = value + times(field[own_first + block].astype(BF16), diag_ref[block])
    add_products(lists_ref, blocks_ref, slot_count, field, total, EARLY, LONG_GROUP)


def ahead_kernel(sub_count, slot_count, lists_ref, blocks_ref, begun_ref, *refs):
    row_refs = refs[:sub_count]
    even_ref, odd_ref, field_ref, total = refs[sub_count:]
    block_len = blocks_ref.shape[1]
    sub_index, blocks_dev, _, tile_blocks = device_place(block_len, even_ref, sub_count)
    for step, row_ref in enumerate(row_refs):
        lay_out(row_ref, field_ref, (sub_index ^ step) * blocks_dev, block_len)
    for block in range(blocks_dev):
        total[block] = begun_ref[tile_blocks + block]
    total[blocks_dev] = jnp.zeros(total.shape[1:], F32)
    add_products(lists_ref, blocks_ref, slot_count, field_ref, total, AHEAD, SHORT_GROUP, 0, tile_blocks)
    is_odd = lax.axis_index("tile") % 2 == 1
    for block in range(blocks_dev):
        span = slice(block * block_len, (block + 1) * block_len)
        products = total[block]
        first_row = field_ref[block]
        even_ref[:, span] = jnp.where(is_odd, first_row, products).astype(BF16)
        odd_ref[:, span] = jnp.where(is_odd, products, first_row).astype(BF16)


def late_kernel(slot_count, lists_ref, blocks_ref, begun_ref, field_ref, total):
    total[...] = begun_ref[...]
    add_products(lists_ref, blocks_ref, slot_count, field_ref, total, LATE, LONG_GROUP)


def part_kernel(
    sub_count, slot_count, is_last, lists_ref, blocks_ref, begun_ref, field_ref, even_ref, odd_ref,
    moments_in_ref, *refs
):
    part_refs = refs[:sub_count]
    moments_ref, total, ahead = refs[sub_count:]
    block_len = blocks_ref.shape[1]
    sub_index, blocks_dev, own_first, tile_blocks = device_place(block_len, even_ref, sub_count)
    is_odd = lax.axis_index("tile") % 2 == 1
    for block in range(blocks_dev):
        span = slice(block * block_len, (block + 1) * block_len)
        even = even_ref[:, span].astype(F32)
        odd = odd_ref[:, span].astype(F32)
        ahead[block] = jnp.where(is_odd, odd, even)
        total[block] = begun_ref[block] + jnp.where(is_odd, even, odd)
    for block in range(blocks_dev, tile_blocks):
        total[block] = begun_ref[block]
    total[begun_ref.shape[0] - 1] = jnp.zeros(total.shape[1:], F32)
    add_products(lists_ref, blocks_ref, slot_count, ahead, total, FROM_AHEAD, SHORT_GROUP, tile_blocks, 0)
    for step in range(sub_count):
        first = (sub_index ^ step) * blocks_dev
        for block in range(blocks_dev):
            span = slice(block * block_len, (block + 1) * block_len)
            part_refs[step][:, span] = total[first + block].astype(part_refs[step].dtype)
    moments = moments_in_ref[...]
    if is_last:
        product = jnp.zeros(total.shape[1:], F32)
        for block in range(tile_blocks):
            product += field_ref[block] * total[block]
        lane = lax.broadcasted_iota(jnp.int32, moments.shape, 1)
        moments = jnp.where(lane == 2 * ITERS - 1, jnp.sum(product, axis=1, keepdims=True), moments)
    moments_ref[...] = moments


def join_kernel(index, after_ref, own_ref, old_ref, moments_in_ref, *refs):
    part_refs = refs[:-3]
    next_ref, rounded_ref, moments_ref = refs[-3:]
    value = own_ref[...]
    for part_ref in part_refs:
        value += part_ref[...].astype(F32)
    next_ref[...] = value
    rounded_ref[...] = value.astype(BF16)
    old = old_ref[...]
    lane = lax.broadcasted_iota(jnp.int32, moments_ref.shape, 1)
    moments = moments_in_ref[...] if index else jnp.zeros(moments_ref.shape, F32)
    found = {2 * index + 1: old * value, 2 * index + 2: value * value}
    if index == 0:
        found[0] = old * old
    for order, product in found.items():
        moments = jnp.where(lane == order, jnp.sum(product, axis=1, keepdims=True), moments)
    moments_ref[...] = moments


def finish_kernel(sub_count, moments_ref, *refs):
    part_refs, basis_refs = refs[:sub_count], refs[sub_count:-2]
    solution_ref, residual_ref = refs[-2:]
    moments = [moments_ref[:, order : order + 1] for order in range(2 * ITERS)]

    def inner(first, second, shift):
        value = 0.0
        for i, a in enumerate(first):
            for j, b in enumerate(second):
                value = value + a * b * moments[i + j + shift]
        return value

    one = jnp.ones_like(moments[0])
    zero = jnp.zeros_like(one)
    direction, residual = [one], [one]
    answer = [zero] * ITERS
    norm_now = moments[0]
    for iteration in range(ITERS):
        step_size = norm_now / inner(direction, direction, 1)
        for power, weight in enumerate(direction):
            answer[power] = answer[power] + step_size * weight
        residual = residual + [zero]
        for power, weight in enumerate(direction):
            residual[power + 1] = residual[power + 1] - step_size * weight
        if iteration + 1 < ITERS:
            norm_next = inner(residual, residual, 0)
            direction = [
                value + (norm_next / norm_now) * old
                for value, old in zip(residual, direction + [zero])
            ]
            norm_now = norm_next
    fields = [basis_ref[...] for basis_ref in basis_refs]
    fields.append(sum(part_ref[...].astype(F32) for part_ref in part_refs))
    solution_ref[...] = sum(weight * field for weight, field in zip(answer, fields))
    residual_ref[...] = sum(weight * field for weight, field in zip(residual, fields))


def shape(rows, columns, kind):
    return jax.ShapeDtypeStruct((rows, columns), kind)


def exchange(block, axis, step):
    count = lax.axis_size(axis)
    return lax.ppermute(block, axis, [(i, i ^ step) for i in range(count)])


def swap(block, axis, first):
    count = lax.axis_size(axis)
    route = []
    for i in range(first, count - 1, 2):
        route += [(i, i + 1), (i + 1, i)]
    return lax.ppermute(block, axis, route)


def call(kernel, outs, ins, name, cost=0, **options):
    single = not isinstance(outs, tuple)
    specs = [SMEM if value.dtype == jnp.int32 else VMEM for value in ins]
    options.setdefault("in_specs", specs)
    options.setdefault("out_specs", VMEM if single else (VMEM,) * len(outs))
    return pl.pallas_call(
        kernel,
        out_shape=outs,
        compiler_params=PARAMS,
        name=name,
        cost_estimate=pl.CostEstimate(flops=int(cost * 1e9), bytes_accessed=0, transcendentals=0),
        **options,
    )(*ins)


def on_device(right_side, point_order, noise_var, block_pairs, pair_blocks, diag_blocks):
    sub_count = lax.axis_size("sub")
    tile_count = lax.axis_size("tile")
    rhs_count, points_dev = right_side.shape
    blocks_dev, block_len = diag_blocks.shape[:2]
    extended = (sub_count + 1) * blocks_dev
    noise = noise_var[None, :]
    full = shape(rhs_count, points_dev, F32)
    half = shape(rhs_count, points_dev, BF16)
    scalars = shape(rhs_count, LANES, F32)
    sums = jax.ShapeDtypeStruct((extended + 1, rhs_count, block_len), F32)

    def scratch(blocks):
        return pltpu.VMEM((blocks, rhs_count, block_len), F32)

    slot_count = pair_blocks.shape[0]
    width = -(-slot_count // LANES) * LANES
    assert 2 * width <= 256 and extended < 256 and slot_count % TURN_GROUP == 0
    lists_shape = (1, len(KINDS) * list_stride(slot_count) + 2 * LANES)
    lists = call(
        functools.partial(lists_kernel, sub_count, blocks_dev, slot_count),
        pltpu.SMEM(lists_shape, jnp.int32),
        (block_pairs.T,),
        "lists",
        1,
        in_specs=[VMEM],
        out_specs=SMEM,
        scratch_shapes=[
            pltpu.VMEM((8, width), F32),
            pltpu.VMEM(lists_shape, jnp.int32),
            pltpu.SemaphoreType.DMA(()),
        ],
    )
    blocks = pair_blocks
    field, rounded = call(order_kernel, (full, half), (right_side, point_order), "curve_order", 10, in_specs=[VMEM, VMEM])
    basis = [field]
    moments = jnp.zeros(scalars.shape, F32)
    for index in range(ITERS):
        is_last = index + 1 == ITERS
        rows = [rounded] + [exchange(rounded, "sub", step) for step in range(1, sub_count)]
        begun = call(
            functools.partial(early_kernel, sub_count, slot_count),
            sums,
            (lists, blocks, diag_blocks, noise, field, *rows[:2]),
            "early",
            3,
            scratch_shapes=[scratch(extended)],
        )
        even, odd, tile_field = call(
            functools.partial(ahead_kernel, sub_count, slot_count),
            (half, half, jax.ShapeDtypeStruct((sub_count * blocks_dev, rhs_count, block_len), F32)),
            (lists, blocks, begun, *rows),
            "ahead",
            1,
            scratch_shapes=[scratch(blocks_dev + 1)],
        )
        even = swap(even, "tile", 0)
        odd = swap(odd, "tile", 1)
        begun = call(functools.partial(late_kernel, slot_count), sums, (lists, blocks, begun, tile_field), "late", 3)
        part = shape(rhs_count, points_dev, F32 if is_last else BF16)
        *parts, moments = call(
            functools.partial(part_kernel, sub_count, slot_count, is_last),
            (full,) + (part,) * (sub_count - 1) + (scalars,),
            (lists, blocks, begun, tile_field, even, odd, moments),
            "parts",
            1,
            scratch_shapes=[scratch(extended + 1), scratch(blocks_dev)],
        )
        if is_last:
            break
        if index == 0:
            blocks = call(
                turn_kernel,
                pltpu.VMEM((2 * slot_count, block_len, block_len), BF16),
                (pair_blocks, moments),
                "turn",
                4,
                scratch_shapes=[pltpu.SemaphoreType.DMA(())],
            )
        arrived = [exchange(parts[step], "sub", step) for step in range(1, sub_count)]
        field, rounded, moments = call(
            functools.partial(join_kernel, index),
            (full, half, scalars),
            (blocks, parts[0], field, moments, *arrived),
            "join",
        )
        basis.append(field)
    arrived = []
    for axis, count in (("sub", sub_count), ("tile", tile_count)):
        step = 1
        while step < count:
            moments = moments + exchange(moments, axis, step)
            if len(arrived) < sub_count - 1:
                far = sub_count - 1 - len(arrived)
                arrived.append(exchange(parts[far], "sub", far))
                moments, *parts = lax.optimization_barrier((moments, *parts))
            step *= 2
    for far in range(sub_count - 1 - len(arrived), 0, -1):
        arrived.append(exchange(parts[far], "sub", far))
    return call(
        functools.partial(finish_kernel, sub_count),
        (full, full),
        (moments, parts[0], *arrived, *basis),
        "finish",
    )


def solution(mesh):
    placed = (
        P(None, ("tile", "sub")),
        P(("tile", "sub"), None),
        P(("tile", "sub")),
        P(("tile", "sub"), None),
        P(("tile", "sub"), None, None),
        P(("tile", "sub"), None, None),
    )
    return jax.shard_map(
        on_device,
        mesh=mesh,
        in_specs=placed,
        out_specs=(P(None, ("tile", "sub")), P(None, ("tile", "sub"))),
        check_vma=False,
    )
```

```python
import functools

import jax
import jax.numpy as jnp
from jax import lax
from jax.experimental import pallas as pl
from jax.experimental.pallas import tpu as pltpu
from jax.sharding import PartitionSpec as P

ITERS = 3
LANES = 128
LONG_GROUP = 16
SHORT_GROUP = 8
TURN_GROUP = 4
F32 = jnp.float32
BF16 = jnp.bfloat16
VMEM = pl.BlockSpec(memory_space=pltpu.VMEM)
SMEM = pl.BlockSpec(memory_space=pltpu.SMEM)
EARLY, AHEAD, LATE, FROM_AHEAD = KINDS = range(4)
PARAMS = pltpu.CompilerParams(vmem_limit_bytes=4 * 1024 * 1024)


def times(field, block):
    return lax.dot_general(field, block, (((1,), (0,)), ((), ())), preferred_element_type=F32)


def times_transposed(field, block):
    return lax.dot_general(field, block, (((1,), (1,)), ((), ())), preferred_element_type=F32)


def order_kernel(right_in, order_in, curve_ref, rounded_ref, right_ref, order_ref, sems):
    copies = [
        pltpu.make_async_copy(right_in, right_ref, sems.at[0]),
        pltpu.make_async_copy(order_in, order_ref, sems.at[1]),
    ]
    for copy in copies:
        copy.start()
    for copy in copies:
        copy.wait()
    rhs_count, points = right_ref.shape
    for start in range(0, points, LANES):
        at = jnp.broadcast_to(order_ref[:, start : start + LANES], (rhs_count, LANES))
        chunk = at // LANES
        lane = at % LANES
        result = jnp.zeros((rhs_count, LANES), F32)
        for source in range(points // LANES):
            values = right_ref[:, source * LANES : (source + 1) * LANES]
            picked = jnp.take_along_axis(values, lane, axis=1)
            result = jnp.where(chunk == source, picked, result)
        curve_ref[:, start : start + LANES] = result
        rounded_ref[:, start : start + LANES] = result.astype(BF16)


def device_place(block_len, field_ref, sub_count):
    blocks_dev = field_ref.shape[1] // block_len
    sub_index = lax.axis_index("sub")
    return sub_index, blocks_dev, sub_index * blocks_dev, blocks_dev * sub_count


def list_stride(slot_count):
    return -(-(2 * slot_count + LONG_GROUP) // LANES) * LANES


def lists_kernel(sub_count, blocks_dev, slot_count, pairs_ref, out_ref, padded, lists_ref, sem):
    width = padded.shape[1]
    stride = list_stride(slot_count)
    sub_index = lax.axis_index("sub")
    tile_blocks = blocks_dev * sub_count
    first_block = lax.axis_index("tile") * tile_blocks
    padded[...] = jnp.full(padded.shape, -1.0, F32)
    padded[0:2, 0:slot_count] = pairs_ref[...].astype(F32)
    by_lane = padded[...]
    by_row = jnp.transpose(by_lane)

    def sides(row, col, axis):
        live = jnp.concatenate([row, row], axis) >= 0.0
        row = row.astype(jnp.int32) - first_block
        col = col.astype(jnp.int32) - first_block
        source = jnp.concatenate([row, col], axis)
        target = jnp.concatenate([col, row], axis)
        return live, source, target

    live, source, target = sides(by_row[:, 0:1], by_row[:, 1:2], 0)
    kind = jnp.where(target >= tile_blocks, AHEAD, LATE)
    first_own = sub_index * blocks_dev
    is_early = (source >= first_own) & (source < first_own + blocks_dev)
    kind = jnp.where(is_early, EARLY, kind)
    kind = jnp.where(source >= tile_blocks, FROM_AHEAD, kind)
    kind = jnp.where(live, kind, -1)
    hot = (kind == lax.broadcasted_iota(jnp.int32, (2 * width, LANES), 1)).astype(F32)
    below = lax.broadcasted_iota(jnp.int32, (2 * width, 2 * width), 0) > lax.broadcasted_iota(
        jnp.int32, (2 * width, 2 * width), 1
    )
    ranks = times(below.astype(F32).astype(BF16), hot.astype(BF16))
    rank = jnp.sum(ranks * hot, axis=1, keepdims=True).astype(jnp.int32)
    counts = jnp.sum(hot, axis=0, keepdims=True)
    at = jnp.where(live, kind * stride + rank, -1)
    spread = at == lax.broadcasted_iota(jnp.int32, (2 * width, len(KINDS) * stride), 1)
    live, source, target = sides(by_lane[0:1, :], by_lane[1:2, :], 1)
    lane = lax.broadcasted_iota(jnp.int32, (1, 2 * width), 1)
    block = jnp.where(lane < width, lane, lane - width + slot_count)
    fields = jnp.concatenate(
        [jnp.where(live, value, 0).astype(F32) for value in (block, source, target)]
        + [jnp.zeros((5, 2 * width), F32)],
        0,
    )
    found = times(fields.astype(BF16), spread.astype(F32).astype(BF16))
    entries = found[0:1] + 256.0 * found[1:2] + 65536.0 * found[2:3]
    entries = entries.astype(jnp.int32)
    idle = (tile_blocks + blocks_dev) * 65536
    idle_source = {
        EARLY: sub_index * blocks_dev,
        AHEAD: tile_blocks - blocks_dev,
        LATE: 0,
        FROM_AHEAD: tile_blocks,
    }
    place = lax.broadcasted_iota(jnp.int32, (1, stride), 1)
    for index in KINDS:
        span = slice(index * stride, (index + 1) * stride)
        count = counts[:, index : index + 1].astype(jnp.int32)
        lists_ref[:, span] = jnp.where(place < count, entries[:, span], idle + 256 * idle_source[index])
    lists_ref[:, len(KINDS) * stride : len(KINDS) * stride + LANES] = counts.astype(jnp.int32)
    by_column = jnp.sum(hot[:width], axis=0, keepdims=True)
    lists_ref[:, len(KINDS) * stride + LANES :] = by_column.astype(jnp.int32)
    copy = pltpu.make_async_copy(lists_ref, out_ref, sem)
    copy.start()
    copy.wait()


def turn_kernel(pairs_blocks_ref, after_ref, blocks_ref, sem):
    slot_count = pairs_blocks_ref.shape[0]
    copy = pltpu.make_async_copy(pairs_blocks_ref, blocks_ref.at[pl.ds(0, slot_count)], sem)
    copy.start()

    def one_group(group, carry):
        for step in range(TURN_GROUP):
            slot = group * TURN_GROUP + step
            blocks_ref[slot_count + slot] = jnp.transpose(pairs_blocks_ref[slot])
        return carry

    lax.fori_loop(0, slot_count // TURN_GROUP, one_group, 0)
    copy.wait()


def add_products(lists_ref, blocks_ref, slot_count, field, total, index, size, source_from=0, target_from=0):
    stride = list_stride(slot_count)
    idle = lists_ref[0, index * stride + stride - 1] >> 16
    count = lists_ref[0, len(KINDS) * stride + index]
    column_count = lists_ref[0, len(KINDS) * stride + LANES + index]

    def add_part(first, end, kind, plain, cuts):
        def one_group(group, carry):
            results = []
            for step in range(size):
                place = first + group * size + step
                entry = lists_ref[0, index * stride + place]
                block, source, target = entry & 255, (entry >> 8) & 255, entry >> 16
                if plain:
                    block = jnp.where(block >= slot_count, block - slot_count, block)
                if cuts:
                    target = jnp.where(place < end, target, idle)
                value = kind(field[source - source_from].astype(BF16), blocks_ref[block])
                results.append((target - target_from, value))
            for at, value in results:
                total[at] += value
            return carry

        lax.fori_loop(0, (end - first + size - 1) // size, one_group, 0)

    if blocks_ref.shape[0] > slot_count:
        add_part(0, count, times, False, False)
    else:
        add_part(0, column_count, times, True, True)
        add_part(column_count, count, times_transposed, True, False)


def lay_out(row_ref, field, first, block_len):
    for block in range(row_ref.shape[1] // block_len):
        piece = row_ref[:, block * block_len : (block + 1) * block_len]
        field[first + block] = piece.astype(F32)


def early_kernel(
    sub_count, slot_count, lists_ref, blocks_ref, diag_ref, noise_ref, own_ref, rounded_ref, total, field
):
    block_len = blocks_ref.shape[1]
    sub_index, blocks_dev, own_first, _ = device_place(block_len, own_ref, sub_count)
    lay_out(rounded_ref, field, own_first, block_len)
    for block in range(total.shape[0]):
        total[block] = jnp.zeros(total.shape[1:], F32)
    for block in range(blocks_dev):
        span = slice(block * block_len, (block + 1) * block_len)
        value = noise_ref[:, span] * own_ref[:, span]
        total[own_first + block] = value + times(field[own_first + block].astype(BF16), diag_ref[block])
    add_products(lists_ref, blocks_ref, slot_count, field, total, EARLY, LONG_GROUP)


def ahead_kernel(sub_count, slot_count, lists_ref, blocks_ref, begun_ref, *refs):
    row_refs = refs[:sub_count]
    even_ref, odd_ref, field_ref, total = refs[sub_count:]
    block_len = blocks_ref.shape[1]
    sub_index, blocks_dev, _, tile_blocks = device_place(block_len, even_ref, sub_count)
    for step, row_ref in enumerate(row_refs):
        lay_out(row_ref, field_ref, (sub_index ^ step) * blocks_dev, block_len)
    for block in range(blocks_dev):
        total[block] = begun_ref[tile_blocks + block]
    total[blocks_dev] = jnp.zeros(total.shape[1:], F32)
    add_products(lists_ref, blocks_ref, slot_count, field_ref, total, AHEAD, SHORT_GROUP, 0, tile_blocks)
    is_odd = lax.axis_index("tile") % 2 == 1
    for block in range(blocks_dev):
        span = slice(block * block_len, (block + 1) * block_len)
        products = total[block]
        first_row = field_ref[block]
        even_ref[:, span] = jnp.where(is_odd, first_row, products).astype(BF16)
        odd_ref[:, span] = jnp.where(is_odd, products, first_row).astype(BF16)


def late_kernel(slot_count, lists_ref, blocks_ref, begun_ref, field_ref, total):
    total[...] = begun_ref[...]
    add_products(lists_ref, blocks_ref, slot_count, field_ref, total, LATE, LONG_GROUP)


def part_kernel(
    sub_count, slot_count, is_last, lists_ref, blocks_ref, begun_ref, field_ref, even_ref, odd_ref,
    moments_in_ref, *refs
):
    part_refs = refs[:sub_count]
    moments_ref, total, ahead = refs[sub_count:]
    block_len = blocks_ref.shape[1]
    sub_index, blocks_dev, own_first, tile_blocks = device_place(block_len, even_ref, sub_count)
    is_odd = lax.axis_index("tile") % 2 == 1
    for block in range(blocks_dev):
        span = slice(block * block_len, (block + 1) * block_len)
        even = even_ref[:, span].astype(F32)
        odd = odd_ref[:, span].astype(F32)
        ahead[block] = jnp.where(is_odd, odd, even)
        total[block] = begun_ref[block] + jnp.where(is_odd, even, odd)
    for block in range(blocks_dev, tile_blocks):
        total[block] = begun_ref[block]
    total[begun_ref.shape[0] - 1] = jnp.zeros(total.shape[1:], F32)
    add_products(lists_ref, blocks_ref, slot_count, ahead, total, FROM_AHEAD, SHORT_GROUP, tile_blocks, 0)
    for step in range(sub_count):
        first = (sub_index ^ step) * blocks_dev
        for block in range(blocks_dev):
            span = slice(block * block_len, (block + 1) * block_len)
            part_refs[step][:, span] = total[first + block].astype(part_refs[step].dtype)
    moments = moments_in_ref[...]
    if is_last:
        product = jnp.zeros(total.shape[1:], F32)
        for block in range(tile_blocks):
            product += field_ref[block] * total[block]
        lane = lax.broadcasted_iota(jnp.int32, moments.shape, 1)
        moments = jnp.where(lane == 2 * ITERS - 1, jnp.sum(product, axis=1, keepdims=True), moments)
    moments_ref[...] = moments


def join_kernel(index, after_ref, own_ref, old_ref, moments_in_ref, *refs):
    part_refs = refs[:-3]
    next_ref, rounded_ref, moments_ref = refs[-3:]
    value = own_ref[...]
    for part_ref in part_refs:
        value += part_ref[...].astype(F32)
    next_ref[...] = value
    rounded_ref[...] = value.astype(BF16)
    old = old_ref[...]
    lane = lax.broadcasted_iota(jnp.int32, moments_ref.shape, 1)
    moments = moments_in_ref[...] if index else jnp.zeros(moments_ref.shape, F32)
    found = {2 * index + 1: old * value, 2 * index + 2: value * value}
    if index == 0:
        found[0] = old * old
    for order, product in found.items():
        moments = jnp.where(lane == order, jnp.sum(product, axis=1, keepdims=True), moments)
    moments_ref[...] = moments


def finish_kernel(sub_count, moments_ref, *refs):
    part_refs, basis_refs = refs[:sub_count], refs[sub_count:-2]
    solution_ref, residual_ref = refs[-2:]
    moments = [moments_ref[:, order : order + 1] for order in range(2 * ITERS)]

    def inner(first, second, shift):
        value = 0.0
        for i, a in enumerate(first):
            for j, b in enumerate(second):
                value = value + a * b * moments[i + j + shift]
        return value

    one = jnp.ones_like(moments[0])
    zero = jnp.zeros_like(one)
    direction, residual = [one], [one]
    answer = [zero] * ITERS
    norm_now = moments[0]
    for iteration in range(ITERS):
        step_size = norm_now / inner(direction, direction, 1)
        for power, weight in enumerate(direction):
            answer[power] = answer[power] + step_size * weight
        residual = residual + [zero]
        for power, weight in enumerate(direction):
            residual[power + 1] = residual[power + 1] - step_size * weight
        if iteration + 1 < ITERS:
            norm_next = inner(residual, residual, 0)
            direction = [
                value + (norm_next / norm_now) * old
                for value, old in zip(residual, direction + [zero])
            ]
            norm_now = norm_next
    fields = [basis_ref[...] for basis_ref in basis_refs]
    fields.append(sum(part_ref[...].astype(F32) for part_ref in part_refs))
    solution_ref[...] = sum(weight * field for weight, field in zip(answer, fields))
    residual_ref[...] = sum(weight * field for weight, field in zip(residual, fields))


def shape(rows, columns, kind):
    return jax.ShapeDtypeStruct((rows, columns), kind)


def exchange(block, axis, step):
    count = lax.axis_size(axis)
    return lax.ppermute(block, axis, [(i, i ^ step) for i in range(count)])


def swap(block, axis, first):
    count = lax.axis_size(axis)
    route = []
    for i in range(first, count - 1, 2):
        route += [(i, i + 1), (i + 1, i)]
    return lax.ppermute(block, axis, route)


def call(kernel, outs, ins, name, cost=0, **options):
    single = not isinstance(outs, tuple)
    specs = [SMEM if value.dtype == jnp.int32 else VMEM for value in ins]
    options.setdefault("in_specs", specs)
    options.setdefault("out_specs", VMEM if single else (VMEM,) * len(outs))
    return pl.pallas_call(
        kernel,
        out_shape=outs,
        compiler_params=PARAMS,
        name=name,
        cost_estimate=pl.CostEstimate(flops=int(cost * 1e9), bytes_accessed=0, transcendentals=0),
        **options,
    )(*ins)


def on_device(right_side, point_order, noise_var, block_pairs, pair_blocks, diag_blocks):
    sub_count = lax.axis_size("sub")
    tile_count = lax.axis_size("tile")
    rhs_count, points_dev = right_side.shape
    blocks_dev, block_len = diag_blocks.shape[:2]
    extended = (sub_count + 1) * blocks_dev
    noise = noise_var[None, :]
    full = shape(rhs_count, points_dev, F32)
    half = shape(rhs_count, points_dev, BF16)
    scalars = shape(rhs_count, LANES, F32)
    sums = jax.ShapeDtypeStruct((extended + 1, rhs_count, block_len), F32)

    def scratch(blocks):
        return pltpu.VMEM((blocks, rhs_count, block_len), F32)

    slot_count = pair_blocks.shape[0]
    width = -(-slot_count // LANES) * LANES
    assert 2 * width <= 256 and extended < 256 and slot_count % TURN_GROUP == 0
    lists_shape = (1, len(KINDS) * list_stride(slot_count) + 2 * LANES)
    lists = call(
        functools.partial(lists_kernel, sub_count, blocks_dev, slot_count),
        pltpu.SMEM(lists_shape, jnp.int32),
        (block_pairs.T,),
        "lists",
        1,
        in_specs=[VMEM],
        out_specs=SMEM,
        scratch_shapes=[
            pltpu.VMEM((8, width), F32),
            pltpu.VMEM(lists_shape, jnp.int32),
            pltpu.SemaphoreType.DMA(()),
        ],
    )
    blocks = pair_blocks
    field, rounded = call(
        order_kernel,
        (full, half),
        [pltpu.with_memory_space_constraint(value, pltpu.HBM) for value in (right_side, point_order)],
        "curve_order",
        10,
        in_specs=[pl.BlockSpec(memory_space=pltpu.HBM)] * 2,
        scratch_shapes=[
            pltpu.VMEM(right_side.shape, F32),
            pltpu.VMEM(point_order.shape, jnp.int32),
            pltpu.SemaphoreType.DMA((2,)),
        ],
    )
    basis = [field]
    moments = jnp.zeros(scalars.shape, F32)
    for index in range(ITERS):
        is_last = index + 1 == ITERS
        rows = [exchange(rounded, "sub", step) for step in range(1, sub_count)]
        begun = call(
            functools.partial(early_kernel, sub_count, slot_count),
            sums,
            (lists, blocks, diag_blocks, noise, field, rounded),
            "early",
            3,
            scratch_shapes=[scratch(extended)],
        )
        even, odd, tile_field = call(
            functools.partial(ahead_kernel, sub_count, slot_count),
            (half, half, jax.ShapeDtypeStruct((sub_count * blocks_dev, rhs_count, block_len), F32)),
            (lists, blocks, begun, rounded, *rows),
            "ahead",
            1,
            scratch_shapes=[scratch(blocks_dev + 1)],
        )
        even = swap(even, "tile", 0)
        odd = swap(odd, "tile", 1)
        begun = call(functools.partial(late_kernel, slot_count), sums, (lists, blocks, begun, tile_field), "late", 3)
        part = shape(rhs_count, points_dev, F32 if is_last else BF16)
        *parts, moments = call(
            functools.partial(part_kernel, sub_count, slot_count, is_last),
            (full,) + (part,) * (sub_count - 1) + (scalars,),
            (lists, blocks, begun, tile_field, even, odd, moments),
            "parts",
            1,
            scratch_shapes=[scratch(extended + 1), scratch(blocks_dev)],
        )
        if is_last:
            break
        if index == 0:
            blocks = call(
                turn_kernel,
                pltpu.VMEM((2 * slot_count, block_len, block_len), BF16),
                (pair_blocks, moments),
                "turn",
                4,
                scratch_shapes=[pltpu.SemaphoreType.DMA(())],
            )
        arrived = [exchange(parts[step], "sub", step) for step in range(sub_count - 1, 0, -1)]
        field, rounded, moments = call(
            functools.partial(join_kernel, index),
            (full, half, scalars),
            (blocks, parts[0], field, moments, *arrived),
            "join",
        )
        basis.append(field)
    arrived = []
    for axis, count in (("sub", sub_count), ("tile", tile_count)):
        step = 1
        while step < count:
            moments = moments + exchange(moments, axis, step)
            if len(arrived) < sub_count - 1:
                far = sub_count - 1 - len(arrived)
                arrived.append(exchange(parts[far], "sub", far))
                moments, *parts = lax.optimization_barrier((moments, *parts))
            step *= 2
    for far in range(sub_count - 1 - len(arrived), 0, -1):
        arrived.append(exchange(parts[far], "sub", far))
    return call(
        functools.partial(finish_kernel, sub_count),
        (full, full),
        (moments, parts[0], *arrived, *basis),
        "finish",
    )


def solution(mesh):
    placed = (
        P(None, ("tile", "sub")),
        P(("tile", "sub"), None),
        P(("tile", "sub")),
        P(("tile", "sub"), None),
        P(("tile", "sub"), None, None),
        P(("tile", "sub"), None, None),
    )
    return jax.shard_map(
        on_device,
        mesh=mesh,
        in_specs=placed,
        out_specs=(P(None, ("tile", "sub")), P(None, ("tile", "sub"))),
        check_vma=False,
    )
```

```python
import functools

import jax
import jax.numpy as jnp
from jax import lax
from jax.experimental import pallas as pl
from jax.experimental.pallas import tpu as pltpu
from jax.sharding import PartitionSpec as P

ITERS = 3
LANES = 128
LONG_GROUP = 16
SHORT_GROUP = 8
TURN_GROUP = 4
F32 = jnp.float32
BF16 = jnp.bfloat16
VMEM = pl.BlockSpec(memory_space=pltpu.VMEM)
SMEM = pl.BlockSpec(memory_space=pltpu.SMEM)
EARLY, AHEAD, LATE, FROM_AHEAD = KINDS = range(4)
PARAMS = pltpu.CompilerParams(vmem_limit_bytes=4 * 1024 * 1024)


def times(field, block):
    return lax.dot_general(field, block, (((1,), (0,)), ((), ())), preferred_element_type=F32)


def times_transposed(field, block):
    return lax.dot_general(field, block, (((1,), (1,)), ((), ())), preferred_element_type=F32)


def order_kernel(right_in, order_in, curve_ref, rounded_ref, right_ref, order_ref, sems):
    copies = [
        pltpu.make_async_copy(right_in, right_ref, sems.at[0]),
        pltpu.make_async_copy(order_in, order_ref, sems.at[1]),
    ]
    for copy in copies:
        copy.start()
    for copy in copies:
        copy.wait()
    rhs_count, points = right_ref.shape
    for start in range(0, points, LANES):
        at = jnp.broadcast_to(order_ref[:, start : start + LANES], (rhs_count, LANES))
        chunk = at // LANES
        lane = at % LANES
        result = jnp.zeros((rhs_count, LANES), F32)
        for source in range(points // LANES):
            values = right_ref[:, source * LANES : (source + 1) * LANES]
            picked = jnp.take_along_axis(values, lane, axis=1)
            result = jnp.where(chunk == source, picked, result)
        curve_ref[:, start : start + LANES] = result
        rounded_ref[:, start : start + LANES] = result.astype(BF16)


def device_place(block_len, field_ref, sub_count):
    blocks_dev = field_ref.shape[1] // block_len
    sub_index = lax.axis_index("sub")
    return sub_index, blocks_dev, sub_index * blocks_dev, blocks_dev * sub_count


def list_stride(slot_count):
    return -(-(2 * slot_count + LONG_GROUP) // LANES) * LANES


def lists_kernel(sub_count, blocks_dev, slot_count, pairs_ref, out_ref, padded, lists_ref, sem):
    width = padded.shape[1]
    stride = list_stride(slot_count)
    sub_index = lax.axis_index("sub")
    tile_blocks = blocks_dev * sub_count
    first_block = lax.axis_index("tile") * tile_blocks
    padded[...] = jnp.full(padded.shape, -1.0, F32)
    padded[0:2, 0:slot_count] = pairs_ref[...].astype(F32)
    by_lane = padded[...]
    by_row = jnp.transpose(by_lane)

    def sides(row, col, axis):
        live = jnp.concatenate([row, row], axis) >= 0.0
        row = row.astype(jnp.int32) - first_block
        col = col.astype(jnp.int32) - first_block
        source = jnp.concatenate([row, col], axis)
        target = jnp.concatenate([col, row], axis)
        return live, source, target

    live, source, target = sides(by_row[:, 0:1], by_row[:, 1:2], 0)
    kind = jnp.where(target >= tile_blocks, AHEAD, LATE)
    first_own = sub_index * blocks_dev
    is_early = (source >= first_own) & (source < first_own + blocks_dev)
    kind = jnp.where(is_early, EARLY, kind)
    kind = jnp.where(source >= tile_blocks, FROM_AHEAD, kind)
    kind = jnp.where(live, kind, -1)
    hot = (kind == lax.broadcasted_iota(jnp.int32, (2 * width, LANES), 1)).astype(F32)
    below = lax.broadcasted_iota(jnp.int32, (2 * width, 2 * width), 0) > lax.broadcasted_iota(
        jnp.int32, (2 * width, 2 * width), 1
    )
    ranks = times(below.astype(F32).astype(BF16), hot.astype(BF16))
    rank = jnp.sum(ranks * hot, axis=1, keepdims=True).astype(jnp.int32)
    counts = jnp.sum(hot, axis=0, keepdims=True)
    at = jnp.where(live, kind * stride + rank, -1)
    spread = at == lax.broadcasted_iota(jnp.int32, (2 * width, len(KINDS) * stride), 1)
    live, source, target = sides(by_lane[0:1, :], by_lane[1:2, :], 1)
    lane = lax.broadcasted_iota(jnp.int32, (1, 2 * width), 1)
    block = jnp.where(lane < width, lane, lane - width + slot_count)
    fields = jnp.concatenate(
        [jnp.where(live, value, 0).astype(F32) for value in (block, source, target)]
        + [jnp.zeros((5, 2 * width), F32)],
        0,
    )
    found = times(fields.astype(BF16), spread.astype(F32).astype(BF16))
    entries = found[0:1] + 256.0 * found[1:2] + 65536.0 * found[2:3]
    entries = entries.astype(jnp.int32)
    idle = (tile_blocks + blocks_dev) * 65536
    idle_source = {
        EARLY: sub_index * blocks_dev,
        AHEAD: tile_blocks - blocks_dev,
        LATE: 0,
        FROM_AHEAD: tile_blocks,
    }
    place = lax.broadcasted_iota(jnp.int32, (1, stride), 1)
    for index in KINDS:
        span = slice(index * stride, (index + 1) * stride)
        count = counts[:, index : index + 1].astype(jnp.int32)
        lists_ref[:, span] = jnp.where(place < count, entries[:, span], idle + 256 * idle_source[index])
    lists_ref[:, len(KINDS) * stride : len(KINDS) * stride + LANES] = counts.astype(jnp.int32)
    by_column = jnp.sum(hot[:width], axis=0, keepdims=True)
    lists_ref[:, len(KINDS) * stride + LANES :] = by_column.astype(jnp.int32)
    copy = pltpu.make_async_copy(lists_ref, out_ref, sem)
    copy.start()
    copy.wait()


def turn_kernel(pairs_blocks_ref, after_ref, blocks_ref, sem):
    slot_count = pairs_blocks_ref.shape[0]
    copy = pltpu.make_async_copy(pairs_blocks_ref, blocks_ref.at[pl.ds(0, slot_count)], sem)
    copy.start()

    def one_group(group, carry):
        for step in range(TURN_GROUP):
            slot = group * TURN_GROUP + step
            blocks_ref[slot_count + slot] = jnp.transpose(pairs_blocks_ref[slot])
        return carry

    lax.fori_loop(0, slot_count // TURN_GROUP, one_group, 0)
    copy.wait()


def add_products(lists_ref, blocks_ref, slot_count, field, total, index, size, source_from=0, target_from=0):
    stride = list_stride(slot_count)
    idle = lists_ref[0, index * stride + stride - 1] >> 16
    count = lists_ref[0, len(KINDS) * stride + index]
    column_count = lists_ref[0, len(KINDS) * stride + LANES + index]

    def add_part(first, end, kind, plain, cuts):
        def one_group(group, carry):
            results = []
            for step in range(size):
                place = first + group * size + step
                entry = lists_ref[0, index * stride + place]
                block, source, target = entry & 255, (entry >> 8) & 255, entry >> 16
                if plain:
                    block = jnp.where(block >= slot_count, block - slot_count, block)
                if cuts:
                    target = jnp.where(place < end, target, idle)
                value = kind(field[source - source_from].astype(BF16), blocks_ref[block])
                results.append((target - target_from, value))
            for at, value in results:
                total[at] += value
            return carry

        lax.fori_loop(0, (end - first + size - 1) // size, one_group, 0)

    if blocks_ref.shape[0] > slot_count:
        add_part(0, count, times, False, False)
    else:
        add_part(0, column_count, times, True, True)
        add_part(column_count, count, times_transposed, True, False)


def raised(value, exponent):
    result = value
    for _ in range(exponent - 1):
        result = result * value
    return result


def widen(tile, columns):
    return jnp.concatenate([tile] * (columns // LANES), axis=1)


def lay_out(row_ref, field, first, blocks_dev, block_len, factor=None):
    for block in range(blocks_dev):
        piece = row_ref[:, block * block_len : (block + 1) * block_len].astype(F32)
        field[first + block] = piece if factor is None else piece * factor


def early_kernel(
    index, sub_count, slot_count, lists_ref, blocks_ref, diag_ref, noise_ref, own_ref, rounded_ref, total,
    *refs
):
    field = refs[-1]
    block_len = blocks_ref.shape[1]
    sub_index, blocks_dev, own_first, _ = device_place(block_len, own_ref, sub_count)
    if index == 0:
        largest = diag_ref[0].astype(F32)
        for block in range(1, blocks_dev):
            largest = jnp.maximum(largest, diag_ref[block].astype(F32))
        refs[0][...] = jnp.full(refs[0].shape, jnp.maximum(jnp.max(largest), 1.0))
    lay_out(rounded_ref, field, own_first, blocks_dev, block_len)
    for block in range(total.shape[0]):
        total[block] = jnp.zeros(total.shape[1:], F32)
    for block in range(blocks_dev):
        span = slice(block * block_len, (block + 1) * block_len)
        value = noise_ref[:, span] * own_ref[:, span]
        total[own_first + block] = value + times(field[own_first + block].astype(BF16), diag_ref[block])
    add_products(lists_ref, blocks_ref, slot_count, field, total, EARLY, LONG_GROUP)


def ahead_kernel(index, sub_count, slot_count, lists_ref, blocks_ref, begun_ref, *refs):
    if index == 1:
        *refs, ratios_ref, total = refs
        row_refs, (even_ref, odd_ref, field_ref) = refs[:-3], refs[-3:]
        points_dev = even_ref.shape[1] - LANES
        units = [row_ref[:, points_dev:].astype(F32) for row_ref in row_refs]
        tile_unit = functools.reduce(jnp.maximum, units)
        ratios = [unit / tile_unit for unit in units]
        ratios_ref[...] = jnp.concatenate(ratios + [tile_unit], axis=1)
    else:
        row_refs, (even_ref, odd_ref, field_ref, total) = refs[:-4], refs[-4:]
        points_dev = even_ref.shape[1]
        if index:
            ratios_ref, *row_refs = row_refs
            ratios = [ratios_ref[:, step * LANES : (step + 1) * LANES] for step in range(sub_count)]
    block_len = blocks_ref.shape[1]
    blocks_dev = points_dev // block_len
    tile_blocks = blocks_dev * sub_count
    sub_index = lax.axis_index("sub")
    for step, row_ref in enumerate(row_refs):
        factor = widen(raised(ratios[step], index), block_len) if index else None
        lay_out(row_ref, field_ref, (sub_index ^ step) * blocks_dev, blocks_dev, block_len, factor)
    for block in range(blocks_dev):
        value = begun_ref[tile_blocks + block]
        total[block] = value * widen(raised(ratios[0], index), block_len) if index else value
    total[blocks_dev] = jnp.zeros(total.shape[1:], F32)
    add_products(lists_ref, blocks_ref, slot_count, field_ref, total, AHEAD, SHORT_GROUP, 0, tile_blocks)
    is_odd = lax.axis_index("tile") % 2 == 1
    for block in range(blocks_dev):
        span = slice(block * block_len, (block + 1) * block_len)
        products = total[block]
        first_row = field_ref[block]
        even_ref[:, span] = jnp.where(is_odd, first_row, products).astype(BF16)
        odd_ref[:, span] = jnp.where(is_odd, products, first_row).astype(BF16)
    if index == 1:
        even_ref[:, points_dev:] = tile_unit.astype(BF16)
        odd_ref[:, points_dev:] = tile_unit.astype(BF16)


def late_kernel(index, slot_count, lists_ref, blocks_ref, begun_ref, field_ref, *refs):
    total = refs[-1]
    if index:
        factor = widen(raised(refs[0][:, :LANES], index), total.shape[2])
        for block in range(total.shape[0]):
            total[block] = begun_ref[block] * factor
    else:
        total[...] = begun_ref[...]
    add_products(lists_ref, blocks_ref, slot_count, field_ref, total, LATE, LONG_GROUP)


def part_kernel(
    index, sub_count, slot_count, lists_ref, blocks_ref, begun_ref, field_ref, even_ref, odd_ref,
    moments_in_ref, unit_ref, *refs
):
    if index == 1:
        ratios_ref, *refs = refs
        *refs, sides_ref, total, ahead = refs
    else:
        if index:
            ratios_ref, sides_ref, *refs = refs
        *refs, total, ahead = refs
    part_refs, moments_ref = refs[:-1], refs[-1]
    block_len = blocks_ref.shape[1]
    sub_index, blocks_dev, own_first, tile_blocks = device_place(block_len, part_refs[0], sub_count)
    is_odd = lax.axis_index("tile") % 2 == 1
    if index == 1:
        points_dev = blocks_dev * block_len
        even = even_ref[:, points_dev:].astype(F32)
        odd = odd_ref[:, points_dev:].astype(F32)
        tile_unit = ratios_ref[:, sub_count * LANES :]
        sides = [jnp.where(is_odd, even, odd) / tile_unit, jnp.where(is_odd, odd, even) / tile_unit]
        sides_ref[...] = jnp.concatenate(sides, axis=1)
    elif index:
        sides = [sides_ref[:, :LANES], sides_ref[:, LANES:]]
    if index:
        before, after = [widen(raised(side, index), block_len) for side in sides]
    for block in range(blocks_dev):
        span = slice(block * block_len, (block + 1) * block_len)
        even = even_ref[:, span].astype(F32)
        odd = odd_ref[:, span].astype(F32)
        products = jnp.where(is_odd, even, odd)
        first_row = jnp.where(is_odd, odd, even)
        ahead[block] = first_row * after if index else first_row
        total[block] = begun_ref[block] + (products * before if index else products)
    for block in range(blocks_dev, tile_blocks):
        total[block] = begun_ref[block]
    total[begun_ref.shape[0] - 1] = jnp.zeros(total.shape[1:], F32)
    add_products(lists_ref, blocks_ref, slot_count, ahead, total, FROM_AHEAD, SHORT_GROUP, tile_blocks, 0)
    for step in range(sub_count):
        first = (sub_index ^ step) * blocks_dev
        for block in range(blocks_dev):
            span = slice(block * block_len, (block + 1) * block_len)
            part_refs[step][:, span] = total[first + block].astype(part_refs[step].dtype)
    moments = moments_in_ref[...]
    if index + 1 == ITERS:
        product = jnp.zeros(total.shape[1:], F32)
        for block in range(tile_blocks):
            product += field_ref[block] * total[block]
        last = jnp.sum(product, axis=1, keepdims=True)
        unit = unit_ref[...]
        last = last / (raised(ratios_ref[:, :LANES], 2 * index) * unit)
        lane = lax.broadcasted_iota(jnp.int32, moments.shape, 1)
        moments = jnp.where(lane == 2 * ITERS - 1, last, moments)
        moments = jnp.where(lane == 2 * ITERS, unit, moments)
    moments_ref[...] = moments


def join_kernel(index, after_ref, unit_ref, ratios_ref, own_ref, old_ref, moments_in_ref, *refs):
    part_refs = refs[:-3]
    next_ref, rounded_ref, moments_ref = refs[-3:]
    points_dev = own_ref.shape[1]
    value = own_ref[...]
    for part_ref in part_refs:
        value += part_ref[...].astype(F32)
    unit = unit_ref[...]
    divisor = raised(ratios_ref[:, :LANES], index) * unit if index else unit
    value = value * widen(1.0 / divisor, points_dev)
    next_ref[...] = value
    rounded_ref[:, :points_dev] = value.astype(BF16)
    if index == 0:
        rounded_ref[:, points_dev:] = unit.astype(BF16)
    old = old_ref[...]
    lane = lax.broadcasted_iota(jnp.int32, moments_ref.shape, 1)
    moments = moments_in_ref[...] if index else jnp.zeros(moments_ref.shape, F32)
    found = {2 * index + 1: old * value, 2 * index + 2: value * value}
    if index == 0:
        found[0] = old * old
    for order, product in found.items():
        moments = jnp.where(lane == order, jnp.sum(product, axis=1, keepdims=True), moments)
    moments_ref[...] = moments


def add_moments_kernel(first_ref, second_ref, sum_ref):
    unit_lane = 2 * ITERS
    lane = lax.broadcasted_iota(jnp.int32, sum_ref.shape, 1)
    units = [ref[:, unit_lane : unit_lane + 1] for ref in (first_ref, second_ref)]
    larger = jnp.maximum(units[0], units[1])
    result = jnp.zeros(sum_ref.shape, F32)
    for ref, unit in zip((first_ref, second_ref), units):
        ratio = unit / larger
        value = ref[...]
        for order in range(1, unit_lane):
            value = jnp.where(lane >= order, value * ratio, value)
        result += value
    sum_ref[...] = jnp.where(lane == unit_lane, larger, result)


def finish_kernel(sub_count, moments_ref, unit_ref, ratios_ref, *refs):
    part_refs, basis_refs = refs[:sub_count], refs[sub_count:-2]
    solution_ref, residual_ref = refs[-2:]
    moments = [moments_ref[:, order : order + 1] for order in range(2 * ITERS)]
    largest = moments_ref[:, 2 * ITERS : 2 * ITERS + 1]
    unit = unit_ref[:, :1]
    ratio = unit / largest

    def inner(first, second, shift):
        value = 0.0
        for i, a in enumerate(first):
            for j, b in enumerate(second):
                value = value + a * b * moments[i + j + shift]
        return value

    one = jnp.ones_like(moments[0])
    zero = jnp.zeros_like(one)
    direction, residual = [one], [one]
    answer = [zero] * ITERS
    norm_now = moments[0]
    for iteration in range(ITERS):
        step_size = norm_now / inner(direction, direction, 1)
        for power, weight in enumerate(direction):
            answer[power] = answer[power] + step_size * weight
        residual = residual + [zero]
        for power, weight in enumerate(direction):
            residual[power + 1] = residual[power + 1] - step_size * weight
        if iteration + 1 < ITERS:
            norm_next = inner(residual, residual, 0)
            direction = [
                value + (norm_next / norm_now) * old
                for value, old in zip(residual, direction + [zero])
            ]
            norm_now = norm_next
    fields = [basis_ref[...] for basis_ref in basis_refs]
    fields.append(sum(part_ref[...].astype(F32) for part_ref in part_refs))
    for order in range(1, ITERS + 1):
        scale = raised(ratio, order)
        if order < ITERS:
            answer[order] = answer[order] * scale
        else:
            scale = scale / (raised(ratios_ref[:, :1], ITERS - 1) * unit)
        residual[order] = residual[order] * scale
    answer = [weight / largest for weight in answer]
    solution_ref[...] = sum(weight * field for weight, field in zip(answer, fields))
    residual_ref[...] = sum(weight * field for weight, field in zip(residual, fields))


def shape(rows, columns, kind):
    return jax.ShapeDtypeStruct((rows, columns), kind)


def exchange(block, axis, step):
    count = lax.axis_size(axis)
    return lax.ppermute(block, axis, [(i, i ^ step) for i in range(count)])


def swap(block, axis, first):
    count = lax.axis_size(axis)
    route = []
    for i in range(first, count - 1, 2):
        route += [(i, i + 1), (i + 1, i)]
    return lax.ppermute(block, axis, route)


def call(kernel, outs, ins, name, cost=0, **options):
    single = not isinstance(outs, tuple)
    specs = [SMEM if value.dtype == jnp.int32 else VMEM for value in ins]
    options.setdefault("in_specs", specs)
    options.setdefault("out_specs", VMEM if single else (VMEM,) * len(outs))
    return pl.pallas_call(
        kernel,
        out_shape=outs,
        compiler_params=PARAMS,
        name=name,
        cost_estimate=pl.CostEstimate(flops=int(cost * 1e9), bytes_accessed=0, transcendentals=0),
        **options,
    )(*ins)


def on_device(right_side, point_order, noise_var, block_pairs, pair_blocks, diag_blocks):
    sub_count = lax.axis_size("sub")
    tile_count = lax.axis_size("tile")
    rhs_count, points_dev = right_side.shape
    blocks_dev, block_len = diag_blocks.shape[:2]
    extended = (sub_count + 1) * blocks_dev
    noise = noise_var[None, :]
    full = shape(rhs_count, points_dev, F32)
    half = shape(rhs_count, points_dev, BF16)
    scalars = shape(rhs_count, LANES, F32)
    sums = jax.ShapeDtypeStruct((extended + 1, rhs_count, block_len), F32)

    def scratch(blocks):
        return pltpu.VMEM((blocks, rhs_count, block_len), F32)

    slot_count = pair_blocks.shape[0]
    width = -(-slot_count // LANES) * LANES
    assert 2 * width <= 256 and extended < 256 and slot_count % TURN_GROUP == 0
    lists_shape = (1, len(KINDS) * list_stride(slot_count) + 2 * LANES)
    lists = call(
        functools.partial(lists_kernel, sub_count, blocks_dev, slot_count),
        pltpu.SMEM(lists_shape, jnp.int32),
        (block_pairs.T,),
        "lists",
        1,
        in_specs=[VMEM],
        out_specs=SMEM,
        scratch_shapes=[
            pltpu.VMEM((8, width), F32),
            pltpu.VMEM(lists_shape, jnp.int32),
            pltpu.SemaphoreType.DMA(()),
        ],
    )
    blocks = pair_blocks
    field, rounded = call(
        order_kernel,
        (full, half),
        [pltpu.with_memory_space_constraint(value, pltpu.HBM) for value in (right_side, point_order)],
        "curve_order",
        10,
        in_specs=[pl.BlockSpec(memory_space=pltpu.HBM)] * 2,
        scratch_shapes=[
            pltpu.VMEM(right_side.shape, F32),
            pltpu.VMEM(point_order.shape, jnp.int32),
            pltpu.SemaphoreType.DMA((2,)),
        ],
    )
    basis = [field]
    moments = unit = jnp.zeros(scalars.shape, F32)
    ratios = sides = ()
    for index in range(ITERS):
        is_last = index + 1 == ITERS
        rows = [exchange(rounded, "sub", step) for step in range(1, sub_count)]
        begun = call(
            functools.partial(early_kernel, index, sub_count, slot_count),
            (sums,) if index else (sums, scalars),
            (lists, blocks, diag_blocks, noise, field, rounded),
            "early",
            3,
            scratch_shapes=[scratch(extended)],
        )
        if index == 0:
            begun, unit = begun
        else:
            (begun,) = begun
        message = shape(rhs_count, points_dev + LANES, BF16) if index == 1 else half
        even, odd, tile_field, *found = call(
            functools.partial(ahead_kernel, index, sub_count, slot_count),
            (message, message, jax.ShapeDtypeStruct((sub_count * blocks_dev, rhs_count, block_len), F32))
            + ((shape(rhs_count, (sub_count + 1) * LANES, F32),) if index == 1 else ()),
            (lists, blocks, begun, *ratios, rounded, *rows),
            "ahead",
            1,
            scratch_shapes=[scratch(blocks_dev + 1)],
        )
        ratios = ratios or tuple(found)
        even = swap(even, "tile", 0)
        odd = swap(odd, "tile", 1)
        begun = call(
            functools.partial(late_kernel, index, slot_count),
            sums,
            (lists, blocks, begun, tile_field, *ratios),
            "late",
            3,
        )
        part = shape(rhs_count, points_dev, F32 if is_last else BF16)
        found = call(
            functools.partial(part_kernel, index, sub_count, slot_count),
            (full,)
            + (part,) * (sub_count - 1)
            + (scalars,)
            + ((shape(rhs_count, 2 * LANES, F32),) if index == 1 else ()),
            (lists, blocks, begun, tile_field, even, odd, moments, unit, *ratios, *sides),
            "parts",
            1,
            scratch_shapes=[scratch(extended + 1), scratch(blocks_dev)],
        )
        parts, moments = list(found[:sub_count]), found[sub_count]
        sides = sides or tuple(found[sub_count + 1 :])
        if is_last:
            break
        if index == 0:
            blocks = call(
                turn_kernel,
                pltpu.VMEM((2 * slot_count, block_len, block_len), BF16),
                (pair_blocks, moments),
                "turn",
                4,
                scratch_shapes=[pltpu.SemaphoreType.DMA(())],
            )
        arrived = [exchange(parts[step], "sub", step) for step in range(sub_count - 1, 0, -1)]
        field, rounded, moments = call(
            functools.partial(join_kernel, index),
            (full, half if index else shape(rhs_count, points_dev + LANES, BF16), scalars),
            (blocks, unit, *(ratios or (unit,)), parts[0], field, moments, *arrived),
            "join",
        )
        basis.append(field)
    arrived = []
    for axis, count in (("sub", sub_count), ("tile", tile_count)):
        step = 1
        while step < count:
            moments = call(add_moments_kernel, scalars, (moments, exchange(moments, axis, step)), "add_moments")
            if len(arrived) < sub_count - 1:
                far = sub_count - 1 - len(arrived)
                arrived.append(exchange(parts[far], "sub", far))
                moments, *parts = lax.optimization_barrier((moments, *parts))
            step *= 2
    for far in range(sub_count - 1 - len(arrived), 0, -1):
        arrived.append(exchange(parts[far], "sub", far))
    return call(
        functools.partial(finish_kernel, sub_count),
        (full, full),
        (moments, unit, *ratios, parts[0], *arrived, *basis),
        "finish",
    )


def solution(mesh):
    placed = (
        P(None, ("tile", "sub")),
        P(("tile", "sub"), None),
        P(("tile", "sub")),
        P(("tile", "sub"), None),
        P(("tile", "sub"), None, None),
        P(("tile", "sub"), None, None),
    )
    return jax.shard_map(
        on_device,
        mesh=mesh,
        in_specs=placed,
        out_specs=(P(None, ("tile", "sub")), P(None, ("tile", "sub"))),
        check_vma=False,
    )
```

```python
import functools

import jax
import jax.numpy as jnp
from jax import lax
from jax.experimental import pallas as pl
from jax.experimental.pallas import tpu as pltpu
from jax.sharding import PartitionSpec as P

ITERS = 3
LANES = 128
LONG_GROUP = 16
SHORT_GROUP = 8
TURN_GROUP = 4
F32 = jnp.float32
BF16 = jnp.bfloat16
VMEM = pl.BlockSpec(memory_space=pltpu.VMEM)
SMEM = pl.BlockSpec(memory_space=pltpu.SMEM)
EARLY, AHEAD, LATE, FROM_AHEAD = KINDS = range(4)
PARAMS = pltpu.CompilerParams(vmem_limit_bytes=4 * 1024 * 1024)


def times(field, block):
    return lax.dot_general(field, block, (((1,), (0,)), ((), ())), preferred_element_type=F32)


def times_transposed(field, block):
    return lax.dot_general(field, block, (((1,), (1,)), ((), ())), preferred_element_type=F32)


def order_kernel(right_in, order_in, curve_ref, rounded_ref, right_ref, order_ref, sems):
    copies = [
        pltpu.make_async_copy(right_in, right_ref, sems.at[0]),
        pltpu.make_async_copy(order_in, order_ref, sems.at[1]),
    ]
    for copy in copies:
        copy.start()
    for copy in copies:
        copy.wait()
    rhs_count, points = right_ref.shape
    for start in range(0, points, LANES):
        at = jnp.broadcast_to(order_ref[:, start : start + LANES], (rhs_count, LANES))
        chunk = at // LANES
        lane = at % LANES
        result = jnp.zeros((rhs_count, LANES), F32)
        for source in range(points // LANES):
            values = right_ref[:, source * LANES : (source + 1) * LANES]
            picked = jnp.take_along_axis(values, lane, axis=1)
            result = jnp.where(chunk == source, picked, result)
        curve_ref[:, start : start + LANES] = result
        rounded_ref[:, start : start + LANES] = result.astype(BF16)


def device_place(block_len, field_ref, sub_count):
    blocks_dev = field_ref.shape[1] // block_len
    sub_index = lax.axis_index("sub")
    return sub_index, blocks_dev, sub_index * blocks_dev, blocks_dev * sub_count


def list_stride(slot_count):
    return -(-(2 * slot_count + LONG_GROUP) // LANES) * LANES


def lists_kernel(sub_count, blocks_dev, slot_count, pairs_ref, out_ref, padded, lists_ref, sem):
    width = padded.shape[1]
    stride = list_stride(slot_count)
    sub_index = lax.axis_index("sub")
    tile_blocks = blocks_dev * sub_count
    first_block = lax.axis_index("tile") * tile_blocks
    padded[...] = jnp.full(padded.shape, -1.0, F32)
    padded[0:2, 0:slot_count] = pairs_ref[...].astype(F32)
    by_lane = padded[...]
    by_row = jnp.transpose(by_lane)

    def sides(row, col, axis):
        live = jnp.concatenate([row, row], axis) >= 0.0
        row = row.astype(jnp.int32) - first_block
        col = col.astype(jnp.int32) - first_block
        source = jnp.concatenate([row, col], axis)
        target = jnp.concatenate([col, row], axis)
        return live, source, target

    live, source, target = sides(by_row[:, 0:1], by_row[:, 1:2], 0)
    kind = jnp.where(target >= tile_blocks, AHEAD, LATE)
    first_own = sub_index * blocks_dev
    is_early = (source >= first_own) & (source < first_own + blocks_dev)
    kind = jnp.where(is_early, EARLY, kind)
    kind = jnp.where(source >= tile_blocks, FROM_AHEAD, kind)
    kind = jnp.where(live, kind, -1)
    hot = (kind == lax.broadcasted_iota(jnp.int32, (2 * width, LANES), 1)).astype(F32)
    below = lax.broadcasted_iota(jnp.int32, (2 * width, 2 * width), 0) > lax.broadcasted_iota(
        jnp.int32, (2 * width, 2 * width), 1
    )
    ranks = times(below.astype(F32).astype(BF16), hot.astype(BF16))
    rank = jnp.sum(ranks * hot, axis=1, keepdims=True).astype(jnp.int32)
    counts = jnp.sum(hot, axis=0, keepdims=True)
    at = jnp.where(live, kind * stride + rank, -1)
    spread = at == lax.broadcasted_iota(jnp.int32, (2 * width, len(KINDS) * stride), 1)
    live, source, target = sides(by_lane[0:1, :], by_lane[1:2, :], 1)
    lane = lax.broadcasted_iota(jnp.int32, (1, 2 * width), 1)
    block = jnp.where(lane < width, lane, lane - width + slot_count)
    fields = jnp.concatenate(
        [jnp.where(live, value, 0).astype(F32) for value in (block, source, target)]
        + [jnp.zeros((5, 2 * width), F32)],
        0,
    )
    found = times(fields.astype(BF16), spread.astype(F32).astype(BF16))
    entries = found[0:1] + 256.0 * found[1:2] + 65536.0 * found[2:3]
    entries = entries.astype(jnp.int32)
    idle = (tile_blocks + blocks_dev) * 65536
    idle_source = {
        EARLY: sub_index * blocks_dev,
        AHEAD: tile_blocks - blocks_dev,
        LATE: 0,
        FROM_AHEAD: tile_blocks,
    }
    place = lax.broadcasted_iota(jnp.int32, (1, stride), 1)
    for index in KINDS:
        span = slice(index * stride, (index + 1) * stride)
        count = counts[:, index : index + 1].astype(jnp.int32)
        lists_ref[:, span] = jnp.where(place < count, entries[:, span], idle + 256 * idle_source[index])
    lists_ref[:, len(KINDS) * stride : len(KINDS) * stride + LANES] = counts.astype(jnp.int32)
    by_column = jnp.sum(hot[:width], axis=0, keepdims=True)
    lists_ref[:, len(KINDS) * stride + LANES :] = by_column.astype(jnp.int32)
    copy = pltpu.make_async_copy(lists_ref, out_ref, sem)
    copy.start()
    copy.wait()


def turn_kernel(pairs_blocks_ref, after_ref, blocks_ref, sem):
    slot_count = pairs_blocks_ref.shape[0]
    copy = pltpu.make_async_copy(pairs_blocks_ref, blocks_ref.at[pl.ds(0, slot_count)], sem)
    copy.start()

    def one_group(group, carry):
        for step in range(TURN_GROUP):
            slot = group * TURN_GROUP + step
            blocks_ref[slot_count + slot] = jnp.transpose(pairs_blocks_ref[slot])
        return carry

    lax.fori_loop(0, slot_count // TURN_GROUP, one_group, 0)
    copy.wait()


def add_products(lists_ref, blocks_ref, slot_count, field, total, index, size, source_from=0, target_from=0):
    stride = list_stride(slot_count)
    idle = lists_ref[0, index * stride + stride - 1] >> 16
    count = lists_ref[0, len(KINDS) * stride + index]
    column_count = lists_ref[0, len(KINDS) * stride + LANES + index]

    def add_part(first, end, kind, plain, cuts):
        def one_group(group, carry):
            results = []
            for step in range(size):
                place = first + group * size + step
                entry = lists_ref[0, index * stride + place]
                block, source, target = entry & 255, (entry >> 8) & 255, entry >> 16
                if plain:
                    block = jnp.where(block >= slot_count, block - slot_count, block)
                if cuts:
                    target = jnp.where(place < end, target, idle)
                value = kind(field[source - source_from].astype(BF16), blocks_ref[block])
                results.append((target - target_from, value))
            for at, value in results:
                total[at] += value
            return carry

        lax.fori_loop(0, (end - first + size - 1) // size, one_group, 0)

    if blocks_ref.shape[0] > slot_count:
        add_part(0, count, times, False, False)
    else:
        add_part(0, column_count, times, True, True)
        add_part(column_count, count, times_transposed, True, False)


def raised(value, exponent):
    result = value
    for _ in range(exponent - 1):
        result = result * value
    return result


def widen(tile, columns):
    return jnp.concatenate([tile] * (columns // LANES), axis=1)


def lay_out(row_ref, field, first, blocks_dev, block_len, factor=None):
    for block in range(blocks_dev):
        piece = row_ref[:, block * block_len : (block + 1) * block_len].astype(F32)
        field[first + block] = piece if factor is None else piece * factor


def early_kernel(
    index, sub_count, slot_count, lists_ref, blocks_ref, diag_ref, noise_ref, own_ref, rounded_ref, total,
    *refs
):
    field = refs[-1]
    block_len = blocks_ref.shape[1]
    sub_index, blocks_dev, own_first, _ = device_place(block_len, own_ref, sub_count)
    if index == 0:
        largest = diag_ref[0].astype(F32)
        for block in range(1, blocks_dev):
            largest = jnp.maximum(largest, diag_ref[block].astype(F32))
        refs[0][...] = jnp.full(refs[0].shape, jnp.maximum(jnp.max(largest) * block_len, 1.0))
    lay_out(rounded_ref, field, own_first, blocks_dev, block_len)
    for block in range(total.shape[0]):
        total[block] = jnp.zeros(total.shape[1:], F32)
    for block in range(blocks_dev):
        span = slice(block * block_len, (block + 1) * block_len)
        value = noise_ref[:, span] * own_ref[:, span]
        total[own_first + block] = value + times(field[own_first + block].astype(BF16), diag_ref[block])
    add_products(lists_ref, blocks_ref, slot_count, field, total, EARLY, LONG_GROUP)


def ahead_kernel(index, sub_count, slot_count, lists_ref, blocks_ref, begun_ref, *refs):
    if index == 1:
        *refs, ratios_ref, total = refs
        row_refs, (even_ref, odd_ref, field_ref) = refs[:-3], refs[-3:]
        points_dev = even_ref.shape[1] - LANES
        units = [row_ref[:, points_dev:].astype(F32) for row_ref in row_refs]
        tile_unit = functools.reduce(jnp.maximum, units)
        ratios = [unit / tile_unit for unit in units]
        ratios_ref[...] = jnp.concatenate(ratios + [tile_unit], axis=1)
    else:
        row_refs, (even_ref, odd_ref, field_ref, total) = refs[:-4], refs[-4:]
        points_dev = even_ref.shape[1]
        if index:
            ratios_ref, *row_refs = row_refs
            ratios = [ratios_ref[:, step * LANES : (step + 1) * LANES] for step in range(sub_count)]
    block_len = blocks_ref.shape[1]
    blocks_dev = points_dev // block_len
    tile_blocks = blocks_dev * sub_count
    sub_index = lax.axis_index("sub")
    for step, row_ref in enumerate(row_refs):
        factor = widen(raised(ratios[step], index), block_len) if index else None
        lay_out(row_ref, field_ref, (sub_index ^ step) * blocks_dev, blocks_dev, block_len, factor)
    for block in range(blocks_dev):
        value = begun_ref[tile_blocks + block]
        total[block] = value * widen(raised(ratios[0], index), block_len) if index else value
    total[blocks_dev] = jnp.zeros(total.shape[1:], F32)
    add_products(lists_ref, blocks_ref, slot_count, field_ref, total, AHEAD, SHORT_GROUP, 0, tile_blocks)
    is_odd = lax.axis_index("tile") % 2 == 1
    for block in range(blocks_dev):
        span = slice(block * block_len, (block + 1) * block_len)
        products = total[block]
        first_row = field_ref[block]
        even_ref[:, span] = jnp.where(is_odd, first_row, products).astype(BF16)
        odd_ref[:, span] = jnp.where(is_odd, products, first_row).astype(BF16)
    if index == 1:
        even_ref[:, points_dev:] = tile_unit.astype(BF16)
        odd_ref[:, points_dev:] = tile_unit.astype(BF16)


def late_kernel(index, slot_count, lists_ref, blocks_ref, begun_ref, field_ref, *refs):
    total = refs[-1]
    if index:
        factor = widen(raised(refs[0][:, :LANES], index), total.shape[2])
        for block in range(total.shape[0]):
            total[block] = begun_ref[block] * factor
    else:
        total[...] = begun_ref[...]
    add_products(lists_ref, blocks_ref, slot_count, field_ref, total, LATE, LONG_GROUP)


def lost_weight(moments):
    inner = [moments[:, order : order + 1] for order in range(4)]
    first = inner[1] / inner[0]
    norm = inner[2] - first * inner[1]
    second = (inner[3] - 2.0 * first * inner[2] + first * first * inner[1]) / norm
    trace = first + 2.0 * second
    return jnp.where((norm > 0.0) & (trace > 0.0) & (trace < 30.0), -trace, 0.0)


def part_kernel(
    index, sub_count, slot_count, lists_ref, blocks_ref, begun_ref, field_ref, even_ref, odd_ref,
    moments_in_ref, unit_ref, *refs
):
    *refs, total, ahead = refs
    if index == 1:
        ratios_ref, *refs, sides_ref = refs
    elif index:
        ratios_ref, sides_ref, *refs = refs
    if index + 1 == ITERS:
        lost_refs, refs = refs[: sub_count - 1], refs[sub_count - 1 :]
    part_refs, moments_ref, *kept_refs = refs[:sub_count], *refs[sub_count:]
    block_len = blocks_ref.shape[1]
    sub_index, blocks_dev, own_first, tile_blocks = device_place(block_len, part_refs[0], sub_count)
    is_odd = lax.axis_index("tile") % 2 == 1
    if index == 1:
        points_dev = blocks_dev * block_len
        even = even_ref[:, points_dev:].astype(F32)
        odd = odd_ref[:, points_dev:].astype(F32)
        tile_unit = ratios_ref[:, sub_count * LANES :]
        sides = [jnp.where(is_odd, even, odd) / tile_unit, jnp.where(is_odd, odd, even) / tile_unit]
        sides_ref[...] = jnp.concatenate(sides, axis=1)
    elif index:
        sides = [sides_ref[:, :LANES], sides_ref[:, LANES:]]
    if index:
        before, after = [widen(raised(side, index), block_len) for side in sides]
    for block in range(blocks_dev):
        span = slice(block * block_len, (block + 1) * block_len)
        even = even_ref[:, span].astype(F32)
        odd = odd_ref[:, span].astype(F32)
        products = jnp.where(is_odd, even, odd)
        first_row = jnp.where(is_odd, odd, even)
        ahead[block] = first_row * after if index else first_row
        total[block] = begun_ref[block] + (products * before if index else products)
    for block in range(blocks_dev, tile_blocks):
        total[block] = begun_ref[block]
    total[begun_ref.shape[0] - 1] = jnp.zeros(total.shape[1:], F32)
    add_products(lists_ref, blocks_ref, slot_count, ahead, total, FROM_AHEAD, SHORT_GROUP, tile_blocks, 0)
    moments = moments_in_ref[...]
    if index + 1 == ITERS:
        weight = lost_weight(moments) * ratios_ref[:, :1]
    for step in range(sub_count):
        first = (sub_index ^ step) * blocks_dev
        for block in range(blocks_dev):
            span = slice(block * block_len, (block + 1) * block_len)
            value = total[first + block]
            if step and index + 1 == ITERS:
                value += weight * lost_refs[step - 1][:, span]
            rounded = value.astype(part_refs[step].dtype)
            part_refs[step][:, span] = rounded
            if step and kept_refs:
                kept_refs[step - 1][:, span] = value - rounded.astype(F32)
    if index + 1 == ITERS:
        product = jnp.zeros(total.shape[1:], F32)
        unit = unit_ref[...]
        scale = widen(1.0 / (raised(ratios_ref[:, :LANES], 2 * index) * unit), block_len)
        for block in range(tile_blocks):
            product += field_ref[block] * (total[block] * scale)
        last = jnp.sum(product, axis=1, keepdims=True)
        lane = lax.broadcasted_iota(jnp.int32, moments.shape, 1)
        moments = jnp.where(lane == 2 * ITERS - 1, last, moments)
        moments = jnp.where(lane == 2 * ITERS, unit, moments)
    moments_ref[...] = moments


def join_kernel(index, after_ref, unit_ref, ratios_ref, own_ref, old_ref, moments_in_ref, *refs):
    part_refs = refs[:-3]
    next_ref, rounded_ref, moments_ref = refs[-3:]
    points_dev = own_ref.shape[1]
    value = own_ref[...]
    for part_ref in part_refs:
        value += part_ref[...].astype(F32)
    unit = unit_ref[...]
    divisor = raised(ratios_ref[:, :LANES], index) * unit if index else unit
    value = value * widen(1.0 / divisor, points_dev)
    next_ref[...] = value
    rounded_ref[:, :points_dev] = value.astype(BF16)
    if index == 0:
        rounded_ref[:, points_dev:] = unit.astype(BF16)
    old = old_ref[...]
    lane = lax.broadcasted_iota(jnp.int32, moments_ref.shape, 1)
    moments = moments_in_ref[...] if index else jnp.zeros(moments_ref.shape, F32)
    found = {2 * index + 1: old * value, 2 * index + 2: value * value}
    if index == 0:
        found[0] = old * old
    for order, product in found.items():
        moments = jnp.where(lane == order, jnp.sum(product, axis=1, keepdims=True), moments)
    moments_ref[...] = moments


def add_moments_kernel(first_ref, second_ref, sum_ref):
    unit_lane = 2 * ITERS
    lane = lax.broadcasted_iota(jnp.int32, sum_ref.shape, 1)
    units = [ref[:, unit_lane : unit_lane + 1] for ref in (first_ref, second_ref)]
    larger = jnp.maximum(units[0], units[1])
    result = jnp.zeros(sum_ref.shape, F32)
    for ref, unit in zip((first_ref, second_ref), units):
        ratio = unit / larger
        value = ref[...]
        for order in range(1, unit_lane):
            value = jnp.where(lane >= order, value * ratio, value)
        result += value
    sum_ref[...] = jnp.where(lane == unit_lane, larger, result)


def finish_kernel(sub_count, moments_ref, unit_ref, ratios_ref, *refs):
    part_refs, basis_refs = refs[:sub_count], refs[sub_count:-2]
    solution_ref, residual_ref = refs[-2:]
    moments = [moments_ref[:, order : order + 1] for order in range(2 * ITERS)]
    largest = moments_ref[:, 2 * ITERS : 2 * ITERS + 1]
    unit = unit_ref[:, :1]
    ratio = unit / largest

    def inner(first, second, shift):
        value = 0.0
        for i, a in enumerate(first):
            for j, b in enumerate(second):
                value = value + a * b * moments[i + j + shift]
        return value

    one = jnp.ones_like(moments[0])
    zero = jnp.zeros_like(one)
    direction, residual = [one], [one]
    answer = [zero] * ITERS
    norm_now = moments[0]
    for iteration in range(ITERS):
        step_size = norm_now / inner(direction, direction, 1)
        for power, weight in enumerate(direction):
            answer[power] = answer[power] + step_size * weight
        residual = residual + [zero]
        for power, weight in enumerate(direction):
            residual[power + 1] = residual[power + 1] - step_size * weight
        if iteration + 1 < ITERS:
            norm_next = inner(residual, residual, 0)
            direction = [
                value + (norm_next / norm_now) * old
                for value, old in zip(residual, direction + [zero])
            ]
            norm_now = norm_next
    fields = [basis_ref[...] for basis_ref in basis_refs]
    fields.append(sum(part_ref[...].astype(F32) for part_ref in part_refs))
    for order in range(1, ITERS + 1):
        scale = raised(ratio, order)
        if order < ITERS:
            answer[order] = answer[order] * scale
        else:
            scale = scale / (raised(ratios_ref[:, :1], ITERS - 1) * unit)
        residual[order] = residual[order] * scale
    answer = [weight / largest for weight in answer]
    solution_ref[...] = sum(weight * field for weight, field in zip(answer, fields))
    residual_ref[...] = sum(weight * field for weight, field in zip(residual, fields))


def shape(rows, columns, kind):
    return jax.ShapeDtypeStruct((rows, columns), kind)


def exchange(block, axis, step):
    count = lax.axis_size(axis)
    return lax.ppermute(block, axis, [(i, i ^ step) for i in range(count)])


def swap(block, axis, first):
    count = lax.axis_size(axis)
    route = []
    for i in range(first, count - 1, 2):
        route += [(i, i + 1), (i + 1, i)]
    return lax.ppermute(block, axis, route)


def call(kernel, outs, ins, name, cost=0, **options):
    single = not isinstance(outs, tuple)
    specs = [SMEM if value.dtype == jnp.int32 else VMEM for value in ins]
    options.setdefault("in_specs", specs)
    options.setdefault("out_specs", VMEM if single else (VMEM,) * len(outs))
    return pl.pallas_call(
        kernel,
        out_shape=outs,
        compiler_params=PARAMS,
        name=name,
        cost_estimate=pl.CostEstimate(flops=int(cost * 1e9), bytes_accessed=0, transcendentals=0),
        **options,
    )(*ins)


def on_device(right_side, point_order, noise_var, block_pairs, pair_blocks, diag_blocks):
    sub_count = lax.axis_size("sub")
    tile_count = lax.axis_size("tile")
    rhs_count, points_dev = right_side.shape
    blocks_dev, block_len = diag_blocks.shape[:2]
    extended = (sub_count + 1) * blocks_dev
    noise = noise_var[None, :]
    full = shape(rhs_count, points_dev, F32)
    half = shape(rhs_count, points_dev, BF16)
    scalars = shape(rhs_count, LANES, F32)
    sums = jax.ShapeDtypeStruct((extended + 1, rhs_count, block_len), F32)

    def scratch(blocks):
        return pltpu.VMEM((blocks, rhs_count, block_len), F32)

    slot_count = pair_blocks.shape[0]
    width = -(-slot_count // LANES) * LANES
    assert 2 * width <= 256 and extended < 256 and slot_count % TURN_GROUP == 0
    lists_shape = (1, len(KINDS) * list_stride(slot_count) + 2 * LANES)
    lists = call(
        functools.partial(lists_kernel, sub_count, blocks_dev, slot_count),
        pltpu.SMEM(lists_shape, jnp.int32),
        (block_pairs.T,),
        "lists",
        1,
        in_specs=[VMEM],
        out_specs=SMEM,
        scratch_shapes=[
            pltpu.VMEM((8, width), F32),
            pltpu.VMEM(lists_shape, jnp.int32),
            pltpu.SemaphoreType.DMA(()),
        ],
    )
    blocks = pair_blocks
    field, rounded = call(
        order_kernel,
        (full, half),
        [pltpu.with_memory_space_constraint(value, pltpu.HBM) for value in (right_side, point_order)],
        "curve_order",
        10,
        in_specs=[pl.BlockSpec(memory_space=pltpu.HBM)] * 2,
        scratch_shapes=[
            pltpu.VMEM(right_side.shape, F32),
            pltpu.VMEM(point_order.shape, jnp.int32),
            pltpu.SemaphoreType.DMA((2,)),
        ],
    )
    basis = [field]
    moments = unit = jnp.zeros(scalars.shape, F32)
    ratios = sides = ()
    for index in range(ITERS):
        is_last = index + 1 == ITERS
        rows = [exchange(rounded, "sub", step) for step in range(1, sub_count)]
        begun = call(
            functools.partial(early_kernel, index, sub_count, slot_count),
            (sums,) if index else (sums, scalars),
            (lists, blocks, diag_blocks, noise, field, rounded),
            "early",
            3,
            scratch_shapes=[scratch(extended)],
        )
        if index == 0:
            begun, unit = begun
        else:
            (begun,) = begun
        message = shape(rhs_count, points_dev + LANES, BF16) if index == 1 else half
        even, odd, tile_field, *found = call(
            functools.partial(ahead_kernel, index, sub_count, slot_count),
            (message, message, jax.ShapeDtypeStruct((sub_count * blocks_dev, rhs_count, block_len), F32))
            + ((shape(rhs_count, (sub_count + 1) * LANES, F32),) if index == 1 else ()),
            (lists, blocks, begun, *ratios, rounded, *rows),
            "ahead",
            1,
            scratch_shapes=[scratch(blocks_dev + 1)],
        )
        ratios = ratios or tuple(found)
        even = swap(even, "tile", 0)
        odd = swap(odd, "tile", 1)
        begun = call(
            functools.partial(late_kernel, index, slot_count),
            sums,
            (lists, blocks, begun, tile_field, *ratios),
            "late",
            3,
        )
        part = shape(rhs_count, points_dev, F32 if is_last else BF16)
        found = call(
            functools.partial(part_kernel, index, sub_count, slot_count),
            (full,)
            + (part,) * (sub_count - 1)
            + (scalars,)
            + ((full,) * (sub_count - 1) if index + 2 == ITERS else ())
            + ((shape(rhs_count, 2 * LANES, F32),) if index == 1 else ()),
            (lists, blocks, begun, tile_field, even, odd, moments, unit, *ratios, *sides, *(lost if is_last else ())),
            "parts",
            1,
            scratch_shapes=[scratch(extended + 1), scratch(blocks_dev)],
        )
        parts, moments = list(found[:sub_count]), found[sub_count]
        if index == 1:
            sides = (found[-1],)
        lost = found[sub_count + 1 : 2 * sub_count]
        if is_last:
            break
        if index == 0:
            blocks = call(
                turn_kernel,
                pltpu.VMEM((2 * slot_count, block_len, block_len), BF16),
                (pair_blocks, moments),
                "turn",
                4,
                scratch_shapes=[pltpu.SemaphoreType.DMA(())],
            )
        arrived = [exchange(parts[step], "sub", step) for step in range(sub_count - 1, 0, -1)]
        field, rounded, moments = call(
            functools.partial(join_kernel, index),
            (full, half if index else shape(rhs_count, points_dev + LANES, BF16), scalars),
            (blocks, unit, *(ratios or (unit,)), parts[0], field, moments, *arrived),
            "join",
        )
        basis.append(field)
    arrived = []
    for axis, count in (("sub", sub_count), ("tile", tile_count)):
        step = 1
        while step < count:
            moments = call(add_moments_kernel, scalars, (moments, exchange(moments, axis, step)), "add_moments")
            if len(arrived) < sub_count - 1:
                far = sub_count - 1 - len(arrived)
                arrived.append(exchange(parts[far], "sub", far))
                moments, *parts = lax.optimization_barrier((moments, *parts))
            step *= 2
    for far in range(sub_count - 1 - len(arrived), 0, -1):
        arrived.append(exchange(parts[far], "sub", far))
    return call(
        functools.partial(finish_kernel, sub_count),
        (full, full),
        (moments, unit, *ratios, parts[0], *arrived, *basis),
        "finish",
    )


def solution(mesh):
    placed = (
        P(None, ("tile", "sub")),
        P(("tile", "sub"), None),
        P(("tile", "sub")),
        P(("tile", "sub"), None),
        P(("tile", "sub"), None, None),
        P(("tile", "sub"), None, None),
    )
    return jax.shard_map(
        on_device,
        mesh=mesh,
        in_specs=placed,
        out_specs=(P(None, ("tile", "sub")), P(None, ("tile", "sub"))),
        check_vma=False,
    )
```

```python
import functools

import jax
import jax.numpy as jnp
from jax import lax
from jax.experimental import pallas as pl
from jax.experimental.pallas import tpu as pltpu
from jax.sharding import PartitionSpec as P

ITERS = 3
LANES = 128
LONG_GROUP = 16
SHORT_GROUP = 8
TURN_GROUP = 4
F32 = jnp.float32
BF16 = jnp.bfloat16
VMEM = pl.BlockSpec(memory_space=pltpu.VMEM)
SMEM = pl.BlockSpec(memory_space=pltpu.SMEM)
EARLY, AHEAD, LATE, FROM_AHEAD = KINDS = range(4)
PARAMS = pltpu.CompilerParams(vmem_limit_bytes=4 * 1024 * 1024)


def times(field, block):
    return lax.dot_general(field, block, (((1,), (0,)), ((), ())), preferred_element_type=F32)


def times_transposed(field, block):
    return lax.dot_general(field, block, (((1,), (1,)), ((), ())), preferred_element_type=F32)


def order_kernel(right_in, order_in, curve_ref, rounded_ref, right_ref, order_ref, sems):
    copies = [
        pltpu.make_async_copy(right_in, right_ref, sems.at[0]),
        pltpu.make_async_copy(order_in, order_ref, sems.at[1]),
    ]
    for copy in copies:
        copy.start()
    for copy in copies:
        copy.wait()
    rhs_count, points = right_ref.shape
    for start in range(0, points, LANES):
        at = jnp.broadcast_to(order_ref[:, start : start + LANES], (rhs_count, LANES))
        chunk = at // LANES
        lane = at % LANES
        result = jnp.zeros((rhs_count, LANES), F32)
        for source in range(points // LANES):
            values = right_ref[:, source * LANES : (source + 1) * LANES]
            picked = jnp.take_along_axis(values, lane, axis=1)
            result = jnp.where(chunk == source, picked, result)
        curve_ref[:, start : start + LANES] = result
        rounded_ref[:, start : start + LANES] = result.astype(BF16)


def device_place(block_len, field_ref, sub_count):
    blocks_dev = field_ref.shape[1] // block_len
    sub_index = lax.axis_index("sub")
    return sub_index, blocks_dev, sub_index * blocks_dev, blocks_dev * sub_count


def list_stride(slot_count):
    return -(-(2 * slot_count + LONG_GROUP) // LANES) * LANES


def lists_kernel(sub_count, blocks_dev, slot_count, pairs_ref, out_ref, padded, lists_ref, sem):
    width = padded.shape[1]
    stride = list_stride(slot_count)
    sub_index = lax.axis_index("sub")
    tile_blocks = blocks_dev * sub_count
    first_block = lax.axis_index("tile") * tile_blocks
    padded[...] = jnp.full(padded.shape, -1.0, F32)
    padded[0:2, 0:slot_count] = pairs_ref[...].astype(F32)
    by_lane = padded[...]
    by_row = jnp.transpose(by_lane)

    def sides(row, col, axis):
        live = jnp.concatenate([row, row], axis) >= 0.0
        row = row.astype(jnp.int32) - first_block
        col = col.astype(jnp.int32) - first_block
        source = jnp.concatenate([row, col], axis)
        target = jnp.concatenate([col, row], axis)
        return live, source, target

    live, source, target = sides(by_row[:, 0:1], by_row[:, 1:2], 0)
    kind = jnp.where(target >= tile_blocks, AHEAD, LATE)
    first_own = sub_index * blocks_dev
    is_early = (source >= first_own) & (source < first_own + blocks_dev)
    kind = jnp.where(is_early, EARLY, kind)
    kind = jnp.where(source >= tile_blocks, FROM_AHEAD, kind)
    kind = jnp.where(live, kind, -1)
    hot = (kind == lax.broadcasted_iota(jnp.int32, (2 * width, LANES), 1)).astype(F32)
    below = lax.broadcasted_iota(jnp.int32, (2 * width, 2 * width), 0) > lax.broadcasted_iota(
        jnp.int32, (2 * width, 2 * width), 1
    )
    ranks = times(below.astype(F32).astype(BF16), hot.astype(BF16))
    rank = jnp.sum(ranks * hot, axis=1, keepdims=True).astype(jnp.int32)
    counts = jnp.sum(hot, axis=0, keepdims=True)
    at = jnp.where(live, kind * stride + rank, -1)
    spread = at == lax.broadcasted_iota(jnp.int32, (2 * width, len(KINDS) * stride), 1)
    live, source, target = sides(by_lane[0:1, :], by_lane[1:2, :], 1)
    lane = lax.broadcasted_iota(jnp.int32, (1, 2 * width), 1)
    block = jnp.where(lane < width, lane, lane - width + slot_count)
    fields = jnp.concatenate(
        [jnp.where(live, value, 0).astype(F32) for value in (block, source, target)]
        + [jnp.zeros((5, 2 * width), F32)],
        0,
    )
    found = times(fields.astype(BF16), spread.astype(F32).astype(BF16))
    entries = found[0:1] + 256.0 * found[1:2] + 65536.0 * found[2:3]
    entries = entries.astype(jnp.int32)
    idle = (tile_blocks + blocks_dev) * 65536
    idle_source = {
        EARLY: sub_index * blocks_dev,
        AHEAD: tile_blocks - blocks_dev,
        LATE: 0,
        FROM_AHEAD: tile_blocks,
    }
    place = lax.broadcasted_iota(jnp.int32, (1, stride), 1)
    for index in KINDS:
        span = slice(index * stride, (index + 1) * stride)
        count = counts[:, index : index + 1].astype(jnp.int32)
        lists_ref[:, span] = jnp.where(place < count, entries[:, span], idle + 256 * idle_source[index])
    lists_ref[:, len(KINDS) * stride : len(KINDS) * stride + LANES] = counts.astype(jnp.int32)
    by_column = jnp.sum(hot[:width], axis=0, keepdims=True)
    lists_ref[:, len(KINDS) * stride + LANES :] = by_column.astype(jnp.int32)
    copy = pltpu.make_async_copy(lists_ref, out_ref, sem)
    copy.start()
    copy.wait()


def turn_kernel(pairs_blocks_ref, after_ref, blocks_ref, sem):
    slot_count = pairs_blocks_ref.shape[0]
    copy = pltpu.make_async_copy(pairs_blocks_ref, blocks_ref.at[pl.ds(0, slot_count)], sem)
    copy.start()

    def one_group(group, carry):
        for step in range(TURN_GROUP):
            slot = group * TURN_GROUP + step
            blocks_ref[slot_count + slot] = jnp.transpose(pairs_blocks_ref[slot])
        return carry

    lax.fori_loop(0, slot_count // TURN_GROUP, one_group, 0)
    copy.wait()


def add_products(lists_ref, blocks_ref, slot_count, field, total, index, size, source_from=0, target_from=0):
    stride = list_stride(slot_count)
    idle = lists_ref[0, index * stride + stride - 1] >> 16
    count = lists_ref[0, len(KINDS) * stride + index]
    column_count = lists_ref[0, len(KINDS) * stride + LANES + index]

    def add_part(first, end, kind, plain, cuts):
        def one_group(group, carry):
            results = []
            for step in range(size):
                place = first + group * size + step
                entry = lists_ref[0, index * stride + place]
                block, source, target = entry & 255, (entry >> 8) & 255, entry >> 16
                if plain:
                    block = jnp.where(block >= slot_count, block - slot_count, block)
                if cuts:
                    target = jnp.where(place < end, target, idle)
                value = kind(field[source - source_from].astype(BF16), blocks_ref[block])
                results.append((target - target_from, value))
            for at, value in results:
                total[at] += value
            return carry

        lax.fori_loop(0, (end - first + size - 1) // size, one_group, 0)

    if blocks_ref.shape[0] > slot_count:
        add_part(0, count, times, False, False)
    else:
        add_part(0, column_count, times, True, True)
        add_part(column_count, count, times_transposed, True, False)


def raised(value, exponent):
    result = value
    for _ in range(exponent - 1):
        result = result * value
    return result


def widen(tile, columns):
    return jnp.concatenate([tile] * (columns // LANES), axis=1)


def lay_out(row_ref, field, first, blocks_dev, block_len, factor=None):
    for block in range(blocks_dev):
        piece = row_ref[:, block * block_len : (block + 1) * block_len].astype(F32)
        field[first + block] = piece if factor is None else piece * factor


def early_kernel(
    index, sub_count, slot_count, lists_ref, blocks_ref, diag_ref, noise_ref, own_ref, rounded_ref, total,
    *refs
):
    field = refs[-1]
    block_len = blocks_ref.shape[1]
    sub_index, blocks_dev, own_first, _ = device_place(block_len, own_ref, sub_count)
    if index == 0:
        largest = diag_ref[0].astype(F32)
        for block in range(1, blocks_dev):
            largest = jnp.maximum(largest, diag_ref[block].astype(F32))
        refs[0][...] = jnp.full(refs[0].shape, jnp.maximum(jnp.max(largest) * block_len, 1.0))
    lay_out(rounded_ref, field, own_first, blocks_dev, block_len)
    for block in range(total.shape[0]):
        total[block] = jnp.zeros(total.shape[1:], F32)
    for block in range(blocks_dev):
        span = slice(block * block_len, (block + 1) * block_len)
        value = noise_ref[:, span] * own_ref[:, span]
        total[own_first + block] = value + times(field[own_first + block].astype(BF16), diag_ref[block])
    add_products(lists_ref, blocks_ref, slot_count, field, total, EARLY, LONG_GROUP)


def ahead_kernel(index, sub_count, slot_count, lists_ref, blocks_ref, begun_ref, *refs):
    if index == 1:
        *refs, ratios_ref, total = refs
        row_refs, (even_ref, odd_ref, field_ref) = refs[:-3], refs[-3:]
        points_dev = even_ref.shape[1] - LANES
        units = [row_ref[:, points_dev:].astype(F32) for row_ref in row_refs]
        tile_unit = functools.reduce(jnp.maximum, units)
        ratios = [unit / tile_unit for unit in units]
        ratios_ref[...] = jnp.concatenate(ratios + [tile_unit], axis=1)
    else:
        row_refs, (even_ref, odd_ref, field_ref, total) = refs[:-4], refs[-4:]
        points_dev = even_ref.shape[1]
        if index:
            ratios_ref, *row_refs = row_refs
            ratios = [ratios_ref[:, step * LANES : (step + 1) * LANES] for step in range(sub_count)]
    block_len = blocks_ref.shape[1]
    blocks_dev = points_dev // block_len
    tile_blocks = blocks_dev * sub_count
    sub_index = lax.axis_index("sub")
    for step, row_ref in enumerate(row_refs):
        factor = widen(raised(ratios[step], index), block_len) if index else None
        lay_out(row_ref, field_ref, (sub_index ^ step) * blocks_dev, blocks_dev, block_len, factor)
    for block in range(blocks_dev):
        value = begun_ref[tile_blocks + block]
        total[block] = value * widen(raised(ratios[0], index), block_len) if index else value
    total[blocks_dev] = jnp.zeros(total.shape[1:], F32)
    add_products(lists_ref, blocks_ref, slot_count, field_ref, total, AHEAD, SHORT_GROUP, 0, tile_blocks)
    is_odd = lax.axis_index("tile") % 2 == 1
    for block in range(blocks_dev):
        span = slice(block * block_len, (block + 1) * block_len)
        products = total[block]
        first_row = field_ref[block]
        even_ref[:, span] = jnp.where(is_odd, first_row, products).astype(BF16)
        odd_ref[:, span] = jnp.where(is_odd, products, first_row).astype(BF16)
    if index == 1:
        even_ref[:, points_dev:] = tile_unit.astype(BF16)
        odd_ref[:, points_dev:] = tile_unit.astype(BF16)


def late_kernel(index, slot_count, lists_ref, blocks_ref, begun_ref, field_ref, *refs):
    total = refs[-1]
    if index:
        factor = widen(raised(refs[0][:, :LANES], index), total.shape[2])
        for block in range(total.shape[0]):
            total[block] = begun_ref[block] * factor
    else:
        total[...] = begun_ref[...]
    add_products(lists_ref, blocks_ref, slot_count, field_ref, total, LATE, LONG_GROUP)


def neighbours(is_odd, even, odd):
    return jnp.where(is_odd, even, odd), jnp.where(is_odd, odd, even)


def curvature_kernel(
    begun_ref, field_ref, even_ref, odd_ref, moments_in_ref, unit_ref, ratios_ref, sides_ref, moments_ref
):
    index = ITERS - 1
    block_len = begun_ref.shape[2]
    blocks_dev = even_ref.shape[1] // block_len
    is_odd = lax.axis_index("tile") % 2 == 1
    unit = unit_ref[...]
    scale = widen(1.0 / (raised(ratios_ref[:, :LANES], 2 * index) * unit), block_len)
    before = widen(2.0 * raised(sides_ref[:, :LANES], index), block_len)
    product = jnp.zeros(begun_ref.shape[1:], F32)
    for block in range(field_ref.shape[0]):
        value = begun_ref[block]
        if block < blocks_dev:
            span = slice(block * block_len, (block + 1) * block_len)
            arrived, _ = neighbours(is_odd, even_ref[:, span].astype(F32), odd_ref[:, span].astype(F32))
            value += arrived * before
        product += field_ref[block] * (value * scale)
    last = jnp.sum(product, axis=1, keepdims=True)
    moments = moments_in_ref[...]
    lane = lax.broadcasted_iota(jnp.int32, moments.shape, 1)
    moments = jnp.where(lane == 2 * ITERS - 1, last, moments)
    moments_ref[...] = jnp.where(lane == 2 * ITERS, unit, moments)


def lost_weight(moments):
    inner = [moments[:, order : order + 1] for order in range(4)]
    first = inner[1] / inner[0]
    norm = inner[2] - first * inner[1]
    second = (inner[3] - 2.0 * first * inner[2] + first * first * inner[1]) / norm
    trace = first + 2.0 * second
    return jnp.where((norm > 0.0) & (trace > 0.0) & (trace < 30.0), -trace, 0.0)


def part_kernel(
    index, sub_count, slot_count, lists_ref, blocks_ref, begun_ref, field_ref, even_ref, odd_ref,
    moments_in_ref, *refs
):
    *refs, total, ahead = refs
    if index == 1:
        ratios_ref, *refs, sides_ref = refs
    elif index:
        ratios_ref, sides_ref, *refs = refs
    if index + 1 == ITERS:
        lost_refs, refs = refs[: sub_count - 1], refs[sub_count - 1 :]
    part_refs, moments_ref, *kept_refs = refs[:sub_count], *refs[sub_count:]
    block_len = blocks_ref.shape[1]
    sub_index, blocks_dev, own_first, tile_blocks = device_place(block_len, part_refs[0], sub_count)
    is_odd = lax.axis_index("tile") % 2 == 1
    if index == 1:
        points_dev = blocks_dev * block_len
        even = even_ref[:, points_dev:].astype(F32)
        odd = odd_ref[:, points_dev:].astype(F32)
        tile_unit = ratios_ref[:, sub_count * LANES :]
        sides = [side / tile_unit for side in neighbours(is_odd, even, odd)]
        sides_ref[...] = jnp.concatenate(sides, axis=1)
    elif index:
        sides = [sides_ref[:, :LANES], sides_ref[:, LANES:]]
    if index:
        before, after = [widen(raised(side, index), block_len) for side in sides]
    for block in range(blocks_dev):
        span = slice(block * block_len, (block + 1) * block_len)
        even = even_ref[:, span].astype(F32)
        odd = odd_ref[:, span].astype(F32)
        products, first_row = neighbours(is_odd, even, odd)
        ahead[block] = first_row * after if index else first_row
        total[block] = begun_ref[block] + (products * before if index else products)
    for block in range(blocks_dev, tile_blocks):
        total[block] = begun_ref[block]
    total[begun_ref.shape[0] - 1] = jnp.zeros(total.shape[1:], F32)
    add_products(lists_ref, blocks_ref, slot_count, ahead, total, FROM_AHEAD, SHORT_GROUP, tile_blocks, 0)
    moments = moments_in_ref[...]
    if index + 1 == ITERS:
        weight = lost_weight(moments) * ratios_ref[:, :1]
    for step in range(sub_count):
        first = (sub_index ^ step) * blocks_dev
        for block in range(blocks_dev):
            span = slice(block * block_len, (block + 1) * block_len)
            value = total[first + block]
            if step and index + 1 == ITERS:
                value += weight * lost_refs[step - 1][:, span]
            rounded = value.astype(part_refs[step].dtype)
            part_refs[step][:, span] = rounded
            if step and kept_refs:
                kept_refs[step - 1][:, span] = value - rounded.astype(F32)
    moments_ref[...] = moments


def join_kernel(index, after_ref, unit_ref, ratios_ref, own_ref, old_ref, moments_in_ref, *refs):
    part_refs = refs[:-3]
    next_ref, rounded_ref, moments_ref = refs[-3:]
    points_dev = own_ref.shape[1]
    value = own_ref[...]
    for part_ref in part_refs:
        value += part_ref[...].astype(F32)
    unit = unit_ref[...]
    divisor = raised(ratios_ref[:, :LANES], index) * unit if index else unit
    value = value * widen(1.0 / divisor, points_dev)
    next_ref[...] = value
    rounded_ref[:, :points_dev] = value.astype(BF16)
    if index == 0:
        rounded_ref[:, points_dev:] = unit.astype(BF16)
    old = old_ref[...]
    lane = lax.broadcasted_iota(jnp.int32, moments_ref.shape, 1)
    moments = moments_in_ref[...] if index else jnp.zeros(moments_ref.shape, F32)
    found = {2 * index + 1: old * value, 2 * index + 2: value * value}
    if index == 0:
        found[0] = old * old
    for order, product in found.items():
        moments = jnp.where(lane == order, jnp.sum(product, axis=1, keepdims=True), moments)
    moments_ref[...] = moments


def add_moments_kernel(first_ref, second_ref, sum_ref):
    unit_lane = 2 * ITERS
    lane = lax.broadcasted_iota(jnp.int32, sum_ref.shape, 1)
    units = [ref[:, unit_lane : unit_lane + 1] for ref in (first_ref, second_ref)]
    larger = jnp.maximum(units[0], units[1])
    result = jnp.zeros(sum_ref.shape, F32)
    for ref, unit in zip((first_ref, second_ref), units):
        ratio = unit / larger
        value = ref[...]
        for order in range(1, unit_lane):
            value = jnp.where(lane >= order, value * ratio, value)
        result += value
    sum_ref[...] = jnp.where(lane == unit_lane, larger, result)


def finish_kernel(sub_count, moments_ref, unit_ref, ratios_ref, *refs):
    part_refs, basis_refs = refs[:sub_count], refs[sub_count:-2]
    solution_ref, residual_ref = refs[-2:]
    moments = [moments_ref[:, order : order + 1] for order in range(2 * ITERS)]
    largest = moments_ref[:, 2 * ITERS : 2 * ITERS + 1]
    unit = unit_ref[:, :1]
    ratio = unit / largest

    def inner(first, second, shift):
        value = 0.0
        for i, a in enumerate(first):
            for j, b in enumerate(second):
                value = value + a * b * moments[i + j + shift]
        return value

    one = jnp.ones_like(moments[0])
    zero = jnp.zeros_like(one)
    direction, residual = [one], [one]
    answer = [zero] * ITERS
    norm_now = moments[0]
    for iteration in range(ITERS):
        step_size = norm_now / inner(direction, direction, 1)
        for power, weight in enumerate(direction):
            answer[power] = answer[power] + step_size * weight
        residual = residual + [zero]
        for power, weight in enumerate(direction):
            residual[power + 1] = residual[power + 1] - step_size * weight
        if iteration + 1 < ITERS:
            norm_next = inner(residual, residual, 0)
            direction = [
                value + (norm_next / norm_now) * old
                for value, old in zip(residual, direction + [zero])
            ]
            norm_now = norm_next
    fields = [basis_ref[...] for basis_ref in basis_refs]
    fields.append(sum(part_ref[...].astype(F32) for part_ref in part_refs))
    for order in range(1, ITERS + 1):
        scale = raised(ratio, order)
        if order < ITERS:
            answer[order] = answer[order] * scale
        else:
            scale = scale / (raised(ratios_ref[:, :1], ITERS - 1) * unit)
        residual[order] = residual[order] * scale
    answer = [weight / largest for weight in answer]
    solution_ref[...] = sum(weight * field for weight, field in zip(answer, fields))
    residual_ref[...] = sum(weight * field for weight, field in zip(residual, fields))


def shape(rows, columns, kind):
    return jax.ShapeDtypeStruct((rows, columns), kind)


def exchange(block, axis, step):
    count = lax.axis_size(axis)
    return lax.ppermute(block, axis, [(i, i ^ step) for i in range(count)])


def swap(block, axis, first):
    count = lax.axis_size(axis)
    route = []
    for i in range(first, count - 1, 2):
        route += [(i, i + 1), (i + 1, i)]
    return lax.ppermute(block, axis, route)


def call(kernel, outs, ins, name, cost=0, **options):
    single = not isinstance(outs, tuple)
    specs = [SMEM if value.dtype == jnp.int32 else VMEM for value in ins]
    options.setdefault("in_specs", specs)
    options.setdefault("out_specs", VMEM if single else (VMEM,) * len(outs))
    return pl.pallas_call(
        kernel,
        out_shape=outs,
        compiler_params=PARAMS,
        name=name,
        cost_estimate=pl.CostEstimate(flops=int(cost * 1e9), bytes_accessed=0, transcendentals=0),
        **options,
    )(*ins)


def on_device(right_side, point_order, noise_var, block_pairs, pair_blocks, diag_blocks):
    sub_count = lax.axis_size("sub")
    tile_count = lax.axis_size("tile")
    rhs_count, points_dev = right_side.shape
    blocks_dev, block_len = diag_blocks.shape[:2]
    extended = (sub_count + 1) * blocks_dev
    noise = noise_var[None, :]
    full = shape(rhs_count, points_dev, F32)
    half = shape(rhs_count, points_dev, BF16)
    scalars = shape(rhs_count, LANES, F32)
    sums = jax.ShapeDtypeStruct((extended + 1, rhs_count, block_len), F32)

    def scratch(blocks):
        return pltpu.VMEM((blocks, rhs_count, block_len), F32)

    slot_count = pair_blocks.shape[0]
    width = -(-slot_count // LANES) * LANES
    assert 2 * width <= 256 and extended < 256 and slot_count % TURN_GROUP == 0
    lists_shape = (1, len(KINDS) * list_stride(slot_count) + 2 * LANES)
    lists = call(
        functools.partial(lists_kernel, sub_count, blocks_dev, slot_count),
        pltpu.SMEM(lists_shape, jnp.int32),
        (block_pairs.T,),
        "lists",
        1,
        in_specs=[VMEM],
        out_specs=SMEM,
        scratch_shapes=[
            pltpu.VMEM((8, width), F32),
            pltpu.VMEM(lists_shape, jnp.int32),
            pltpu.SemaphoreType.DMA(()),
        ],
    )
    blocks = pair_blocks
    field, rounded = call(
        order_kernel,
        (full, half),
        [pltpu.with_memory_space_constraint(value, pltpu.HBM) for value in (right_side, point_order)],
        "curve_order",
        10,
        in_specs=[pl.BlockSpec(memory_space=pltpu.HBM)] * 2,
        scratch_shapes=[
            pltpu.VMEM(right_side.shape, F32),
            pltpu.VMEM(point_order.shape, jnp.int32),
            pltpu.SemaphoreType.DMA((2,)),
        ],
    )
    basis = [field]
    moments = unit = jnp.zeros(scalars.shape, F32)
    ratios = sides = ()
    for index in range(ITERS):
        is_last = index + 1 == ITERS
        rows = [exchange(rounded, "sub", step) for step in range(1, sub_count)]
        begun = call(
            functools.partial(early_kernel, index, sub_count, slot_count),
            (sums,) if index else (sums, scalars),
            (lists, blocks, diag_blocks, noise, field, rounded),
            "early",
            3,
            scratch_shapes=[scratch(extended)],
        )
        if index == 0:
            begun, unit = begun
        else:
            (begun,) = begun
        message = shape(rhs_count, points_dev + LANES, BF16) if index == 1 else half
        even, odd, tile_field, *found = call(
            functools.partial(ahead_kernel, index, sub_count, slot_count),
            (message, message, jax.ShapeDtypeStruct((sub_count * blocks_dev, rhs_count, block_len), F32))
            + ((shape(rhs_count, (sub_count + 1) * LANES, F32),) if index == 1 else ()),
            (lists, blocks, begun, *ratios, rounded, *rows),
            "ahead",
            1,
            scratch_shapes=[scratch(blocks_dev + 1)],
        )
        ratios = ratios or tuple(found)
        even = swap(even, "tile", 0)
        odd = swap(odd, "tile", 1)
        begun = call(
            functools.partial(late_kernel, index, slot_count),
            sums,
            (lists, blocks, begun, tile_field, *ratios),
            "late",
            3,
        )
        if is_last:
            curved = call(
                curvature_kernel,
                scalars,
                (begun, tile_field, even, odd, moments, unit, *ratios, *sides),
                "curvature",
            )
        part = shape(rhs_count, points_dev, F32 if is_last else BF16)
        found = call(
            functools.partial(part_kernel, index, sub_count, slot_count),
            (full,)
            + (part,) * (sub_count - 1)
            + (scalars,)
            + ((full,) * (sub_count - 1) if index + 2 == ITERS else ())
            + ((shape(rhs_count, 2 * LANES, F32),) if index == 1 else ()),
            (lists, blocks, begun, tile_field, even, odd, moments, *ratios, *sides, *(lost if is_last else ())),
            "parts",
            1,
            scratch_shapes=[scratch(extended + 1), scratch(blocks_dev)],
        )
        parts, moments = list(found[:sub_count]), found[sub_count]
        if index == 1:
            sides = (found[-1],)
        lost = found[sub_count + 1 : 2 * sub_count]
        if is_last:
            break
        if index == 0:
            blocks = call(
                turn_kernel,
                pltpu.VMEM((2 * slot_count, block_len, block_len), BF16),
                (pair_blocks, moments),
                "turn",
                4,
                scratch_shapes=[pltpu.SemaphoreType.DMA(())],
            )
        arrived = [exchange(parts[step], "sub", step) for step in range(sub_count - 1, 0, -1)]
        field, rounded, moments = call(
            functools.partial(join_kernel, index),
            (full, half if index else shape(rhs_count, points_dev + LANES, BF16), scalars),
            (blocks, unit, *(ratios or (unit,)), parts[0], field, moments, *arrived),
            "join",
        )
        basis.append(field)
    moments = curved
    arrived = []
    for axis, count in (("sub", sub_count), ("tile", tile_count)):
        step = 1
        while step < count:
            moments = call(add_moments_kernel, scalars, (moments, exchange(moments, axis, step)), "add_moments")
            if len(arrived) < sub_count - 1:
                far = sub_count - 1 - len(arrived)
                arrived.append(exchange(parts[far], "sub", far))
                moments, *parts = lax.optimization_barrier((moments, *parts))
            step *= 2
    for far in range(sub_count - 1 - len(arrived), 0, -1):
        arrived.append(exchange(parts[far], "sub", far))
    return call(
        functools.partial(finish_kernel, sub_count),
        (full, full),
        (moments, unit, *ratios, parts[0], *arrived, *basis),
        "finish",
    )


def solution(mesh):
    placed = (
        P(None, ("tile", "sub")),
        P(("tile", "sub"), None),
        P(("tile", "sub")),
        P(("tile", "sub"), None),
        P(("tile", "sub"), None, None),
        P(("tile", "sub"), None, None),
    )
    return jax.shard_map(
        on_device,
        mesh=mesh,
        in_specs=placed,
        out_specs=(P(None, ("tile", "sub")), P(None, ("tile", "sub"))),
        check_vma=False,
    )
```

```python
import functools

import jax
import jax.numpy as jnp
from jax import lax
from jax.experimental import pallas as pl
from jax.experimental.pallas import tpu as pltpu
from jax.sharding import PartitionSpec as P

ITERS = 3
LANES = 128
LONG_GROUP = 16
SHORT_GROUP = 8
TURN_GROUP = 4
F32 = jnp.float32
BF16 = jnp.bfloat16
VMEM = pl.BlockSpec(memory_space=pltpu.VMEM)
SMEM = pl.BlockSpec(memory_space=pltpu.SMEM)
EARLY, SOON, AHEAD, LATE, FROM_AHEAD = KINDS = range(5)
PARAMS = pltpu.CompilerParams(vmem_limit_bytes=4 * 1024 * 1024)


def times(field, block):
    return lax.dot_general(field, block, (((1,), (0,)), ((), ())), preferred_element_type=F32)


def times_transposed(field, block):
    return lax.dot_general(field, block, (((1,), (1,)), ((), ())), preferred_element_type=F32)


def order_kernel(right_in, order_in, curve_ref, rounded_ref, right_ref, order_ref, sems):
    copies = [
        pltpu.make_async_copy(right_in, right_ref, sems.at[0]),
        pltpu.make_async_copy(order_in, order_ref, sems.at[1]),
    ]
    for copy in copies:
        copy.start()
    for copy in copies:
        copy.wait()
    rhs_count, points = right_ref.shape
    for start in range(0, points, LANES):
        at = jnp.broadcast_to(order_ref[:, start : start + LANES], (rhs_count, LANES))
        chunk = at // LANES
        lane = at % LANES
        result = jnp.zeros((rhs_count, LANES), F32)
        for source in range(points // LANES):
            values = right_ref[:, source * LANES : (source + 1) * LANES]
            picked = jnp.take_along_axis(values, lane, axis=1)
            result = jnp.where(chunk == source, picked, result)
        curve_ref[:, start : start + LANES] = result
        rounded_ref[:, start : start + LANES] = result.astype(BF16)


def device_place(block_len, field_ref, sub_count):
    blocks_dev = field_ref.shape[1] // block_len
    sub_index = lax.axis_index("sub")
    return sub_index, blocks_dev, sub_index * blocks_dev, blocks_dev * sub_count


def list_stride(slot_count):
    return -(-(2 * slot_count + LONG_GROUP) // LANES) * LANES


def lists_kernel(sub_count, blocks_dev, slot_count, pairs_ref, out_ref, padded, lists_ref, sem):
    width = padded.shape[1]
    stride = list_stride(slot_count)
    sub_index = lax.axis_index("sub")
    tile_blocks = blocks_dev * sub_count
    first_block = lax.axis_index("tile") * tile_blocks
    padded[...] = jnp.full(padded.shape, -1.0, F32)
    padded[0:2, 0:slot_count] = pairs_ref[...].astype(F32)
    by_lane = padded[...]
    by_row = jnp.transpose(by_lane)

    def sides(row, col, axis):
        live = jnp.concatenate([row, row], axis) >= 0.0
        row = row.astype(jnp.int32) - first_block
        col = col.astype(jnp.int32) - first_block
        source = jnp.concatenate([row, col], axis)
        target = jnp.concatenate([col, row], axis)
        return live, source, target

    live, source, target = sides(by_row[:, 0:1], by_row[:, 1:2], 0)
    kind = jnp.where(target >= tile_blocks, AHEAD, LATE)
    for index, step in ((EARLY, 0), (SOON, sub_count - 1)):
        first = (sub_index ^ step) * blocks_dev
        kind = jnp.where((source >= first) & (source < first + blocks_dev), index, kind)
    kind = jnp.where(source >= tile_blocks, FROM_AHEAD, kind)
    kind = jnp.where(live, kind, -1)
    hot = (kind == lax.broadcasted_iota(jnp.int32, (2 * width, LANES), 1)).astype(F32)
    below = lax.broadcasted_iota(jnp.int32, (2 * width, 2 * width), 0) > lax.broadcasted_iota(
        jnp.int32, (2 * width, 2 * width), 1
    )
    ranks = times(below.astype(F32).astype(BF16), hot.astype(BF16))
    rank = jnp.sum(ranks * hot, axis=1, keepdims=True).astype(jnp.int32)
    counts = jnp.sum(hot, axis=0, keepdims=True)
    at = jnp.where(live, kind * stride + rank, -1)
    spread = at == lax.broadcasted_iota(jnp.int32, (2 * width, len(KINDS) * stride), 1)
    live, source, target = sides(by_lane[0:1, :], by_lane[1:2, :], 1)
    lane = lax.broadcasted_iota(jnp.int32, (1, 2 * width), 1)
    block = jnp.where(lane < width, lane, lane - width + slot_count)
    fields = jnp.concatenate(
        [jnp.where(live, value, 0).astype(F32) for value in (block, source, target)]
        + [jnp.zeros((5, 2 * width), F32)],
        0,
    )
    found = times(fields.astype(BF16), spread.astype(F32).astype(BF16))
    entries = found[0:1] + 256.0 * found[1:2] + 65536.0 * found[2:3]
    entries = entries.astype(jnp.int32)
    idle = (tile_blocks + blocks_dev) * 65536
    idle_source = {
        EARLY: sub_index * blocks_dev,
        SOON: (sub_index ^ (sub_count - 1)) * blocks_dev,
        AHEAD: tile_blocks - blocks_dev,
        LATE: 0,
        FROM_AHEAD: tile_blocks,
    }
    place = lax.broadcasted_iota(jnp.int32, (1, stride), 1)
    for index in KINDS:
        span = slice(index * stride, (index + 1) * stride)
        count = counts[:, index : index + 1].astype(jnp.int32)
        lists_ref[:, span] = jnp.where(place < count, entries[:, span], idle + 256 * idle_source[index])
    lists_ref[:, len(KINDS) * stride : len(KINDS) * stride + LANES] = counts.astype(jnp.int32)
    by_column = jnp.sum(hot[:width], axis=0, keepdims=True)
    lists_ref[:, len(KINDS) * stride + LANES :] = by_column.astype(jnp.int32)
    copy = pltpu.make_async_copy(lists_ref, out_ref, sem)
    copy.start()
    copy.wait()


def turn_kernel(pairs_blocks_ref, after_ref, blocks_ref, sem):
    slot_count = pairs_blocks_ref.shape[0]
    copy = pltpu.make_async_copy(pairs_blocks_ref, blocks_ref.at[pl.ds(0, slot_count)], sem)
    copy.start()

    def one_group(group, carry):
        for step in range(TURN_GROUP):
            slot = group * TURN_GROUP + step
            blocks_ref[slot_count + slot] = jnp.transpose(pairs_blocks_ref[slot])
        return carry

    lax.fori_loop(0, slot_count // TURN_GROUP, one_group, 0)
    copy.wait()


def add_products(lists_ref, blocks_ref, slot_count, field, total, index, size, source_from=0, target_from=0):
    stride = list_stride(slot_count)
    idle = lists_ref[0, index * stride + stride - 1] >> 16
    count = lists_ref[0, len(KINDS) * stride + index]
    column_count = lists_ref[0, len(KINDS) * stride + LANES + index]

    def add_part(first, end, kind, plain, cuts):
        def one_group(group, carry):
            results = []
            for step in range(size):
                place = first + group * size + step
                entry = lists_ref[0, index * stride + place]
                block, source, target = entry & 255, (entry >> 8) & 255, entry >> 16
                if plain:
                    block = jnp.where(block >= slot_count, block - slot_count, block)
                if cuts:
                    target = jnp.where(place < end, target, idle)
                value = kind(field[source - source_from].astype(BF16), blocks_ref[block])
                results.append((target - target_from, value))
            for at, value in results:
                total[at] += value
            return carry

        lax.fori_loop(0, (end - first + size - 1) // size, one_group, 0)

    if blocks_ref.shape[0] > slot_count:
        add_part(0, count, times, False, False)
    else:
        add_part(0, column_count, times, True, True)
        add_part(column_count, count, times_transposed, True, False)


def raised(value, exponent):
    result = value
    for _ in range(exponent - 1):
        result = result * value
    return result


def widen(tile, columns):
    return jnp.concatenate([tile] * (columns // LANES), axis=1)


def lay_out(row_ref, field, first, blocks_dev, block_len, factor=None):
    for block in range(blocks_dev):
        piece = row_ref[:, block * block_len : (block + 1) * block_len].astype(F32)
        field[first + block] = piece if factor is None else piece * factor


def early_kernel(
    index, sub_count, slot_count, lists_ref, blocks_ref, diag_ref, noise_ref, own_ref, rounded_ref, total,
    *refs
):
    field = refs[-1]
    block_len = blocks_ref.shape[1]
    sub_index, blocks_dev, own_first, _ = device_place(block_len, own_ref, sub_count)
    if index == 0:
        largest = diag_ref[0].astype(F32)
        for block in range(1, blocks_dev):
            largest = jnp.maximum(largest, diag_ref[block].astype(F32))
        refs[0][...] = jnp.full(refs[0].shape, jnp.maximum(jnp.max(largest) * block_len, 1.0))
    lay_out(rounded_ref, field, own_first, blocks_dev, block_len)
    for block in range(total.shape[0]):
        total[block] = jnp.zeros(total.shape[1:], F32)
    for block in range(blocks_dev):
        span = slice(block * block_len, (block + 1) * block_len)
        value = noise_ref[:, span] * own_ref[:, span]
        total[own_first + block] = value + times(field[own_first + block].astype(BF16), diag_ref[block])
    add_products(lists_ref, blocks_ref, slot_count, field, total, EARLY, LONG_GROUP)


def soon_kernel(index, sub_count, slot_count, blocks_dev, lists_ref, blocks_ref, begun_ref, row_ref, total, field):
    lay_out(row_ref, field, (lax.axis_index("sub") ^ (sub_count - 1)) * blocks_dev, blocks_dev, blocks_ref.shape[1])
    total[...] = begun_ref[...]
    add_products(lists_ref, blocks_ref, slot_count, field, total, SOON, LONG_GROUP)


def ahead_kernel(index, sub_count, slot_count, lists_ref, blocks_ref, begun_ref, *refs):
    if index == 1:
        *refs, ratios_ref, total = refs
        row_refs, (even_ref, odd_ref, field_ref) = refs[:-3], refs[-3:]
        points_dev = even_ref.shape[1] - LANES
        units = [row_ref[:, points_dev:].astype(F32) for row_ref in row_refs]
        tile_unit = functools.reduce(jnp.maximum, units)
        ratios = [unit / tile_unit for unit in units]
        ratios_ref[...] = jnp.concatenate(ratios + [tile_unit], axis=1)
    else:
        row_refs, (even_ref, odd_ref, field_ref, total) = refs[:-4], refs[-4:]
        points_dev = even_ref.shape[1]
        if index:
            ratios_ref, *row_refs = row_refs
            ratios = [ratios_ref[:, step * LANES : (step + 1) * LANES] for step in range(sub_count)]
    block_len = blocks_ref.shape[1]
    blocks_dev = points_dev // block_len
    tile_blocks = blocks_dev * sub_count
    sub_index = lax.axis_index("sub")
    for step, row_ref in enumerate(row_refs):
        factor = widen(raised(ratios[step], index), block_len) if index else None
        lay_out(row_ref, field_ref, (sub_index ^ step) * blocks_dev, blocks_dev, block_len, factor)
    for block in range(blocks_dev):
        value = begun_ref[tile_blocks + block]
        total[block] = value * widen(raised(ratios[0], index), block_len) if index else value
    total[blocks_dev] = jnp.zeros(total.shape[1:], F32)
    add_products(lists_ref, blocks_ref, slot_count, field_ref, total, AHEAD, SHORT_GROUP, 0, tile_blocks)
    is_odd = lax.axis_index("tile") % 2 == 1
    for block in range(blocks_dev):
        span = slice(block * block_len, (block + 1) * block_len)
        products = total[block]
        first_row = field_ref[block]
        even_ref[:, span] = jnp.where(is_odd, first_row, products).astype(BF16)
        odd_ref[:, span] = jnp.where(is_odd, products, first_row).astype(BF16)
    if index == 1:
        even_ref[:, points_dev:] = tile_unit.astype(BF16)
        odd_ref[:, points_dev:] = tile_unit.astype(BF16)


def late_kernel(index, slot_count, lists_ref, blocks_ref, begun_ref, field_ref, *refs):
    total = refs[-1]
    if index:
        factor = widen(raised(refs[0][:, :LANES], index), total.shape[2])
        for block in range(total.shape[0]):
            total[block] = begun_ref[block] * factor
    else:
        total[...] = begun_ref[...]
    add_products(lists_ref, blocks_ref, slot_count, field_ref, total, LATE, LONG_GROUP)


def neighbours(is_odd, even, odd):
    return jnp.where(is_odd, even, odd), jnp.where(is_odd, odd, even)


def curvature_kernel(
    begun_ref, field_ref, even_ref, odd_ref, moments_in_ref, unit_ref, ratios_ref, sides_ref, moments_ref
):
    index = ITERS - 1
    block_len = begun_ref.shape[2]
    blocks_dev = even_ref.shape[1] // block_len
    is_odd = lax.axis_index("tile") % 2 == 1
    unit = unit_ref[...]
    scale = widen(1.0 / (raised(ratios_ref[:, :LANES], 2 * index) * unit), block_len)
    before = widen(2.0 * raised(sides_ref[:, :LANES], index), block_len)
    product = jnp.zeros(begun_ref.shape[1:], F32)
    for block in range(field_ref.shape[0]):
        value = begun_ref[block]
        if block < blocks_dev:
            span = slice(block * block_len, (block + 1) * block_len)
            arrived, _ = neighbours(is_odd, even_ref[:, span].astype(F32), odd_ref[:, span].astype(F32))
            value += arrived * before
        product += field_ref[block] * (value * scale)
    last = jnp.sum(product, axis=1, keepdims=True)
    moments = moments_in_ref[...]
    lane = lax.broadcasted_iota(jnp.int32, moments.shape, 1)
    moments = jnp.where(lane == 2 * ITERS - 1, last, moments)
    moments_ref[...] = jnp.where(lane == 2 * ITERS, unit, moments)


def lost_weight(moments):
    inner = [moments[:, order : order + 1] for order in range(4)]
    first = inner[1] / inner[0]
    norm = inner[2] - first * inner[1]
    second = (inner[3] - 2.0 * first * inner[2] + first * first * inner[1]) / norm
    trace = first + 2.0 * second
    return jnp.where((norm > 0.0) & (trace > 0.0) & (trace < 30.0), -trace, 0.0)


def part_kernel(
    index, sub_count, slot_count, lists_ref, blocks_ref, begun_ref, field_ref, even_ref, odd_ref,
    moments_in_ref, *refs
):
    *refs, total, ahead = refs
    if index == 1:
        ratios_ref, *refs, sides_ref = refs
    elif index:
        ratios_ref, sides_ref, *refs = refs
    if index + 1 == ITERS:
        lost_refs, refs = refs[: sub_count - 1], refs[sub_count - 1 :]
    part_refs, moments_ref, *kept_refs = refs[:sub_count], *refs[sub_count:]
    block_len = blocks_ref.shape[1]
    sub_index, blocks_dev, own_first, tile_blocks = device_place(block_len, part_refs[0], sub_count)
    is_odd = lax.axis_index("tile") % 2 == 1
    if index == 1:
        points_dev = blocks_dev * block_len
        even = even_ref[:, points_dev:].astype(F32)
        odd = odd_ref[:, points_dev:].astype(F32)
        tile_unit = ratios_ref[:, sub_count * LANES :]
        sides = [side / tile_unit for side in neighbours(is_odd, even, odd)]
        sides_ref[...] = jnp.concatenate(sides, axis=1)
    elif index:
        sides = [sides_ref[:, :LANES], sides_ref[:, LANES:]]
    if index:
        before, after = [widen(raised(side, index), block_len) for side in sides]
    for block in range(blocks_dev):
        span = slice(block * block_len, (block + 1) * block_len)
        even = even_ref[:, span].astype(F32)
        odd = odd_ref[:, span].astype(F32)
        products, first_row = neighbours(is_odd, even, odd)
        ahead[block] = first_row * after if index else first_row
        total[block] = begun_ref[block] + (products * before if index else products)
    for block in range(blocks_dev, tile_blocks):
        total[block] = begun_ref[block]
    total[begun_ref.shape[0] - 1] = jnp.zeros(total.shape[1:], F32)
    add_products(lists_ref, blocks_ref, slot_count, ahead, total, FROM_AHEAD, SHORT_GROUP, tile_blocks, 0)
    moments = moments_in_ref[...]
    if index + 1 == ITERS:
        weight = lost_weight(moments) * ratios_ref[:, :1]
    for step in range(sub_count):
        first = (sub_index ^ step) * blocks_dev
        for block in range(blocks_dev):
            span = slice(block * block_len, (block + 1) * block_len)
            value = total[first + block]
            if step and index + 1 == ITERS:
                value += weight * lost_refs[step - 1][:, span]
            rounded = value.astype(part_refs[step].dtype)
            part_refs[step][:, span] = rounded
            if step and kept_refs:
                kept_refs[step - 1][:, span] = value - rounded.astype(F32)
    moments_ref[...] = moments


def join_kernel(index, after_ref, unit_ref, ratios_ref, own_ref, old_ref, moments_in_ref, *refs):
    part_refs = refs[:-3]
    next_ref, rounded_ref, moments_ref = refs[-3:]
    points_dev = own_ref.shape[1]
    value = own_ref[...]
    for part_ref in part_refs:
        value += part_ref[...].astype(F32)
    unit = unit_ref[...]
    divisor = raised(ratios_ref[:, :LANES], index) * unit if index else unit
    value = value * widen(1.0 / divisor, points_dev)
    next_ref[...] = value
    rounded_ref[:, :points_dev] = value.astype(BF16)
    if index == 0:
        rounded_ref[:, points_dev:] = unit.astype(BF16)
    old = old_ref[...]
    lane = lax.broadcasted_iota(jnp.int32, moments_ref.shape, 1)
    moments = moments_in_ref[...] if index else jnp.zeros(moments_ref.shape, F32)
    found = {2 * index + 1: old * value, 2 * index + 2: value * value}
    if index == 0:
        found[0] = old * old
    for order, product in found.items():
        moments = jnp.where(lane == order, jnp.sum(product, axis=1, keepdims=True), moments)
    moments_ref[...] = moments


def add_moments_kernel(first_ref, second_ref, sum_ref):
    unit_lane = 2 * ITERS
    lane = lax.broadcasted_iota(jnp.int32, sum_ref.shape, 1)
    units = [ref[:, unit_lane : unit_lane + 1] for ref in (first_ref, second_ref)]
    larger = jnp.maximum(units[0], units[1])
    result = jnp.zeros(sum_ref.shape, F32)
    for ref, unit in zip((first_ref, second_ref), units):
        ratio = unit / larger
        value = ref[...]
        for order in range(1, unit_lane):
            value = jnp.where(lane >= order, value * ratio, value)
        result += value
    sum_ref[...] = jnp.where(lane == unit_lane, larger, result)


def finish_kernel(sub_count, moments_ref, unit_ref, ratios_ref, *refs):
    part_refs, basis_refs = refs[:sub_count], refs[sub_count:-2]
    solution_ref, residual_ref = refs[-2:]
    moments = [moments_ref[:, order : order + 1] for order in range(2 * ITERS)]
    largest = moments_ref[:, 2 * ITERS : 2 * ITERS + 1]
    unit = unit_ref[:, :1]
    ratio = unit / largest

    def inner(first, second, shift):
        value = 0.0
        for i, a in enumerate(first):
            for j, b in enumerate(second):
                value = value + a * b * moments[i + j + shift]
        return value

    one = jnp.ones_like(moments[0])
    zero = jnp.zeros_like(one)
    direction, residual = [one], [one]
    answer = [zero] * ITERS
    norm_now = moments[0]
    for iteration in range(ITERS):
        step_size = norm_now / inner(direction, direction, 1)
        for power, weight in enumerate(direction):
            answer[power] = answer[power] + step_size * weight
        residual = residual + [zero]
        for power, weight in enumerate(direction):
            residual[power + 1] = residual[power + 1] - step_size * weight
        if iteration + 1 < ITERS:
            norm_next = inner(residual, residual, 0)
            direction = [
                value + (norm_next / norm_now) * old
                for value, old in zip(residual, direction + [zero])
            ]
            norm_now = norm_next
    fields = [basis_ref[...] for basis_ref in basis_refs]
    fields.append(sum(part_ref[...].astype(F32) for part_ref in part_refs))
    for order in range(1, ITERS + 1):
        scale = raised(ratio, order)
        if order < ITERS:
            answer[order] = answer[order] * scale
        else:
            scale = scale / (raised(ratios_ref[:, :1], ITERS - 1) * unit)
        residual[order] = residual[order] * scale
    answer = [weight / largest for weight in answer]
    solution_ref[...] = sum(weight * field for weight, field in zip(answer, fields))
    residual_ref[...] = sum(weight * field for weight, field in zip(residual, fields))


def shape(rows, columns, kind):
    return jax.ShapeDtypeStruct((rows, columns), kind)


def exchange(block, axis, step):
    count = lax.axis_size(axis)
    return lax.ppermute(block, axis, [(i, i ^ step) for i in range(count)])


def swap(block, axis, first):
    count = lax.axis_size(axis)
    route = []
    for i in range(first, count - 1, 2):
        route += [(i, i + 1), (i + 1, i)]
    return lax.ppermute(block, axis, route)


def call(kernel, outs, ins, name, cost=0, **options):
    single = not isinstance(outs, tuple)
    specs = [SMEM if value.dtype == jnp.int32 else VMEM for value in ins]
    options.setdefault("in_specs", specs)
    options.setdefault("out_specs", VMEM if single else (VMEM,) * len(outs))
    return pl.pallas_call(
        kernel,
        out_shape=outs,
        compiler_params=PARAMS,
        name=name,
        cost_estimate=pl.CostEstimate(flops=int(cost * 1e9), bytes_accessed=0, transcendentals=0),
        **options,
    )(*ins)


def on_device(right_side, point_order, noise_var, block_pairs, pair_blocks, diag_blocks):
    sub_count = lax.axis_size("sub")
    tile_count = lax.axis_size("tile")
    rhs_count, points_dev = right_side.shape
    blocks_dev, block_len = diag_blocks.shape[:2]
    extended = (sub_count + 1) * blocks_dev
    noise = noise_var[None, :]
    full = shape(rhs_count, points_dev, F32)
    half = shape(rhs_count, points_dev, BF16)
    scalars = shape(rhs_count, LANES, F32)
    sums = jax.ShapeDtypeStruct((extended + 1, rhs_count, block_len), F32)

    def scratch(blocks):
        return pltpu.VMEM((blocks, rhs_count, block_len), F32)

    slot_count = pair_blocks.shape[0]
    width = -(-slot_count // LANES) * LANES
    assert 2 * width <= 256 and extended < 256 and slot_count % TURN_GROUP == 0
    lists_shape = (1, len(KINDS) * list_stride(slot_count) + 2 * LANES)
    lists = call(
        functools.partial(lists_kernel, sub_count, blocks_dev, slot_count),
        pltpu.SMEM(lists_shape, jnp.int32),
        (block_pairs.T,),
        "lists",
        1,
        in_specs=[VMEM],
        out_specs=SMEM,
        scratch_shapes=[
            pltpu.VMEM((8, width), F32),
            pltpu.VMEM(lists_shape, jnp.int32),
            pltpu.SemaphoreType.DMA(()),
        ],
    )
    blocks = pair_blocks
    field, rounded = call(
        order_kernel,
        (full, half),
        [pltpu.with_memory_space_constraint(value, pltpu.HBM) for value in (right_side, point_order)],
        "curve_order",
        10,
        in_specs=[pl.BlockSpec(memory_space=pltpu.HBM)] * 2,
        scratch_shapes=[
            pltpu.VMEM(right_side.shape, F32),
            pltpu.VMEM(point_order.shape, jnp.int32),
            pltpu.SemaphoreType.DMA((2,)),
        ],
    )
    basis = [field]
    moments = unit = jnp.zeros(scalars.shape, F32)
    ratios = sides = ()
    for index in range(ITERS):
        is_last = index + 1 == ITERS
        rows = [exchange(rounded, "sub", step) for step in range(1, sub_count)]
        begun = call(
            functools.partial(early_kernel, index, sub_count, slot_count),
            (sums,) if index else (sums, scalars),
            (lists, blocks, diag_blocks, noise, field, rounded),
            "early",
            0.1,
            scratch_shapes=[scratch(extended)],
        )
        if index == 0:
            begun, unit = begun
        else:
            (begun,) = begun
        begun = call(
            functools.partial(soon_kernel, index, sub_count, slot_count, blocks_dev),
            sums,
            (lists, blocks, begun, rows[-1]),
            "soon",
            3,
            scratch_shapes=[scratch(extended)],
        )
        message = shape(rhs_count, points_dev + LANES, BF16) if index == 1 else half
        even, odd, tile_field, *found = call(
            functools.partial(ahead_kernel, index, sub_count, slot_count),
            (message, message, jax.ShapeDtypeStruct((sub_count * blocks_dev, rhs_count, block_len), F32))
            + ((shape(rhs_count, (sub_count + 1) * LANES, F32),) if index == 1 else ()),
            (lists, blocks, begun, *ratios, rounded, *rows),
            "ahead",
            1,
            scratch_shapes=[scratch(blocks_dev + 1)],
        )
        ratios = ratios or tuple(found)
        even = swap(even, "tile", 0)
        odd = swap(odd, "tile", 1)
        begun = call(
            functools.partial(late_kernel, index, slot_count),
            sums,
            (lists, blocks, begun, tile_field, *ratios),
            "late",
            3,
        )
        if is_last:
            curved = call(
                curvature_kernel,
                scalars,
                (begun, tile_field, even, odd, moments, unit, *ratios, *sides),
                "curvature",
            )
        part = shape(rhs_count, points_dev, F32 if is_last else BF16)
        found = call(
            functools.partial(part_kernel, index, sub_count, slot_count),
            (full,)
            + (part,) * (sub_count - 1)
            + (scalars,)
            + ((full,) * (sub_count - 1) if index + 2 == ITERS else ())
            + ((shape(rhs_count, 2 * LANES, F32),) if index == 1 else ()),
            (lists, blocks, begun, tile_field, even, odd, moments, *ratios, *sides, *(lost if is_last else ())),
            "parts",
            1,
            scratch_shapes=[scratch(extended + 1), scratch(blocks_dev)],
        )
        parts, moments = list(found[:sub_count]), found[sub_count]
        if index == 1:
            sides = (found[-1],)
        lost = found[sub_count + 1 : 2 * sub_count]
        if is_last:
            break
        if index == 0:
            blocks = call(
                turn_kernel,
                pltpu.VMEM((2 * slot_count, block_len, block_len), BF16),
                (pair_blocks, moments),
                "turn",
                4,
                scratch_shapes=[pltpu.SemaphoreType.DMA(())],
            )
        arrived = [exchange(parts[step], "sub", step) for step in range(sub_count - 1, 0, -1)]
        field, rounded, moments = call(
            functools.partial(join_kernel, index),
            (full, half if index else shape(rhs_count, points_dev + LANES, BF16), scalars),
            (blocks, unit, *(ratios or (unit,)), parts[0], field, moments, *arrived),
            "join",
        )
        basis.append(field)
    moments = curved
    arrived = []
    for axis, count in (("sub", sub_count), ("tile", tile_count)):
        step = 1
        while step < count:
            moments = call(add_moments_kernel, scalars, (moments, exchange(moments, axis, step)), "add_moments")
            if len(arrived) < sub_count - 1:
                far = sub_count - 1 - len(arrived)
                arrived.append(exchange(parts[far], "sub", far))
                moments, *parts = lax.optimization_barrier((moments, *parts))
            step *= 2
    for far in range(sub_count - 1 - len(arrived), 0, -1):
        arrived.append(exchange(parts[far], "sub", far))
    return call(
        functools.partial(finish_kernel, sub_count),
        (full, full),
        (moments, unit, *ratios, parts[0], *arrived, *basis),
        "finish",
    )


def solution(mesh):
    placed = (
        P(None, ("tile", "sub")),
        P(("tile", "sub"), None),
        P(("tile", "sub")),
        P(("tile", "sub"), None),
        P(("tile", "sub"), None, None),
        P(("tile", "sub"), None, None),
    )
    return jax.shard_map(
        on_device,
        mesh=mesh,
        in_specs=placed,
        out_specs=(P(None, ("tile", "sub")), P(None, ("tile", "sub"))),
        check_vma=False,
    )
```

```python
import functools

import jax
import jax.numpy as jnp
from jax import lax
from jax.experimental import pallas as pl
from jax.experimental.pallas import tpu as pltpu
from jax.sharding import PartitionSpec as P

ITERS = 3
LANES = 128
LONG_GROUP = 16
SHORT_GROUP = 8
TURN_GROUP = 24
TURN_PRODUCTS = 6
F32 = jnp.float32
BF16 = jnp.bfloat16
VMEM = pl.BlockSpec(memory_space=pltpu.VMEM)
SMEM = pl.BlockSpec(memory_space=pltpu.SMEM)
EARLY, AHEAD, LATE, FROM_AHEAD = KINDS = range(4)
PARAMS = pltpu.CompilerParams(vmem_limit_bytes=4 * 1024 * 1024)


def times(field, block):
    return lax.dot_general(field, block, (((1,), (0,)), ((), ())), preferred_element_type=F32)


def times_transposed(field, block):
    return lax.dot_general(field, block, (((1,), (1,)), ((), ())), preferred_element_type=F32)


def order_kernel(right_in, order_in, curve_ref, rounded_ref, right_ref, order_ref, sems):
    copies = [
        pltpu.make_async_copy(right_in, right_ref, sems.at[0]),
        pltpu.make_async_copy(order_in, order_ref, sems.at[1]),
    ]
    for copy in copies:
        copy.start()
    for copy in copies:
        copy.wait()
    rhs_count, points = right_ref.shape
    for start in range(0, points, LANES):
        at = jnp.broadcast_to(order_ref[:, start : start + LANES], (rhs_count, LANES))
        chunk = at // LANES
        lane = at % LANES
        result = jnp.zeros((rhs_count, LANES), F32)
        for source in range(points // LANES):
            values = right_ref[:, source * LANES : (source + 1) * LANES]
            picked = jnp.take_along_axis(values, lane, axis=1)
            result = jnp.where(chunk == source, picked, result)
        curve_ref[:, start : start + LANES] = result
        rounded_ref[:, start : start + LANES] = result.astype(BF16)


def device_place(block_len, field_ref, sub_count):
    blocks_dev = field_ref.shape[1] // block_len
    sub_index = lax.axis_index("sub")
    return sub_index, blocks_dev, sub_index * blocks_dev, blocks_dev * sub_count


def list_stride(slot_count):
    return -(-(2 * slot_count + LONG_GROUP) // LANES) * LANES


def lists_kernel(sub_count, blocks_dev, slot_count, pairs_ref, out_ref, padded, lists_ref, sem):
    width = padded.shape[1]
    stride = list_stride(slot_count)
    sub_index = lax.axis_index("sub")
    tile_blocks = blocks_dev * sub_count
    first_block = lax.axis_index("tile") * tile_blocks
    padded[...] = jnp.full(padded.shape, -1.0, F32)
    padded[0:2, 0:slot_count] = pairs_ref[...].astype(F32)
    by_lane = padded[...]
    by_row = jnp.transpose(by_lane)

    def sides(row, col, axis):
        live = jnp.concatenate([row, row], axis) >= 0.0
        row = row.astype(jnp.int32) - first_block
        col = col.astype(jnp.int32) - first_block
        source = jnp.concatenate([row, col], axis)
        target = jnp.concatenate([col, row], axis)
        return live, source, target

    live, source, target = sides(by_row[:, 0:1], by_row[:, 1:2], 0)
    kind = jnp.where(target >= tile_blocks, AHEAD, LATE)
    first_own = sub_index * blocks_dev
    is_early = (source >= first_own) & (source < first_own + blocks_dev)
    kind = jnp.where(is_early, EARLY, kind)
    kind = jnp.where(source >= tile_blocks, FROM_AHEAD, kind)
    kind = jnp.where(live, kind, -1)
    hot = (kind == lax.broadcasted_iota(jnp.int32, (2 * width, LANES), 1)).astype(F32)
    below = lax.broadcasted_iota(jnp.int32, (2 * width, 2 * width), 0) > lax.broadcasted_iota(
        jnp.int32, (2 * width, 2 * width), 1
    )
    ranks = times(below.astype(F32).astype(BF16), hot.astype(BF16))
    rank = jnp.sum(ranks * hot, axis=1, keepdims=True).astype(jnp.int32)
    counts = jnp.sum(hot, axis=0, keepdims=True)
    at = jnp.where(live, kind * stride + rank, -1)
    spread = at == lax.broadcasted_iota(jnp.int32, (2 * width, len(KINDS) * stride), 1)
    live, source, target = sides(by_lane[0:1, :], by_lane[1:2, :], 1)
    lane = lax.broadcasted_iota(jnp.int32, (1, 2 * width), 1)
    block = jnp.where(lane < width, lane, lane - width + slot_count)
    fields = jnp.concatenate(
        [jnp.where(live, value, 0).astype(F32) for value in (block, source, target)]
        + [jnp.zeros((5, 2 * width), F32)],
        0,
    )
    found = times(fields.astype(BF16), spread.astype(F32).astype(BF16))
    entries = found[0:1] + 256.0 * found[1:2] + 65536.0 * found[2:3]
    entries = entries.astype(jnp.int32)
    idle = (tile_blocks + blocks_dev) * 65536
    idle_source = {
        EARLY: sub_index * blocks_dev,
        AHEAD: tile_blocks - blocks_dev,
        LATE: 0,
        FROM_AHEAD: tile_blocks,
    }
    place = lax.broadcasted_iota(jnp.int32, (1, stride), 1)
    for index in KINDS:
        span = slice(index * stride, (index + 1) * stride)
        count = counts[:, index : index + 1].astype(jnp.int32)
        lists_ref[:, span] = jnp.where(place < count, entries[:, span], idle + 256 * idle_source[index])
    lists_ref[:, len(KINDS) * stride : len(KINDS) * stride + LANES] = counts.astype(jnp.int32)
    by_column = jnp.sum(hot[:width], axis=0, keepdims=True)
    lists_ref[:, len(KINDS) * stride + LANES :] = by_column.astype(jnp.int32)
    copy = pltpu.make_async_copy(lists_ref, out_ref, sem)
    copy.start()
    copy.wait()


def turn_kernel(pairs_blocks_ref, after_ref, blocks_ref, sem):
    slot_count = pairs_blocks_ref.shape[0]
    copy = pltpu.make_async_copy(pairs_blocks_ref, blocks_ref.at[pl.ds(0, slot_count)], sem)
    copy.start()

    square = blocks_ref.shape[1:]
    identity = lax.broadcasted_iota(jnp.int32, square, 0) == lax.broadcasted_iota(jnp.int32, square, 1)
    identity = identity.astype(F32).astype(BF16)

    def one_group(group, carry):
        for step in range(TURN_GROUP):
            slot = group * TURN_GROUP + step
            block = pairs_blocks_ref[slot]
            if step < TURN_GROUP - TURN_PRODUCTS:
                turned = jnp.transpose(block)
            else:
                turned = times_transposed(identity, block).astype(BF16)
            blocks_ref[slot_count + slot] = turned
        return carry

    lax.fori_loop(0, slot_count // TURN_GROUP, one_group, 0)
    copy.wait()


def add_products(lists_ref, blocks_ref, slot_count, field, total, index, size, source_from=0, target_from=0):
    stride = list_stride(slot_count)
    idle = lists_ref[0, index * stride + stride - 1] >> 16
    count = lists_ref[0, len(KINDS) * stride + index]
    column_count = lists_ref[0, len(KINDS) * stride + LANES + index]

    def add_part(first, end, kind, plain, cuts):
        def one_group(group, carry):
            results = []
            for step in range(size):
                place = first + group * size + step
                entry = lists_ref[0, index * stride + place]
                block, source, target = entry & 255, (entry >> 8) & 255, entry >> 16
                if plain:
                    block = jnp.where(block >= slot_count, block - slot_count, block)
                if cuts:
                    target = jnp.where(place < end, target, idle)
                value = kind(field[source - source_from].astype(BF16), blocks_ref[block])
                results.append((target - target_from, value))
            for at, value in results:
                total[at] += value
            return carry

        lax.fori_loop(0, (end - first + size - 1) // size, one_group, 0)

    if blocks_ref.shape[0] > slot_count:
        add_part(0, count, times, False, False)
    else:
        add_part(0, column_count, times, True, True)
        add_part(column_count, count, times_transposed, True, False)


def raised(value, exponent):
    result = value
    for _ in range(exponent - 1):
        result = result * value
    return result


def widen(tile, columns):
    return jnp.concatenate([tile] * (columns // LANES), axis=1)


def lay_out(row_ref, field, first, blocks_dev, block_len, factor=None):
    for block in range(blocks_dev):
        piece = row_ref[:, block * block_len : (block + 1) * block_len].astype(F32)
        field[first + block] = piece if factor is None else piece * factor


def own_products(diag_ref, noise_ref, own_ref, rounded, block):
    block_len = diag_ref.shape[1]
    span = slice(block * block_len, (block + 1) * block_len)
    return noise_ref[:, span] * own_ref[:, span] + times(rounded, diag_ref[block])


def early_kernel(index, sub_count, slot_count, lists_ref, blocks_ref, *refs):
    *refs, rounded_ref, total, field = refs
    block_len = blocks_ref.shape[1]
    blocks_dev = rounded_ref.shape[1] // block_len
    own_first = lax.axis_index("sub") * blocks_dev
    lay_out(rounded_ref, field, own_first, blocks_dev, block_len)
    for block in range(total.shape[0]):
        total[block] = jnp.zeros(total.shape[1:], F32)
    if index:
        for block in range(blocks_dev):
            total[own_first + block] = own_products(*refs, field[own_first + block].astype(BF16), block)
    add_products(lists_ref, blocks_ref, slot_count, field, total, EARLY, LONG_GROUP)


def own_kernel(after_ref, diag_ref, noise_ref, own_ref, rounded_ref, sum_ref, unit_ref):
    blocks_dev, block_len = diag_ref.shape[:2]
    largest = diag_ref[0].astype(F32)
    for block in range(1, blocks_dev):
        largest = jnp.maximum(largest, diag_ref[block].astype(F32))
    unit_ref[...] = jnp.full(unit_ref.shape, jnp.maximum(jnp.max(largest) * block_len, 1.0))
    for block in range(blocks_dev):
        span = slice(block * block_len, (block + 1) * block_len)
        sum_ref[:, span] = own_products(diag_ref, noise_ref, own_ref, rounded_ref[:, span], block)


def ahead_kernel(index, sub_count, slot_count, lists_ref, blocks_ref, begun_ref, *refs):
    if index == 1:
        *refs, ratios_ref, total = refs
        row_refs, (even_ref, odd_ref, field_ref) = refs[:-3], refs[-3:]
        points_dev = even_ref.shape[1] - LANES
        units = [row_ref[:, points_dev:].astype(F32) for row_ref in row_refs]
        tile_unit = functools.reduce(jnp.maximum, units)
        ratios = [unit / tile_unit for unit in units]
        ratios_ref[...] = jnp.concatenate(ratios + [tile_unit], axis=1)
    else:
        row_refs, (even_ref, odd_ref, field_ref, total) = refs[:-4], refs[-4:]
        points_dev = even_ref.shape[1]
        if index:
            ratios_ref, *row_refs = row_refs
            ratios = [ratios_ref[:, step * LANES : (step + 1) * LANES] for step in range(sub_count)]
    block_len = blocks_ref.shape[1]
    blocks_dev = points_dev // block_len
    tile_blocks = blocks_dev * sub_count
    sub_index = lax.axis_index("sub")
    for step, row_ref in enumerate(row_refs):
        factor = widen(raised(ratios[step], index), block_len) if index else None
        lay_out(row_ref, field_ref, (sub_index ^ step) * blocks_dev, blocks_dev, block_len, factor)
    for block in range(blocks_dev):
        value = begun_ref[tile_blocks + block]
        total[block] = value * widen(raised(ratios[0], index), block_len) if index else value
    total[blocks_dev] = jnp.zeros(total.shape[1:], F32)
    add_products(lists_ref, blocks_ref, slot_count, field_ref, total, AHEAD, SHORT_GROUP, 0, tile_blocks)
    is_odd = lax.axis_index("tile") % 2 == 1
    for block in range(blocks_dev):
        span = slice(block * block_len, (block + 1) * block_len)
        products = total[block]
        first_row = field_ref[block]
        even_ref[:, span] = jnp.where(is_odd, first_row, products).astype(BF16)
        odd_ref[:, span] = jnp.where(is_odd, products, first_row).astype(BF16)
    if index == 1:
        even_ref[:, points_dev:] = tile_unit.astype(BF16)
        odd_ref[:, points_dev:] = tile_unit.astype(BF16)


def late_kernel(index, slot_count, lists_ref, blocks_ref, begun_ref, field_ref, *refs):
    total = refs[-1]
    if index:
        factor = widen(raised(refs[0][:, :LANES], index), total.shape[2])
        for block in range(total.shape[0]):
            total[block] = begun_ref[block] * factor
    else:
        total[...] = begun_ref[...]
    add_products(lists_ref, blocks_ref, slot_count, field_ref, total, LATE, LONG_GROUP)


def neighbours(is_odd, even, odd):
    return jnp.where(is_odd, even, odd), jnp.where(is_odd, odd, even)


def curvature_kernel(
    begun_ref, field_ref, even_ref, odd_ref, moments_in_ref, unit_ref, ratios_ref, sides_ref, moments_ref
):
    index = ITERS - 1
    block_len = begun_ref.shape[2]
    blocks_dev = even_ref.shape[1] // block_len
    is_odd = lax.axis_index("tile") % 2 == 1
    unit = unit_ref[...]
    scale = widen(1.0 / (raised(ratios_ref[:, :LANES], 2 * index) * unit), block_len)
    before = widen(2.0 * raised(sides_ref[:, :LANES], index), block_len)
    product = jnp.zeros(begun_ref.shape[1:], F32)
    for block in range(field_ref.shape[0]):
        value = begun_ref[block]
        if block < blocks_dev:
            span = slice(block * block_len, (block + 1) * block_len)
            arrived, _ = neighbours(is_odd, even_ref[:, span].astype(F32), odd_ref[:, span].astype(F32))
            value += arrived * before
        product += field_ref[block] * (value * scale)
    last = jnp.sum(product, axis=1, keepdims=True)
    moments = moments_in_ref[...]
    lane = lax.broadcasted_iota(jnp.int32, moments.shape, 1)
    moments = jnp.where(lane == 2 * ITERS - 1, last, moments)
    moments_ref[...] = jnp.where(lane == 2 * ITERS, unit, moments)


def lost_weight(moments):
    inner = [moments[:, order : order + 1] for order in range(4)]
    first = inner[1] / inner[0]
    norm = inner[2] - first * inner[1]
    second = (inner[3] - 2.0 * first * inner[2] + first * first * inner[1]) / norm
    trace = first + 2.0 * second
    return jnp.where((norm > 0.0) & (trace > 0.0) & (trace < 30.0), -trace, 0.0)


def part_kernel(
    index, sub_count, slot_count, lists_ref, blocks_ref, begun_ref, field_ref, even_ref, odd_ref,
    moments_in_ref, *refs
):
    *refs, total, ahead = refs
    if index == 1:
        ratios_ref, *refs, sides_ref = refs
    elif index:
        ratios_ref, sides_ref, *refs = refs
    if index + 1 == ITERS:
        lost_refs, refs = refs[: sub_count - 1], refs[sub_count - 1 :]
    part_refs, moments_ref, *kept_refs = refs[:sub_count], *refs[sub_count:]
    block_len = blocks_ref.shape[1]
    sub_index, blocks_dev, own_first, tile_blocks = device_place(block_len, part_refs[0], sub_count)
    is_odd = lax.axis_index("tile") % 2 == 1
    if index == 1:
        points_dev = blocks_dev * block_len
        even = even_ref[:, points_dev:].astype(F32)
        odd = odd_ref[:, points_dev:].astype(F32)
        tile_unit = ratios_ref[:, sub_count * LANES :]
        sides = [side / tile_unit for side in neighbours(is_odd, even, odd)]
        sides_ref[...] = jnp.concatenate(sides, axis=1)
    elif index:
        sides = [sides_ref[:, :LANES], sides_ref[:, LANES:]]
    if index:
        before, after = [widen(raised(side, index), block_len) for side in sides]
    for block in range(blocks_dev):
        span = slice(block * block_len, (block + 1) * block_len)
        even = even_ref[:, span].astype(F32)
        odd = odd_ref[:, span].astype(F32)
        products, first_row = neighbours(is_odd, even, odd)
        ahead[block] = first_row * after if index else first_row
        total[block] = begun_ref[block] + (products * before if index else products)
    for block in range(blocks_dev, tile_blocks):
        total[block] = begun_ref[block]
    total[begun_ref.shape[0] - 1] = jnp.zeros(total.shape[1:], F32)
    add_products(lists_ref, blocks_ref, slot_count, ahead, total, FROM_AHEAD, SHORT_GROUP, tile_blocks, 0)
    moments = moments_in_ref[...]
    if index + 1 == ITERS:
        weight = lost_weight(moments) * ratios_ref[:, :1]
    for step in range(sub_count):
        first = (sub_index ^ step) * blocks_dev
        for block in range(blocks_dev):
            span = slice(block * block_len, (block + 1) * block_len)
            value = total[first + block]
            if step and index + 1 == ITERS:
                value += weight * lost_refs[step - 1][:, span]
            rounded = value.astype(part_refs[step].dtype)
            part_refs[step][:, span] = rounded
            if step and kept_refs:
                kept_refs[step - 1][:, span] = value - rounded.astype(F32)
    moments_ref[...] = moments


def join_kernel(index, after_ref, unit_ref, ratios_ref, own_ref, old_ref, moments_in_ref, *refs):
    part_refs = refs[:-3]
    next_ref, rounded_ref, moments_ref = refs[-3:]
    points_dev = own_ref.shape[1]
    value = own_ref[...]
    for part_ref in part_refs:
        value += part_ref[...].astype(F32)
    unit = unit_ref[...]
    divisor = raised(ratios_ref[:, :LANES], index) * unit if index else unit
    value = value * widen(1.0 / divisor, points_dev)
    next_ref[...] = value
    rounded_ref[:, :points_dev] = value.astype(BF16)
    if index == 0:
        rounded_ref[:, points_dev:] = unit.astype(BF16)
    old = old_ref[...]
    lane = lax.broadcasted_iota(jnp.int32, moments_ref.shape, 1)
    moments = moments_in_ref[...] if index else jnp.zeros(moments_ref.shape, F32)
    found = {2 * index + 1: old * value, 2 * index + 2: value * value}
    if index == 0:
        found[0] = old * old
    for order, product in found.items():
        moments = jnp.where(lane == order, jnp.sum(product, axis=1, keepdims=True), moments)
    moments_ref[...] = moments


def add_moments_kernel(first_ref, second_ref, sum_ref):
    unit_lane = 2 * ITERS
    lane = lax.broadcasted_iota(jnp.int32, sum_ref.shape, 1)
    units = [ref[:, unit_lane : unit_lane + 1] for ref in (first_ref, second_ref)]
    larger = jnp.maximum(units[0], units[1])
    result = jnp.zeros(sum_ref.shape, F32)
    for ref, unit in zip((first_ref, second_ref), units):
        ratio = unit / larger
        value = ref[...]
        for order in range(1, unit_lane):
            value = jnp.where(lane >= order, value * ratio, value)
        result += value
    sum_ref[...] = jnp.where(lane == unit_lane, larger, result)


def finish_kernel(sub_count, moments_ref, unit_ref, ratios_ref, *refs):
    part_refs, basis_refs = refs[:sub_count], refs[sub_count:-2]
    solution_ref, residual_ref = refs[-2:]
    moments = [moments_ref[:, order : order + 1] for order in range(2 * ITERS)]
    largest = moments_ref[:, 2 * ITERS : 2 * ITERS + 1]
    unit = unit_ref[:, :1]
    ratio = unit / largest

    def inner(first, second, shift):
        value = 0.0
        for i, a in enumerate(first):
            for j, b in enumerate(second):
                value = value + a * b * moments[i + j + shift]
        return value

    one = jnp.ones_like(moments[0])
    zero = jnp.zeros_like(one)
    direction, residual = [one], [one]
    answer = [zero] * ITERS
    norm_now = moments[0]
    for iteration in range(ITERS):
        step_size = norm_now / inner(direction, direction, 1)
        for power, weight in enumerate(direction):
            answer[power] = answer[power] + step_size * weight
        residual = residual + [zero]
        for power, weight in enumerate(direction):
            residual[power + 1] = residual[power + 1] - step_size * weight
        if iteration + 1 < ITERS:
            norm_next = inner(residual, residual, 0)
            direction = [
                value + (norm_next / norm_now) * old
                for value, old in zip(residual, direction + [zero])
            ]
            norm_now = norm_next
    fields = [basis_ref[...] for basis_ref in basis_refs]
    fields.append(sum(part_ref[...].astype(F32) for part_ref in part_refs))
    for order in range(1, ITERS + 1):
        scale = raised(ratio, order)
        if order < ITERS:
            answer[order] = answer[order] * scale
        else:
            scale = scale / (raised(ratios_ref[:, :1], ITERS - 1) * unit)
        residual[order] = residual[order] * scale
    answer = [weight / largest for weight in answer]
    solution_ref[...] = sum(weight * field for weight, field in zip(answer, fields))
    residual_ref[...] = sum(weight * field for weight, field in zip(residual, fields))


def shape(rows, columns, kind):
    return jax.ShapeDtypeStruct((rows, columns), kind)


def exchange(block, axis, step):
    count = lax.axis_size(axis)
    return lax.ppermute(block, axis, [(i, i ^ step) for i in range(count)])


def swap(block, axis, first):
    count = lax.axis_size(axis)
    route = []
    for i in range(first, count - 1, 2):
        route += [(i, i + 1), (i + 1, i)]
    return lax.ppermute(block, axis, route)


def call(kernel, outs, ins, name, cost=0, **options):
    single = not isinstance(outs, tuple)
    specs = [SMEM if value.dtype == jnp.int32 else VMEM for value in ins]
    options.setdefault("in_specs", specs)
    options.setdefault("out_specs", VMEM if single else (VMEM,) * len(outs))
    return pl.pallas_call(
        kernel,
        out_shape=outs,
        compiler_params=PARAMS,
        name=name,
        cost_estimate=pl.CostEstimate(flops=int(cost * 1e9), bytes_accessed=0, transcendentals=0),
        **options,
    )(*ins)


def on_device(right_side, point_order, noise_var, block_pairs, pair_blocks, diag_blocks):
    sub_count = lax.axis_size("sub")
    tile_count = lax.axis_size("tile")
    rhs_count, points_dev = right_side.shape
    blocks_dev, block_len = diag_blocks.shape[:2]
    extended = (sub_count + 1) * blocks_dev
    noise = noise_var[None, :]
    full = shape(rhs_count, points_dev, F32)
    half = shape(rhs_count, points_dev, BF16)
    scalars = shape(rhs_count, LANES, F32)
    sums = jax.ShapeDtypeStruct((extended + 1, rhs_count, block_len), F32)

    def scratch(blocks):
        return pltpu.VMEM((blocks, rhs_count, block_len), F32)

    slot_count = pair_blocks.shape[0]
    width = -(-slot_count // LANES) * LANES
    assert 2 * width <= 256 and extended < 256 and slot_count % TURN_GROUP == 0
    lists_shape = (1, len(KINDS) * list_stride(slot_count) + 2 * LANES)
    lists = call(
        functools.partial(lists_kernel, sub_count, blocks_dev, slot_count),
        pltpu.SMEM(lists_shape, jnp.int32),
        (block_pairs.T,),
        "lists",
        1,
        in_specs=[VMEM],
        out_specs=SMEM,
        scratch_shapes=[
            pltpu.VMEM((8, width), F32),
            pltpu.VMEM(lists_shape, jnp.int32),
            pltpu.SemaphoreType.DMA(()),
        ],
    )
    blocks = pair_blocks
    field, rounded = call(
        order_kernel,
        (full, half),
        [pltpu.with_memory_space_constraint(value, pltpu.HBM) for value in (right_side, point_order)],
        "curve_order",
        10,
        in_specs=[pl.BlockSpec(memory_space=pltpu.HBM)] * 2,
        scratch_shapes=[
            pltpu.VMEM(right_side.shape, F32),
            pltpu.VMEM(point_order.shape, jnp.int32),
            pltpu.SemaphoreType.DMA((2,)),
        ],
    )
    basis = [field]
    moments = jnp.zeros(scalars.shape, F32)
    ratios = sides = ()
    for index in range(ITERS):
        is_last = index + 1 == ITERS
        rows = [exchange(rounded, "sub", step) for step in range(1, sub_count)]
        begun = call(
            functools.partial(early_kernel, index, sub_count, slot_count),
            sums,
            (lists, blocks, *((diag_blocks, noise, field) if index else ()), rounded),
            "early",
            3,
            scratch_shapes=[scratch(extended)],
        )
        message = shape(rhs_count, points_dev + LANES, BF16) if index == 1 else half
        even, odd, tile_field, *found = call(
            functools.partial(ahead_kernel, index, sub_count, slot_count),
            (message, message, jax.ShapeDtypeStruct((sub_count * blocks_dev, rhs_count, block_len), F32))
            + ((shape(rhs_count, (sub_count + 1) * LANES, F32),) if index == 1 else ()),
            (lists, blocks, begun, *ratios, rounded, *rows),
            "ahead",
            1,
            scratch_shapes=[scratch(blocks_dev + 1)],
        )
        ratios = ratios or tuple(found)
        even = swap(even, "tile", 0)
        odd = swap(odd, "tile", 1)
        begun = call(
            functools.partial(late_kernel, index, slot_count),
            sums,
            (lists, blocks, begun, tile_field, *ratios),
            "late",
            3,
        )
        if is_last:
            curved = call(
                curvature_kernel,
                scalars,
                (begun, tile_field, even, odd, moments, unit, *ratios, *sides),
                "curvature",
            )
        part = shape(rhs_count, points_dev, F32 if is_last else BF16)
        found = call(
            functools.partial(part_kernel, index, sub_count, slot_count),
            (full,)
            + (part,) * (sub_count - 1)
            + (scalars,)
            + ((full,) * (sub_count - 1) if index + 2 == ITERS else ())
            + ((shape(rhs_count, 2 * LANES, F32),) if index == 1 else ()),
            (lists, blocks, begun, tile_field, even, odd, moments, *ratios, *sides, *(lost if is_last else ())),
            "parts",
            1,
            scratch_shapes=[scratch(extended + 1), scratch(blocks_dev)],
        )
        parts, moments = list(found[:sub_count]), found[sub_count]
        if index == 1:
            sides = (found[-1],)
        lost = found[sub_count + 1 : 2 * sub_count]
        if is_last:
            break
        if index == 0:
            blocks = call(
                turn_kernel,
                pltpu.VMEM((2 * slot_count, block_len, block_len), BF16),
                (pair_blocks, moments),
                "turn",
                4,
                scratch_shapes=[pltpu.SemaphoreType.DMA(())],
            )
            own_sum, unit = call(
                own_kernel, (full, scalars), (moments, diag_blocks, noise, field, rounded), "own", 0.5
            )
        arrived = [exchange(parts[step], "sub", step) for step in range(sub_count - 1, 0, -1)]
        if index == 0:
            arrived.append(own_sum)
        field, rounded, moments = call(
            functools.partial(join_kernel, index),
            (full, half if index else shape(rhs_count, points_dev + LANES, BF16), scalars),
            (blocks, unit, *(ratios or (unit,)), parts[0], field, moments, *arrived),
            "join",
        )
        basis.append(field)
    moments = curved
    arrived = []
    for axis, count in (("sub", sub_count), ("tile", tile_count)):
        step = 1
        while step < count:
            moments = call(add_moments_kernel, scalars, (moments, exchange(moments, axis, step)), "add_moments")
            if len(arrived) < sub_count - 1:
                far = sub_count - 1 - len(arrived)
                arrived.append(exchange(parts[far], "sub", far))
                moments, *parts = lax.optimization_barrier((moments, *parts))
            step *= 2
    for far in range(sub_count - 1 - len(arrived), 0, -1):
        arrived.append(exchange(parts[far], "sub", far))
    return call(
        functools.partial(finish_kernel, sub_count),
        (full, full),
        (moments, unit, *ratios, parts[0], *arrived, *basis),
        "finish",
    )


def solution(mesh):
    placed = (
        P(None, ("tile", "sub")),
        P(("tile", "sub"), None),
        P(("tile", "sub")),
        P(("tile", "sub"), None),
        P(("tile", "sub"), None, None),
        P(("tile", "sub"), None, None),
    )
    return jax.shard_map(
        on_device,
        mesh=mesh,
        in_specs=placed,
        out_specs=(P(None, ("tile", "sub")), P(None, ("tile", "sub"))),
        check_vma=False,
    )
```

```python
import functools

import jax
import jax.numpy as jnp
from jax import lax
from jax.experimental import pallas as pl
from jax.experimental.pallas import tpu as pltpu
from jax.sharding import PartitionSpec as P

ITERS = 3
LANES = 128
LONG_GROUP = 16
SHORT_GROUP = 8
TURN_GROUP = 24
TURN_PRODUCTS = 6
QUARTERS = 4
F32 = jnp.float32
BF16 = jnp.bfloat16
VMEM = pl.BlockSpec(memory_space=pltpu.VMEM)
SMEM = pl.BlockSpec(memory_space=pltpu.SMEM)
EARLY, AHEAD, LATE, FROM_AHEAD = KINDS = range(4)
PARAMS = pltpu.CompilerParams(vmem_limit_bytes=4 * 1024 * 1024)


def times(field, block):
    return lax.dot_general(field, block, (((1,), (0,)), ((), ())), preferred_element_type=F32)


def times_transposed(field, block):
    return lax.dot_general(field, block, (((1,), (1,)), ((), ())), preferred_element_type=F32)


def order_kernel(right_in, order_in, curve_ref, rounded_ref, right_ref, order_ref, sems):
    copies = [
        pltpu.make_async_copy(right_in, right_ref, sems.at[0]),
        pltpu.make_async_copy(order_in, order_ref, sems.at[1]),
    ]
    for copy in copies:
        copy.start()
    for copy in copies:
        copy.wait()
    rhs_count, points = right_ref.shape
    for start in range(0, points, LANES):
        at = jnp.broadcast_to(order_ref[:, start : start + LANES], (rhs_count, LANES))
        chunk = at // LANES
        lane = at % LANES
        result = jnp.zeros((rhs_count, LANES), F32)
        for source in range(points // LANES):
            values = right_ref[:, source * LANES : (source + 1) * LANES]
            picked = jnp.take_along_axis(values, lane, axis=1)
            result = jnp.where(chunk == source, picked, result)
        curve_ref[:, start : start + LANES] = result
        rounded_ref[:, start : start + LANES] = result.astype(BF16)


def device_place(block_len, field_ref, sub_count):
    blocks_dev = field_ref.shape[1] // block_len
    sub_index = lax.axis_index("sub")
    return sub_index, blocks_dev, sub_index * blocks_dev, blocks_dev * sub_count


def list_stride(slot_count):
    return -(-(2 * slot_count + LONG_GROUP) // LANES) * LANES


def lists_kernel(sub_count, blocks_dev, slot_count, pairs_ref, out_ref, padded, lists_ref, sem):
    width = padded.shape[1]
    stride = list_stride(slot_count)
    sub_index = lax.axis_index("sub")
    tile_blocks = blocks_dev * sub_count
    first_block = lax.axis_index("tile") * tile_blocks
    padded[...] = jnp.full(padded.shape, -1.0, F32)
    padded[0:2, 0:slot_count] = pairs_ref[...].astype(F32)
    by_lane = padded[...]
    by_row = jnp.transpose(by_lane)

    def sides(row, col, axis):
        live = jnp.concatenate([row, row], axis) >= 0.0
        row = row.astype(jnp.int32) - first_block
        col = col.astype(jnp.int32) - first_block
        source = jnp.concatenate([row, col], axis)
        target = jnp.concatenate([col, row], axis)
        return live, source, target

    live, source, target = sides(by_row[:, 0:1], by_row[:, 1:2], 0)
    kind = jnp.where(target >= tile_blocks, AHEAD, LATE)
    first_own = sub_index * blocks_dev
    is_early = (source >= first_own) & (source < first_own + blocks_dev)
    kind = jnp.where(is_early, EARLY, kind)
    kind = jnp.where(source >= tile_blocks, FROM_AHEAD, kind)
    kind = jnp.where(live, kind, -1)
    hot = (kind == lax.broadcasted_iota(jnp.int32, (2 * width, LANES), 1)).astype(F32)
    below = lax.broadcasted_iota(jnp.int32, (2 * width, 2 * width), 0) > lax.broadcasted_iota(
        jnp.int32, (2 * width, 2 * width), 1
    )
    ranks = times(below.astype(F32).astype(BF16), hot.astype(BF16))
    rank = jnp.sum(ranks * hot, axis=1, keepdims=True).astype(jnp.int32)
    counts = jnp.sum(hot, axis=0, keepdims=True)
    at = jnp.where(live, kind * stride + rank, -1)
    spread = at == lax.broadcasted_iota(jnp.int32, (2 * width, len(KINDS) * stride), 1)
    live, source, target = sides(by_lane[0:1, :], by_lane[1:2, :], 1)
    lane = lax.broadcasted_iota(jnp.int32, (1, 2 * width), 1)
    block = jnp.where(lane < width, lane, lane - width + slot_count)
    fields = jnp.concatenate(
        [jnp.where(live, value, 0).astype(F32) for value in (block, source, target)]
        + [jnp.zeros((5, 2 * width), F32)],
        0,
    )
    found = times(fields.astype(BF16), spread.astype(F32).astype(BF16))
    entries = found[0:1] + 256.0 * found[1:2] + 65536.0 * found[2:3]
    entries = entries.astype(jnp.int32)
    idle = (tile_blocks + blocks_dev) * 65536
    idle_source = {
        EARLY: sub_index * blocks_dev,
        AHEAD: tile_blocks - blocks_dev,
        LATE: 0,
        FROM_AHEAD: tile_blocks,
    }
    place = lax.broadcasted_iota(jnp.int32, (1, stride), 1)
    for index in KINDS:
        span = slice(index * stride, (index + 1) * stride)
        count = counts[:, index : index + 1].astype(jnp.int32)
        lists_ref[:, span] = jnp.where(place < count, entries[:, span], idle + 256 * idle_source[index])
    lists_ref[:, len(KINDS) * stride : len(KINDS) * stride + LANES] = counts.astype(jnp.int32)
    by_column = jnp.sum(hot[:width], axis=0, keepdims=True)
    lists_ref[:, len(KINDS) * stride + LANES :] = by_column.astype(jnp.int32)
    copy = pltpu.make_async_copy(lists_ref, out_ref, sem)
    copy.start()
    copy.wait()


def turn_kernel(pairs_blocks_ref, after_ref, blocks_ref, sem):
    slot_count = pairs_blocks_ref.shape[0]
    copy = pltpu.make_async_copy(pairs_blocks_ref, blocks_ref.at[pl.ds(0, slot_count)], sem)
    copy.start()

    square = blocks_ref.shape[1:]
    identity = lax.broadcasted_iota(jnp.int32, square, 0) == lax.broadcasted_iota(jnp.int32, square, 1)
    identity = identity.astype(F32).astype(BF16)

    def one_group(group, carry):
        for step in range(TURN_GROUP):
            slot = group * TURN_GROUP + step
            block = pairs_blocks_ref[slot]
            if step < TURN_GROUP - TURN_PRODUCTS:
                turned = jnp.transpose(block)
            else:
                turned = times_transposed(identity, block).astype(BF16)
            blocks_ref[slot_count + slot] = turned
        return carry

    lax.fori_loop(0, slot_count // TURN_GROUP, one_group, 0)
    copy.wait()


def add_products(lists_ref, blocks_ref, slot_count, field, total, index, size, source_from=0, target_from=0):
    stride = list_stride(slot_count)
    idle = lists_ref[0, index * stride + stride - 1] >> 16
    count = lists_ref[0, len(KINDS) * stride + index]
    column_count = lists_ref[0, len(KINDS) * stride + LANES + index]

    def add_part(first, end, kind, plain, cuts):
        def one_group(group, carry):
            results = []
            for step in range(size):
                place = first + group * size + step
                entry = lists_ref[0, index * stride + place]
                block, source, target = entry & 255, (entry >> 8) & 255, entry >> 16
                if plain:
                    block = jnp.where(block >= slot_count, block - slot_count, block)
                if cuts:
                    target = jnp.where(place < end, target, idle)
                value = kind(field[source - source_from].astype(BF16), blocks_ref[block])
                results.append((target - target_from, value))
            for at, value in results:
                total[at] += value
            return carry

        lax.fori_loop(0, (end - first + size - 1) // size, one_group, 0)

    if blocks_ref.shape[0] > slot_count:
        add_part(0, count, times, False, False)
    else:
        add_part(0, column_count, times, True, True)
        add_part(column_count, count, times_transposed, True, False)


def raised(value, exponent):
    result = value
    for _ in range(exponent - 1):
        result = result * value
    return result


def widen(tile, columns):
    return jnp.concatenate([tile] * (columns // LANES), axis=1)


def lay_out(row_ref, field, first, blocks_dev, block_len, factor=None):
    for block in range(blocks_dev):
        piece = row_ref[:, block * block_len : (block + 1) * block_len].astype(F32)
        field[first + block] = piece if factor is None else piece * factor


def own_products(diag_ref, noise_ref, own_ref, rounded, block):
    block_len = diag_ref.shape[1]
    span = slice(block * block_len, (block + 1) * block_len)
    return noise_ref[:, span] * own_ref[:, span] + times(rounded, diag_ref[block])


def early_kernel(index, sub_count, slot_count, lists_ref, blocks_ref, *refs):
    *refs, rounded_ref, total, field = refs
    block_len = blocks_ref.shape[1]
    blocks_dev = rounded_ref.shape[1] // block_len
    own_first = lax.axis_index("sub") * blocks_dev
    lay_out(rounded_ref, field, own_first, blocks_dev, block_len)
    for block in range(total.shape[0]):
        total[block] = jnp.zeros(total.shape[1:], F32)
    if index:
        for block in range(blocks_dev):
            total[own_first + block] = own_products(*refs, field[own_first + block].astype(BF16), block)
    add_products(lists_ref, blocks_ref, slot_count, field, total, EARLY, LONG_GROUP)


def own_kernel(after_ref, diag_ref, noise_ref, own_ref, rounded_ref, sum_ref, unit_ref):
    blocks_dev, block_len = diag_ref.shape[:2]
    largest = diag_ref[0].astype(F32)
    for block in range(1, blocks_dev):
        largest = jnp.maximum(largest, diag_ref[block].astype(F32))
    unit_ref[...] = jnp.full(unit_ref.shape, jnp.maximum(jnp.max(largest) * block_len, 1.0))
    for block in range(blocks_dev):
        span = slice(block * block_len, (block + 1) * block_len)
        sum_ref[:, span] = own_products(diag_ref, noise_ref, own_ref, rounded_ref[:, span], block)


def ahead_kernel(index, sub_count, slot_count, lists_ref, blocks_ref, begun_ref, *refs):
    if index == 1:
        *refs, ratios_ref, total = refs
        row_refs, (even_ref, odd_ref, field_ref) = refs[:-3], refs[-3:]
        points_dev = even_ref.shape[1] - LANES
        units = [row_ref[:, points_dev:].astype(F32) for row_ref in row_refs]
        tile_unit = functools.reduce(jnp.maximum, units)
        ratios = [unit / tile_unit for unit in units]
        ratios_ref[...] = jnp.concatenate(ratios + [tile_unit], axis=1)
    else:
        row_refs, (even_ref, odd_ref, field_ref, total) = refs[:-4], refs[-4:]
        points_dev = even_ref.shape[1]
        if index:
            ratios_ref, *row_refs = row_refs
            ratios = [ratios_ref[:, step * LANES : (step + 1) * LANES] for step in range(sub_count)]
    block_len = blocks_ref.shape[1]
    blocks_dev = points_dev // block_len
    tile_blocks = blocks_dev * sub_count
    sub_index = lax.axis_index("sub")
    for step, row_ref in enumerate(row_refs):
        factor = widen(raised(ratios[step], index), block_len) if index else None
        lay_out(row_ref, field_ref, (sub_index ^ step) * blocks_dev, blocks_dev, block_len, factor)
    for block in range(blocks_dev):
        value = begun_ref[tile_blocks + block]
        total[block] = value * widen(raised(ratios[0], index), block_len) if index else value
    total[blocks_dev] = jnp.zeros(total.shape[1:], F32)
    add_products(lists_ref, blocks_ref, slot_count, field_ref, total, AHEAD, SHORT_GROUP, 0, tile_blocks)
    is_odd = lax.axis_index("tile") % 2 == 1
    for block in range(blocks_dev):
        span = slice(block * block_len, (block + 1) * block_len)
        products = total[block]
        first_row = field_ref[block]
        even_ref[:, span] = jnp.where(is_odd, first_row, products).astype(BF16)
        odd_ref[:, span] = jnp.where(is_odd, products, first_row).astype(BF16)
    if index == 1:
        even_ref[:, points_dev:] = tile_unit.astype(BF16)
        odd_ref[:, points_dev:] = tile_unit.astype(BF16)


def late_kernel(index, slot_count, lists_ref, blocks_ref, begun_ref, field_ref, *refs):
    total = refs[-1]
    if index:
        factor = widen(raised(refs[0][:, :LANES], index), total.shape[2])
        for block in range(total.shape[0]):
            total[block] = begun_ref[block] * factor
    else:
        total[...] = begun_ref[...]
    add_products(lists_ref, blocks_ref, slot_count, field_ref, total, LATE, LONG_GROUP)


def neighbours(is_odd, even, odd):
    return jnp.where(is_odd, even, odd), jnp.where(is_odd, odd, even)


def curvature_kernel(
    begun_ref, field_ref, even_ref, odd_ref, moments_in_ref, unit_ref, ratios_ref, sides_ref, moments_ref
):
    index = ITERS - 1
    block_len = begun_ref.shape[2]
    blocks_dev = even_ref.shape[1] // block_len
    is_odd = lax.axis_index("tile") % 2 == 1
    unit = unit_ref[...]
    scale = widen(1.0 / (raised(ratios_ref[:, :LANES], 2 * index) * unit), block_len)
    before = widen(2.0 * raised(sides_ref[:, :LANES], index), block_len)
    product = jnp.zeros(begun_ref.shape[1:], F32)
    for block in range(field_ref.shape[0]):
        value = begun_ref[block]
        if block < blocks_dev:
            span = slice(block * block_len, (block + 1) * block_len)
            arrived, _ = neighbours(is_odd, even_ref[:, span].astype(F32), odd_ref[:, span].astype(F32))
            value += arrived * before
        product += field_ref[block] * (value * scale)
    last = jnp.sum(product, axis=1, keepdims=True)
    moments = moments_in_ref[...]
    lane = lax.broadcasted_iota(jnp.int32, moments.shape, 1)
    moments = jnp.where(lane == 2 * ITERS - 1, last, moments)
    moments_ref[...] = jnp.where(lane == 2 * ITERS, unit, moments)


def lost_weight(moments):
    inner = [moments[:, order : order + 1] for order in range(4)]
    first = inner[1] / inner[0]
    norm = inner[2] - first * inner[1]
    second = (inner[3] - 2.0 * first * inner[2] + first * first * inner[1]) / norm
    trace = first + 2.0 * second
    return jnp.where((norm > 0.0) & (trace > 0.0) & (trace < 30.0), -trace, 0.0)


def part_kernel(
    index, sub_count, slot_count, lists_ref, blocks_ref, begun_ref, field_ref, even_ref, odd_ref,
    moments_in_ref, *refs
):
    *refs, total, ahead = refs
    if index == 1:
        ratios_ref, *refs, sides_ref = refs
    elif index:
        ratios_ref, sides_ref, *refs = refs
    if index + 1 == ITERS:
        lost_refs, refs = refs[: sub_count - 1], refs[sub_count - 1 :]
    part_refs, kept_refs = refs[:sub_count], refs[sub_count:]
    if index + 1 < ITERS:
        moments_ref, *kept_refs = kept_refs
        moments_ref[...] = moments_in_ref[...]
    block_len = blocks_ref.shape[1]
    sub_index, blocks_dev, own_first, tile_blocks = device_place(block_len, part_refs[0], sub_count)
    is_odd = lax.axis_index("tile") % 2 == 1
    if index == 1:
        points_dev = blocks_dev * block_len
        even = even_ref[:, points_dev:].astype(F32)
        odd = odd_ref[:, points_dev:].astype(F32)
        tile_unit = ratios_ref[:, sub_count * LANES :]
        sides = [side / tile_unit for side in neighbours(is_odd, even, odd)]
        sides_ref[...] = jnp.concatenate(sides, axis=1)
    elif index:
        sides = [sides_ref[:, :LANES], sides_ref[:, LANES:]]
    if index:
        before, after = [widen(raised(side, index), block_len) for side in sides]
    for block in range(blocks_dev):
        span = slice(block * block_len, (block + 1) * block_len)
        even = even_ref[:, span].astype(F32)
        odd = odd_ref[:, span].astype(F32)
        products, first_row = neighbours(is_odd, even, odd)
        ahead[block] = first_row * after if index else first_row
        total[block] = begun_ref[block] + (products * before if index else products)
    for block in range(blocks_dev, tile_blocks):
        total[block] = begun_ref[block]
    total[begun_ref.shape[0] - 1] = jnp.zeros(total.shape[1:], F32)
    add_products(lists_ref, blocks_ref, slot_count, ahead, total, FROM_AHEAD, SHORT_GROUP, tile_blocks, 0)
    if index + 1 == ITERS:
        weight = lost_weight(moments_in_ref[...]) * ratios_ref[:, :1]
    for step in range(sub_count):
        first = (sub_index ^ step) * blocks_dev
        for block in range(blocks_dev):
            span = slice(block * block_len, (block + 1) * block_len)
            value = total[first + block]
            if step and index + 1 == ITERS:
                value += weight * lost_refs[step - 1][:, span]
            rounded = value.astype(part_refs[step].dtype)
            part_refs[step][:, span] = rounded
            if step and kept_refs:
                kept_refs[step - 1][:, span] = value - rounded.astype(F32)


def join_kernel(index, after_ref, unit_ref, ratios_ref, own_ref, old_ref, moments_in_ref, *refs):
    part_refs = refs[:-3]
    next_ref, rounded_ref, moments_ref = refs[-3:]
    points_dev = own_ref.shape[1]
    value = own_ref[...]
    for part_ref in part_refs:
        value += part_ref[...].astype(F32)
    unit = unit_ref[...]
    divisor = raised(ratios_ref[:, :LANES], index) * unit if index else unit
    value = value * widen(1.0 / divisor, points_dev)
    next_ref[...] = value
    rounded_ref[:, :points_dev] = value.astype(BF16)
    if index == 0:
        rounded_ref[:, points_dev:] = unit.astype(BF16)
    old = old_ref[...]
    lane = lax.broadcasted_iota(jnp.int32, moments_ref.shape, 1)
    moments = moments_in_ref[...] if index else jnp.zeros(moments_ref.shape, F32)
    found = {2 * index + 1: old * value, 2 * index + 2: value * value}
    if index == 0:
        found[0] = old * old
    for order, product in found.items():
        moments = jnp.where(lane == order, jnp.sum(product, axis=1, keepdims=True), moments)
    moments_ref[...] = moments


def add_moments_kernel(first_ref, second_ref, sum_ref):
    unit_lane = 2 * ITERS
    lane = lax.broadcasted_iota(jnp.int32, sum_ref.shape, 1)
    units = [ref[:, unit_lane : unit_lane + 1] for ref in (first_ref, second_ref)]
    larger = jnp.maximum(units[0], units[1])
    result = jnp.zeros(sum_ref.shape, F32)
    for ref, unit in zip((first_ref, second_ref), units):
        ratio = unit / larger
        value = ref[...]
        for order in range(1, unit_lane):
            value = jnp.where(lane >= order, value * ratio, value)
        result += value
    sum_ref[...] = jnp.where(lane == unit_lane, larger, result)


def finish_kernel(sub_count, moments_ref, unit_ref, ratios_ref, *refs):
    part_refs, basis_refs = refs[:sub_count], refs[sub_count:-5]
    outs, (solution_ref, residual_ref, sems) = refs[-5:-3], refs[-3:]
    moments = [moments_ref[:, order : order + 1] for order in range(2 * ITERS)]
    largest = moments_ref[:, 2 * ITERS : 2 * ITERS + 1]
    unit = unit_ref[:, :1]
    ratio = unit / largest

    def inner(first, second, shift):
        value = 0.0
        for i, a in enumerate(first):
            for j, b in enumerate(second):
                value = value + a * b * moments[i + j + shift]
        return value

    one = jnp.ones_like(moments[0])
    zero = jnp.zeros_like(one)
    direction, residual = [one], [one]
    answer = [zero] * ITERS
    norm_now = moments[0]
    for iteration in range(ITERS):
        step_size = norm_now / inner(direction, direction, 1)
        for power, weight in enumerate(direction):
            answer[power] = answer[power] + step_size * weight
        residual = residual + [zero]
        for power, weight in enumerate(direction):
            residual[power + 1] = residual[power + 1] - step_size * weight
        if iteration + 1 < ITERS:
            norm_next = inner(residual, residual, 0)
            direction = [
                value + (norm_next / norm_now) * old
                for value, old in zip(residual, direction + [zero])
            ]
            norm_now = norm_next
    for order in range(1, ITERS + 1):
        scale = raised(ratio, order)
        if order < ITERS:
            answer[order] = answer[order] * scale
        else:
            scale = scale / (raised(ratios_ref[:, :1], ITERS - 1) * unit)
        residual[order] = residual[order] * scale
    answer = [weight / largest for weight in answer]
    size = solution_ref.shape[1] // QUARTERS
    copies = []
    for quarter in range(QUARTERS):
        span = slice(quarter * size, (quarter + 1) * size)
        fields = [basis_ref[:, span] for basis_ref in basis_refs]
        fields.append(sum(part_ref[:, span].astype(F32) for part_ref in part_refs))
        for index, (ref, weights) in enumerate(((solution_ref, answer), (residual_ref, residual))):
            ref[:, span] = sum(weight * field for weight, field in zip(weights, fields))
            copy = pltpu.make_async_copy(ref.at[:, span], outs[index].at[:, span], sems.at[index, quarter])
            copy.start()
            copies.append(copy)
    for copy in copies:
        copy.wait()


def shape(rows, columns, kind):
    return jax.ShapeDtypeStruct((rows, columns), kind)


def exchange(block, axis, step):
    count = lax.axis_size(axis)
    return lax.ppermute(block, axis, [(i, i ^ step) for i in range(count)])


def swap(block, axis, first):
    count = lax.axis_size(axis)
    route = []
    for i in range(first, count - 1, 2):
        route += [(i, i + 1), (i + 1, i)]
    return lax.ppermute(block, axis, route)


def call(kernel, outs, ins, name, cost=0, **options):
    single = not isinstance(outs, tuple)
    specs = [SMEM if value.dtype == jnp.int32 else VMEM for value in ins]
    options.setdefault("in_specs", specs)
    options.setdefault("out_specs", VMEM if single else (VMEM,) * len(outs))
    return pl.pallas_call(
        kernel,
        out_shape=outs,
        compiler_params=PARAMS,
        name=name,
        cost_estimate=pl.CostEstimate(flops=int(cost * 1e9), bytes_accessed=0, transcendentals=0),
        **options,
    )(*ins)


def on_device(right_side, point_order, noise_var, block_pairs, pair_blocks, diag_blocks):
    sub_count = lax.axis_size("sub")
    tile_count = lax.axis_size("tile")
    rhs_count, points_dev = right_side.shape
    blocks_dev, block_len = diag_blocks.shape[:2]
    extended = (sub_count + 1) * blocks_dev
    noise = noise_var[None, :]
    full = shape(rhs_count, points_dev, F32)
    half = shape(rhs_count, points_dev, BF16)
    scalars = shape(rhs_count, LANES, F32)
    sums = jax.ShapeDtypeStruct((extended + 1, rhs_count, block_len), F32)

    def scratch(blocks):
        return pltpu.VMEM((blocks, rhs_count, block_len), F32)

    slot_count = pair_blocks.shape[0]
    width = -(-slot_count // LANES) * LANES
    assert 2 * width <= 256 and extended < 256 and slot_count % TURN_GROUP == 0
    lists_shape = (1, len(KINDS) * list_stride(slot_count) + 2 * LANES)
    lists = call(
        functools.partial(lists_kernel, sub_count, blocks_dev, slot_count),
        pltpu.SMEM(lists_shape, jnp.int32),
        (block_pairs.T,),
        "lists",
        1,
        in_specs=[VMEM],
        out_specs=SMEM,
        scratch_shapes=[
            pltpu.VMEM((8, width), F32),
            pltpu.VMEM(lists_shape, jnp.int32),
            pltpu.SemaphoreType.DMA(()),
        ],
    )
    field, rounded = call(
        order_kernel,
        (full, half),
        [pltpu.with_memory_space_constraint(value, pltpu.HBM) for value in (right_side, point_order)],
        "curve_order",
        10,
        in_specs=[pl.BlockSpec(memory_space=pltpu.HBM)] * 2,
        scratch_shapes=[
            pltpu.VMEM(right_side.shape, F32),
            pltpu.VMEM(point_order.shape, jnp.int32),
            pltpu.SemaphoreType.DMA((2,)),
        ],
    )
    blocks = pair_blocks
    basis = [field]
    moments = jnp.zeros(scalars.shape, F32)
    ratios = sides = ()
    for index in range(ITERS):
        is_last = index + 1 == ITERS
        rows = [exchange(rounded, "sub", step) for step in range(1, sub_count)]
        begun = call(
            functools.partial(early_kernel, index, sub_count, slot_count),
            sums,
            (lists, blocks, *((diag_blocks, noise, field) if index else ()), rounded),
            "early",
            3,
            scratch_shapes=[scratch(extended)],
        )
        message = shape(rhs_count, points_dev + LANES, BF16) if index == 1 else half
        even, odd, tile_field, *found = call(
            functools.partial(ahead_kernel, index, sub_count, slot_count),
            (message, message, jax.ShapeDtypeStruct((sub_count * blocks_dev, rhs_count, block_len), F32))
            + ((shape(rhs_count, (sub_count + 1) * LANES, F32),) if index == 1 else ()),
            (lists, blocks, begun, *ratios, rounded, *rows),
            "ahead",
            1,
            scratch_shapes=[scratch(blocks_dev + 1)],
        )
        ratios = ratios or tuple(found)
        even = swap(even, "tile", 0)
        odd = swap(odd, "tile", 1)
        begun = call(
            functools.partial(late_kernel, index, slot_count),
            sums,
            (lists, blocks, begun, tile_field, *ratios),
            "late",
            3,
        )
        if is_last:
            curved = call(
                curvature_kernel,
                scalars,
                (begun, tile_field, even, odd, moments, unit, *ratios, *sides),
                "curvature",
            )
        part = shape(rhs_count, points_dev, F32 if is_last else BF16)
        found = call(
            functools.partial(part_kernel, index, sub_count, slot_count),
            (full,)
            + (part,) * (sub_count - 1)
            + (() if is_last else (scalars,))
            + ((full,) * (sub_count - 1) if index + 2 == ITERS else ())
            + ((shape(rhs_count, 2 * LANES, F32),) if index == 1 else ()),
            (lists, blocks, begun, tile_field, even, odd, moments, *ratios, *sides, *(lost if is_last else ())),
            "parts",
            1,
            scratch_shapes=[scratch(extended + 1), scratch(blocks_dev)],
        )
        parts = list(found[:sub_count])
        if not is_last:
            moments = found[sub_count]
        if index == 1:
            sides = (found[-1],)
        lost = found[sub_count + 1 : 2 * sub_count]
        if is_last:
            break
        if index == 0:
            blocks = call(
                turn_kernel,
                pltpu.VMEM((2 * slot_count, block_len, block_len), BF16),
                (pair_blocks, moments),
                "turn",
                4,
                scratch_shapes=[pltpu.SemaphoreType.DMA(())],
            )
            own_sum, unit = call(
                own_kernel, (full, scalars), (moments, diag_blocks, noise, field, rounded), "own", 0.5
            )
        arrived = [exchange(parts[step], "sub", step) for step in range(sub_count - 1, 0, -1)]
        if index == 0:
            arrived.append(own_sum)
        field, rounded, moments = call(
            functools.partial(join_kernel, index),
            (full, half if index else shape(rhs_count, points_dev + LANES, BF16), scalars),
            (blocks, unit, *(ratios or (unit,)), parts[0], field, moments, *arrived),
            "join",
        )
        basis.append(field)
    moments = curved
    arrived = []
    for axis, count in (("sub", sub_count), ("tile", tile_count)):
        step = 1
        while step < count:
            moments = call(add_moments_kernel, scalars, (moments, exchange(moments, axis, step)), "add_moments")
            if len(arrived) < sub_count - 1:
                far = sub_count - 1 - len(arrived)
                arrived.append(exchange(parts[far], "sub", far))
                moments, *parts = lax.optimization_barrier((moments, *parts))
            step *= 2
    for far in range(sub_count - 1 - len(arrived), 0, -1):
        arrived.append(exchange(parts[far], "sub", far))
    return call(
        functools.partial(finish_kernel, sub_count),
        (full, full),
        (moments, unit, *ratios, parts[0], *arrived, *basis),
        "finish",
        out_specs=(pl.BlockSpec(memory_space=pltpu.HBM),) * 2,
        scratch_shapes=[
            pltpu.VMEM(right_side.shape, F32),
            pltpu.VMEM(right_side.shape, F32),
            pltpu.SemaphoreType.DMA((2, QUARTERS)),
        ],
    )


def solution(mesh):
    placed = (
        P(None, ("tile", "sub")),
        P(("tile", "sub"), None),
        P(("tile", "sub")),
        P(("tile", "sub"), None),
        P(("tile", "sub"), None, None),
        P(("tile", "sub"), None, None),
    )
    return jax.shard_map(
        on_device,
        mesh=mesh,
        in_specs=placed,
        out_specs=(P(None, ("tile", "sub")), P(None, ("tile", "sub"))),
        check_vma=False,
    )
```

```python
import functools

import jax
import jax.numpy as jnp
from jax import lax
from jax.experimental import pallas as pl
from jax.experimental.pallas import tpu as pltpu
from jax.sharding import PartitionSpec as P

ITERS = 3
LANES = 128
LONG_GROUP = 24
SHORT_GROUP = 12
TURN_GROUP = 24
TURN_PRODUCTS = 6
QUARTERS = 4
F32 = jnp.float32
BF16 = jnp.bfloat16
VMEM = pl.BlockSpec(memory_space=pltpu.VMEM)
SMEM = pl.BlockSpec(memory_space=pltpu.SMEM)
EARLY, AHEAD, LATE, FROM_AHEAD = KINDS = range(4)
PARAMS = pltpu.CompilerParams(vmem_limit_bytes=4 * 1024 * 1024)


def times(field, block):
    return lax.dot_general(field, block, (((1,), (0,)), ((), ())), preferred_element_type=F32)


def times_transposed(field, block):
    return lax.dot_general(field, block, (((1,), (1,)), ((), ())), preferred_element_type=F32)


def order_kernel(right_in, order_in, curve_ref, rounded_ref, right_ref, order_ref, sems):
    copies = [
        pltpu.make_async_copy(right_in, right_ref, sems.at[0]),
        pltpu.make_async_copy(order_in, order_ref, sems.at[1]),
    ]
    for copy in copies:
        copy.start()
    for copy in copies:
        copy.wait()
    rhs_count, points = right_ref.shape
    for start in range(0, points, LANES):
        at = jnp.broadcast_to(order_ref[:, start : start + LANES], (rhs_count, LANES))
        chunk = at // LANES
        lane = at % LANES
        result = jnp.zeros((rhs_count, LANES), F32)
        for source in range(points // LANES):
            values = right_ref[:, source * LANES : (source + 1) * LANES]
            picked = jnp.take_along_axis(values, lane, axis=1)
            result = jnp.where(chunk == source, picked, result)
        curve_ref[:, start : start + LANES] = result
        rounded_ref[:, start : start + LANES] = result.astype(BF16)


def device_place(block_len, field_ref, sub_count):
    blocks_dev = field_ref.shape[1] // block_len
    sub_index = lax.axis_index("sub")
    return sub_index, blocks_dev, sub_index * blocks_dev, blocks_dev * sub_count


def list_stride(slot_count):
    return -(-(2 * slot_count + LONG_GROUP) // LANES) * LANES


def lists_kernel(sub_count, blocks_dev, slot_count, pairs_ref, out_ref, padded, lists_ref, sem):
    width = padded.shape[1]
    stride = list_stride(slot_count)
    sub_index = lax.axis_index("sub")
    tile_blocks = blocks_dev * sub_count
    first_block = lax.axis_index("tile") * tile_blocks
    padded[...] = jnp.full(padded.shape, -1.0, F32)
    padded[0:2, 0:slot_count] = pairs_ref[...].astype(F32)
    by_lane = padded[...]
    by_row = jnp.transpose(by_lane)

    def sides(row, col, axis):
        live = jnp.concatenate([row, row], axis) >= 0.0
        row = row.astype(jnp.int32) - first_block
        col = col.astype(jnp.int32) - first_block
        source = jnp.concatenate([row, col], axis)
        target = jnp.concatenate([col, row], axis)
        return live, source, target

    live, source, target = sides(by_row[:, 0:1], by_row[:, 1:2], 0)
    kind = jnp.where(target >= tile_blocks, AHEAD, LATE)
    first_own = sub_index * blocks_dev
    is_early = (source >= first_own) & (source < first_own + blocks_dev)
    kind = jnp.where(is_early, EARLY, kind)
    kind = jnp.where(source >= tile_blocks, FROM_AHEAD, kind)
    kind = jnp.where(live, kind, -1)
    hot = (kind == lax.broadcasted_iota(jnp.int32, (2 * width, LANES), 1)).astype(F32)
    below = lax.broadcasted_iota(jnp.int32, (2 * width, 2 * width), 0) > lax.broadcasted_iota(
        jnp.int32, (2 * width, 2 * width), 1
    )
    ranks = times(below.astype(F32).astype(BF16), hot.astype(BF16))
    rank = jnp.sum(ranks * hot, axis=1, keepdims=True).astype(jnp.int32)
    counts = jnp.sum(hot, axis=0, keepdims=True)
    at = jnp.where(live, kind * stride + rank, -1)
    spread = at == lax.broadcasted_iota(jnp.int32, (2 * width, len(KINDS) * stride), 1)
    live, source, target = sides(by_lane[0:1, :], by_lane[1:2, :], 1)
    lane = lax.broadcasted_iota(jnp.int32, (1, 2 * width), 1)
    block = jnp.where(lane < width, lane, lane - width + slot_count)
    fields = jnp.concatenate(
        [jnp.where(live, value, 0).astype(F32) for value in (block, source, target)]
        + [jnp.zeros((5, 2 * width), F32)],
        0,
    )
    found = times(fields.astype(BF16), spread.astype(F32).astype(BF16))
    entries = found[0:1] + 256.0 * found[1:2] + 65536.0 * found[2:3]
    entries = entries.astype(jnp.int32)
    idle = (tile_blocks + blocks_dev) * 65536
    idle_source = {
        EARLY: sub_index * blocks_dev,
        AHEAD: tile_blocks - blocks_dev,
        LATE: 0,
        FROM_AHEAD: tile_blocks,
    }
    place = lax.broadcasted_iota(jnp.int32, (1, stride), 1)
    for index in KINDS:
        span = slice(index * stride, (index + 1) * stride)
        count = counts[:, index : index + 1].astype(jnp.int32)
        lists_ref[:, span] = jnp.where(place < count, entries[:, span], idle + 256 * idle_source[index])
    lists_ref[:, len(KINDS) * stride : len(KINDS) * stride + LANES] = counts.astype(jnp.int32)
    by_column = jnp.sum(hot[:width], axis=0, keepdims=True)
    lists_ref[:, len(KINDS) * stride + LANES :] = by_column.astype(jnp.int32)
    copy = pltpu.make_async_copy(lists_ref, out_ref, sem)
    copy.start()
    copy.wait()


def turn_kernel(pairs_blocks_ref, after_ref, blocks_ref, sem):
    slot_count = pairs_blocks_ref.shape[0]
    copy = pltpu.make_async_copy(pairs_blocks_ref, blocks_ref.at[pl.ds(0, slot_count)], sem)
    copy.start()

    square = blocks_ref.shape[1:]
    identity = lax.broadcasted_iota(jnp.int32, square, 0) == lax.broadcasted_iota(jnp.int32, square, 1)
    identity = identity.astype(F32).astype(BF16)

    def one_group(group, carry):
        for step in range(TURN_GROUP):
            slot = group * TURN_GROUP + step
            block = pairs_blocks_ref[slot]
            if step < TURN_GROUP - TURN_PRODUCTS:
                turned = jnp.transpose(block)
            else:
                turned = times_transposed(identity, block).astype(BF16)
            blocks_ref[slot_count + slot] = turned
        return carry

    lax.fori_loop(0, slot_count // TURN_GROUP, one_group, 0)
    copy.wait()


def add_products(lists_ref, blocks_ref, slot_count, field, total, index, size, source_from=0, target_from=0):
    stride = list_stride(slot_count)
    idle = lists_ref[0, index * stride + stride - 1] >> 16
    count = lists_ref[0, len(KINDS) * stride + index]
    column_count = lists_ref[0, len(KINDS) * stride + LANES + index]

    def add_part(first, end, kind, plain, cuts):
        def one_group(group, carry):
            results = []
            for step in range(size):
                place = first + group * size + step
                entry = lists_ref[0, index * stride + place]
                block, source, target = entry & 255, (entry >> 8) & 255, entry >> 16
                if plain:
                    block = jnp.where(block >= slot_count, block - slot_count, block)
                if cuts:
                    target = jnp.where(place < end, target, idle)
                value = kind(field[source - source_from].astype(BF16), blocks_ref[block])
                results.append((target - target_from, value))
            for at, value in results:
                total[at] += value
            return carry

        lax.fori_loop(0, (end - first + size - 1) // size, one_group, 0)

    if blocks_ref.shape[0] > slot_count:
        add_part(0, count, times, False, False)
    else:
        add_part(0, column_count, times, True, True)
        add_part(column_count, count, times_transposed, True, False)


def raised(value, exponent):
    result = value
    for _ in range(exponent - 1):
        result = result * value
    return result


def widen(tile, columns):
    return jnp.concatenate([tile] * (columns // LANES), axis=1)


def lay_out(row_ref, field, first, blocks_dev, block_len, factor=None):
    for block in range(blocks_dev):
        piece = row_ref[:, block * block_len : (block + 1) * block_len].astype(F32)
        field[first + block] = piece if factor is None else piece * factor


def own_products(diag_ref, noise_ref, own_ref, rounded, block):
    block_len = diag_ref.shape[1]
    span = slice(block * block_len, (block + 1) * block_len)
    return noise_ref[:, span] * own_ref[:, span] + times(rounded, diag_ref[block])


def early_kernel(index, sub_count, slot_count, lists_ref, blocks_ref, *refs):
    *refs, rounded_ref, total, field = refs
    block_len = blocks_ref.shape[1]
    blocks_dev = rounded_ref.shape[1] // block_len
    own_first = lax.axis_index("sub") * blocks_dev
    lay_out(rounded_ref, field, own_first, blocks_dev, block_len)
    for block in range(total.shape[0]):
        total[block] = jnp.zeros(total.shape[1:], F32)
    if index:
        for block in range(blocks_dev):
            total[own_first + block] = own_products(*refs, field[own_first + block].astype(BF16), block)
    add_products(lists_ref, blocks_ref, slot_count, field, total, EARLY, LONG_GROUP)


def own_kernel(after_ref, diag_ref, noise_ref, own_ref, rounded_ref, sum_ref, unit_ref):
    blocks_dev, block_len = diag_ref.shape[:2]
    largest = diag_ref[0].astype(F32)
    for block in range(1, blocks_dev):
        largest = jnp.maximum(largest, diag_ref[block].astype(F32))
    unit_ref[...] = jnp.full(unit_ref.shape, jnp.maximum(jnp.max(largest) * block_len, 1.0))
    for block in range(blocks_dev):
        span = slice(block * block_len, (block + 1) * block_len)
        sum_ref[:, span] = own_products(diag_ref, noise_ref, own_ref, rounded_ref[:, span], block)


def ahead_kernel(index, sub_count, slot_count, lists_ref, blocks_ref, begun_ref, *refs):
    if index == 1:
        *refs, ratios_ref, total = refs
        row_refs, (even_ref, odd_ref, field_ref) = refs[:-3], refs[-3:]
        points_dev = even_ref.shape[1] - LANES
        units = [row_ref[:, points_dev:].astype(F32) for row_ref in row_refs]
        tile_unit = functools.reduce(jnp.maximum, units)
        ratios = [unit / tile_unit for unit in units]
        ratios_ref[...] = jnp.concatenate(ratios + [tile_unit], axis=1)
    else:
        row_refs, (even_ref, odd_ref, field_ref, total) = refs[:-4], refs[-4:]
        points_dev = even_ref.shape[1]
        if index:
            ratios_ref, *row_refs = row_refs
            ratios = [ratios_ref[:, step * LANES : (step + 1) * LANES] for step in range(sub_count)]
    block_len = blocks_ref.shape[1]
    blocks_dev = points_dev // block_len
    tile_blocks = blocks_dev * sub_count
    sub_index = lax.axis_index("sub")
    for step, row_ref in enumerate(row_refs):
        factor = widen(raised(ratios[step], index), block_len) if index else None
        lay_out(row_ref, field_ref, (sub_index ^ step) * blocks_dev, blocks_dev, block_len, factor)
    for block in range(blocks_dev):
        value = begun_ref[tile_blocks + block]
        total[block] = value * widen(raised(ratios[0], index), block_len) if index else value
    total[blocks_dev] = jnp.zeros(total.shape[1:], F32)
    add_products(lists_ref, blocks_ref, slot_count, field_ref, total, AHEAD, SHORT_GROUP, 0, tile_blocks)
    is_odd = lax.axis_index("tile") % 2 == 1
    for block in range(blocks_dev):
        span = slice(block * block_len, (block + 1) * block_len)
        products = total[block]
        first_row = field_ref[block]
        even_ref[:, span] = jnp.where(is_odd, first_row, products).astype(BF16)
        odd_ref[:, span] = jnp.where(is_odd, products, first_row).astype(BF16)
    if index == 1:
        even_ref[:, points_dev:] = tile_unit.astype(BF16)
        odd_ref[:, points_dev:] = tile_unit.astype(BF16)


def late_kernel(index, slot_count, lists_ref, blocks_ref, begun_ref, field_ref, *refs):
    total = refs[-1]
    if index:
        factor = widen(raised(refs[0][:, :LANES], index), total.shape[2])
        for block in range(total.shape[0]):
            total[block] = begun_ref[block] * factor
    else:
        total[...] = begun_ref[...]
    add_products(lists_ref, blocks_ref, slot_count, field_ref, total, LATE, LONG_GROUP)


def neighbours(is_odd, even, odd):
    return jnp.where(is_odd, even, odd), jnp.where(is_odd, odd, even)


def curvature_kernel(
    begun_ref, field_ref, even_ref, odd_ref, moments_in_ref, unit_ref, ratios_ref, sides_ref, moments_ref
):
    index = ITERS - 1
    block_len = begun_ref.shape[2]
    blocks_dev = even_ref.shape[1] // block_len
    is_odd = lax.axis_index("tile") % 2 == 1
    unit = unit_ref[...]
    scale = widen(1.0 / (raised(ratios_ref[:, :LANES], 2 * index) * unit), block_len)
    before = widen(2.0 * raised(sides_ref[:, :LANES], index), block_len)
    product = jnp.zeros(begun_ref.shape[1:], F32)
    for block in range(field_ref.shape[0]):
        value = begun_ref[block]
        if block < blocks_dev:
            span = slice(block * block_len, (block + 1) * block_len)
            arrived, _ = neighbours(is_odd, even_ref[:, span].astype(F32), odd_ref[:, span].astype(F32))
            value += arrived * before
        product += field_ref[block] * (value * scale)
    last = jnp.sum(product, axis=1, keepdims=True)
    moments = moments_in_ref[...]
    lane = lax.broadcasted_iota(jnp.int32, moments.shape, 1)
    moments = jnp.where(lane == 2 * ITERS - 1, last, moments)
    moments_ref[...] = jnp.where(lane == 2 * ITERS, unit, moments)


def lost_weight(moments):
    inner = [moments[:, order : order + 1] for order in range(4)]
    first = inner[1] / inner[0]
    norm = inner[2] - first * inner[1]
    second = (inner[3] - 2.0 * first * inner[2] + first * first * inner[1]) / norm
    trace = first + 2.0 * second
    return jnp.where((norm > 0.0) & (trace > 0.0) & (trace < 30.0), -trace, 0.0)


def part_kernel(
    index, sub_count, slot_count, lists_ref, blocks_ref, begun_ref, field_ref, even_ref, odd_ref,
    moments_in_ref, *refs
):
    *refs, total, ahead = refs
    if index == 1:
        ratios_ref, *refs, sides_ref = refs
    elif index:
        ratios_ref, sides_ref, *refs = refs
    if index + 1 == ITERS:
        lost_refs, refs = refs[: sub_count - 1], refs[sub_count - 1 :]
    part_refs, kept_refs = refs[:sub_count], refs[sub_count:]
    if index + 1 < ITERS:
        moments_ref, *kept_refs = kept_refs
        moments_ref[...] = moments_in_ref[...]
    block_len = blocks_ref.shape[1]
    sub_index, blocks_dev, own_first, tile_blocks = device_place(block_len, part_refs[0], sub_count)
    is_odd = lax.axis_index("tile") % 2 == 1
    if index == 1:
        points_dev = blocks_dev * block_len
        even = even_ref[:, points_dev:].astype(F32)
        odd = odd_ref[:, points_dev:].astype(F32)
        tile_unit = ratios_ref[:, sub_count * LANES :]
        sides = [side / tile_unit for side in neighbours(is_odd, even, odd)]
        sides_ref[...] = jnp.concatenate(sides, axis=1)
    elif index:
        sides = [sides_ref[:, :LANES], sides_ref[:, LANES:]]
    if index:
        before, after = [widen(raised(side, index), block_len) for side in sides]
    for block in range(blocks_dev):
        span = slice(block * block_len, (block + 1) * block_len)
        even = even_ref[:, span].astype(F32)
        odd = odd_ref[:, span].astype(F32)
        products, first_row = neighbours(is_odd, even, odd)
        ahead[block] = first_row * after if index else first_row
        total[block] = begun_ref[block] + (products * before if index else products)
    for block in range(blocks_dev, tile_blocks):
        total[block] = begun_ref[block]
    total[begun_ref.shape[0] - 1] = jnp.zeros(total.shape[1:], F32)
    add_products(lists_ref, blocks_ref, slot_count, ahead, total, FROM_AHEAD, SHORT_GROUP, tile_blocks, 0)
    if index + 1 == ITERS:
        weight = lost_weight(moments_in_ref[...]) * ratios_ref[:, :1]
    for step in range(sub_count):
        first = (sub_index ^ step) * blocks_dev
        for block in range(blocks_dev):
            span = slice(block * block_len, (block + 1) * block_len)
            value = total[first + block]
            if step and index + 1 == ITERS:
                value += weight * lost_refs[step - 1][:, span]
            rounded = value.astype(part_refs[step].dtype)
            part_refs[step][:, span] = rounded
            if step and kept_refs:
                kept_refs[step - 1][:, span] = value - rounded.astype(F32)


def join_kernel(index, after_ref, unit_ref, ratios_ref, own_ref, old_ref, moments_in_ref, *refs):
    part_refs = refs[:-3]
    next_ref, rounded_ref, moments_ref = refs[-3:]
    points_dev = own_ref.shape[1]
    value = own_ref[...]
    for part_ref in part_refs:
        value += part_ref[...].astype(F32)
    unit = unit_ref[...]
    divisor = raised(ratios_ref[:, :LANES], index) * unit if index else unit
    value = value * widen(1.0 / divisor, points_dev)
    next_ref[...] = value
    rounded_ref[:, :points_dev] = value.astype(BF16)
    if index == 0:
        rounded_ref[:, points_dev:] = unit.astype(BF16)
    old = old_ref[...]
    lane = lax.broadcasted_iota(jnp.int32, moments_ref.shape, 1)
    moments = moments_in_ref[...] if index else jnp.zeros(moments_ref.shape, F32)
    found = {2 * index + 1: old * value, 2 * index + 2: value * value}
    if index == 0:
        found[0] = old * old
    for order, product in found.items():
        moments = jnp.where(lane == order, jnp.sum(product, axis=1, keepdims=True), moments)
    moments_ref[...] = moments


def add_moments_kernel(first_ref, second_ref, sum_ref):
    unit_lane = 2 * ITERS
    lane = lax.broadcasted_iota(jnp.int32, sum_ref.shape, 1)
    units = [ref[:, unit_lane : unit_lane + 1] for ref in (first_ref, second_ref)]
    larger = jnp.maximum(units[0], units[1])
    result = jnp.zeros(sum_ref.shape, F32)
    for ref, unit in zip((first_ref, second_ref), units):
        ratio = unit / larger
        value = ref[...]
        for order in range(1, unit_lane):
            value = jnp.where(lane >= order, value * ratio, value)
        result += value
    sum_ref[...] = jnp.where(lane == unit_lane, larger, result)


def finish_kernel(sub_count, moments_ref, unit_ref, ratios_ref, *refs):
    part_refs, basis_refs = refs[:sub_count], refs[sub_count:-5]
    outs, (solution_ref, residual_ref, sems) = refs[-5:-3], refs[-3:]
    moments = [moments_ref[:, order : order + 1] for order in range(2 * ITERS)]
    largest = moments_ref[:, 2 * ITERS : 2 * ITERS + 1]
    unit = unit_ref[:, :1]
    ratio = unit / largest

    def inner(first, second, shift):
        value = 0.0
        for i, a in enumerate(first):
            for j, b in enumerate(second):
                value = value + a * b * moments[i + j + shift]
        return value

    one = jnp.ones_like(moments[0])
    zero = jnp.zeros_like(one)
    direction, residual = [one], [one]
    answer = [zero] * ITERS
    norm_now = moments[0]
    for iteration in range(ITERS):
        step_size = norm_now / inner(direction, direction, 1)
        for power, weight in enumerate(direction):
            answer[power] = answer[power] + step_size * weight
        residual = residual + [zero]
        for power, weight in enumerate(direction):
            residual[power + 1] = residual[power + 1] - step_size * weight
        if iteration + 1 < ITERS:
            norm_next = inner(residual, residual, 0)
            direction = [
                value + (norm_next / norm_now) * old
                for value, old in zip(residual, direction + [zero])
            ]
            norm_now = norm_next
    for order in range(1, ITERS + 1):
        scale = raised(ratio, order)
        if order < ITERS:
            answer[order] = answer[order] * scale
        else:
            scale = scale / (raised(ratios_ref[:, :1], ITERS - 1) * unit)
        residual[order] = residual[order] * scale
    answer = [weight / largest for weight in answer]
    size = solution_ref.shape[1] // QUARTERS
    copies = []
    for quarter in range(QUARTERS):
        span = slice(quarter * size, (quarter + 1) * size)
        fields = [basis_ref[:, span] for basis_ref in basis_refs]
        fields.append(sum(part_ref[:, span].astype(F32) for part_ref in part_refs))
        for index, (ref, weights) in enumerate(((solution_ref, answer), (residual_ref, residual))):
            ref[:, span] = sum(weight * field for weight, field in zip(weights, fields))
            copy = pltpu.make_async_copy(ref.at[:, span], outs[index].at[:, span], sems.at[index, quarter])
            copy.start()
            copies.append(copy)
    for copy in copies:
        copy.wait()


def shape(rows, columns, kind):
    return jax.ShapeDtypeStruct((rows, columns), kind)


def exchange(block, axis, step):
    count = lax.axis_size(axis)
    return lax.ppermute(block, axis, [(i, i ^ step) for i in range(count)])


def swap(block, axis, first):
    count = lax.axis_size(axis)
    route = []
    for i in range(first, count - 1, 2):
        route += [(i, i + 1), (i + 1, i)]
    return lax.ppermute(block, axis, route)


def call(kernel, outs, ins, name, cost=0, **options):
    single = not isinstance(outs, tuple)
    specs = [SMEM if value.dtype == jnp.int32 else VMEM for value in ins]
    options.setdefault("in_specs", specs)
    options.setdefault("out_specs", VMEM if single else (VMEM,) * len(outs))
    return pl.pallas_call(
        kernel,
        out_shape=outs,
        compiler_params=PARAMS,
        name=name,
        cost_estimate=pl.CostEstimate(flops=int(cost * 1e9), bytes_accessed=0, transcendentals=0),
        **options,
    )(*ins)


def on_device(right_side, point_order, noise_var, block_pairs, pair_blocks, diag_blocks):
    sub_count = lax.axis_size("sub")
    tile_count = lax.axis_size("tile")
    rhs_count, points_dev = right_side.shape
    blocks_dev, block_len = diag_blocks.shape[:2]
    extended = (sub_count + 1) * blocks_dev
    noise = noise_var[None, :]
    full = shape(rhs_count, points_dev, F32)
    half = shape(rhs_count, points_dev, BF16)
    scalars = shape(rhs_count, LANES, F32)
    sums = jax.ShapeDtypeStruct((extended + 1, rhs_count, block_len), F32)

    def scratch(blocks):
        return pltpu.VMEM((blocks, rhs_count, block_len), F32)

    slot_count = pair_blocks.shape[0]
    width = -(-slot_count // LANES) * LANES
    assert 2 * width <= 256 and extended < 256 and slot_count % TURN_GROUP == 0
    lists_shape = (1, len(KINDS) * list_stride(slot_count) + 2 * LANES)
    lists = call(
        functools.partial(lists_kernel, sub_count, blocks_dev, slot_count),
        pltpu.SMEM(lists_shape, jnp.int32),
        (block_pairs.T,),
        "lists",
        1,
        in_specs=[VMEM],
        out_specs=SMEM,
        scratch_shapes=[
            pltpu.VMEM((8, width), F32),
            pltpu.VMEM(lists_shape, jnp.int32),
            pltpu.SemaphoreType.DMA(()),
        ],
    )
    field, rounded = call(
        order_kernel,
        (full, half),
        [pltpu.with_memory_space_constraint(value, pltpu.HBM) for value in (right_side, point_order)],
        "curve_order",
        10,
        in_specs=[pl.BlockSpec(memory_space=pltpu.HBM)] * 2,
        scratch_shapes=[
            pltpu.VMEM(right_side.shape, F32),
            pltpu.VMEM(point_order.shape, jnp.int32),
            pltpu.SemaphoreType.DMA((2,)),
        ],
    )
    blocks = pair_blocks
    basis = [field]
    moments = jnp.zeros(scalars.shape, F32)
    ratios = sides = ()
    for index in range(ITERS):
        is_last = index + 1 == ITERS
        rows = [exchange(rounded, "sub", step) for step in range(1, sub_count)]
        begun = call(
            functools.partial(early_kernel, index, sub_count, slot_count),
            sums,
            (lists, blocks, *((diag_blocks, noise, field) if index else ()), rounded),
            "early",
            3,
            scratch_shapes=[scratch(extended)],
        )
        message = shape(rhs_count, points_dev + LANES, BF16) if index == 1 else half
        even, odd, tile_field, *found = call(
            functools.partial(ahead_kernel, index, sub_count, slot_count),
            (message, message, jax.ShapeDtypeStruct((sub_count * blocks_dev, rhs_count, block_len), F32))
            + ((shape(rhs_count, (sub_count + 1) * LANES, F32),) if index == 1 else ()),
            (lists, blocks, begun, *ratios, rounded, *rows),
            "ahead",
            1,
            scratch_shapes=[scratch(blocks_dev + 1)],
        )
        ratios = ratios or tuple(found)
        even = swap(even, "tile", 0)
        odd = swap(odd, "tile", 1)
        begun = call(
            functools.partial(late_kernel, index, slot_count),
            sums,
            (lists, blocks, begun, tile_field, *ratios),
            "late",
            3,
        )
        if is_last:
            curved = call(
                curvature_kernel,
                scalars,
                (begun, tile_field, even, odd, moments, unit, *ratios, *sides),
                "curvature",
            )
        part = shape(rhs_count, points_dev, F32 if is_last else BF16)
        found = call(
            functools.partial(part_kernel, index, sub_count, slot_count),
            (full,)
            + (part,) * (sub_count - 1)
            + (() if is_last else (scalars,))
            + ((full,) * (sub_count - 1) if index + 2 == ITERS else ())
            + ((shape(rhs_count, 2 * LANES, F32),) if index == 1 else ()),
            (lists, blocks, begun, tile_field, even, odd, moments, *ratios, *sides, *(lost if is_last else ())),
            "parts",
            1,
            scratch_shapes=[scratch(extended + 1), scratch(blocks_dev)],
        )
        parts = list(found[:sub_count])
        if not is_last:
            moments = found[sub_count]
        if index == 1:
            sides = (found[-1],)
        lost = found[sub_count + 1 : 2 * sub_count]
        if is_last:
            break
        if index == 0:
            blocks = call(
                turn_kernel,
                pltpu.VMEM((2 * slot_count, block_len, block_len), BF16),
                (pair_blocks, moments),
                "turn",
                4,
                scratch_shapes=[pltpu.SemaphoreType.DMA(())],
            )
            own_sum, unit = call(
                own_kernel, (full, scalars), (moments, diag_blocks, noise, field, rounded), "own", 0.5
            )
        arrived = [exchange(parts[step], "sub", step) for step in range(sub_count - 1, 0, -1)]
        if index == 0:
            arrived.append(own_sum)
        field, rounded, moments = call(
            functools.partial(join_kernel, index),
            (full, half if index else shape(rhs_count, points_dev + LANES, BF16), scalars),
            (blocks, unit, *(ratios or (unit,)), parts[0], field, moments, *arrived),
            "join",
        )
        basis.append(field)
    moments = curved
    arrived = []
    for axis, count in (("sub", sub_count), ("tile", tile_count)):
        step = 1
        while step < count:
            moments = call(add_moments_kernel, scalars, (moments, exchange(moments, axis, step)), "add_moments")
            if len(arrived) < sub_count - 1:
                far = sub_count - 1 - len(arrived)
                arrived.append(exchange(parts[far], "sub", far))
                moments, *parts = lax.optimization_barrier((moments, *parts))
            step *= 2
    for far in range(sub_count - 1 - len(arrived), 0, -1):
        arrived.append(exchange(parts[far], "sub", far))
    return call(
        functools.partial(finish_kernel, sub_count),
        (full, full),
        (moments, unit, *ratios, parts[0], *arrived, *basis),
        "finish",
        out_specs=(pl.BlockSpec(memory_space=pltpu.HBM),) * 2,
        scratch_shapes=[
            pltpu.VMEM(right_side.shape, F32),
            pltpu.VMEM(right_side.shape, F32),
            pltpu.SemaphoreType.DMA((2, QUARTERS)),
        ],
    )


def solution(mesh):
    placed = (
        P(None, ("tile", "sub")),
        P(("tile", "sub"), None),
        P(("tile", "sub")),
        P(("tile", "sub"), None),
        P(("tile", "sub"), None, None),
        P(("tile", "sub"), None, None),
    )
    return jax.shard_map(
        on_device,
        mesh=mesh,
        in_specs=placed,
        out_specs=(P(None, ("tile", "sub")), P(None, ("tile", "sub"))),
        check_vma=False,
    )
```

```python
import functools

import jax
import jax.numpy as jnp
from jax import lax
from jax.experimental import pallas as pl
from jax.experimental.pallas import tpu as pltpu
from jax.sharding import PartitionSpec as P

ITERS = 3
LANES = 128
LONG_GROUP = 16
SHORT_GROUP = 8
TURN_GROUP = 24
TURN_PRODUCTS = 6
QUARTERS = 4
F32 = jnp.float32
BF16 = jnp.bfloat16
VMEM = pl.BlockSpec(memory_space=pltpu.VMEM)
SMEM = pl.BlockSpec(memory_space=pltpu.SMEM)
EARLY, AHEAD, LATE, FROM_AHEAD = KINDS = range(4)
PARAMS = pltpu.CompilerParams(vmem_limit_bytes=4 * 1024 * 1024)


def times(field, block):
    return lax.dot_general(field, block, (((1,), (0,)), ((), ())), preferred_element_type=F32)


def times_transposed(field, block):
    return lax.dot_general(field, block, (((1,), (1,)), ((), ())), preferred_element_type=F32)


def order_kernel(right_in, order_in, curve_ref, rounded_ref, right_ref, order_ref, sems):
    copies = [
        pltpu.make_async_copy(right_in, right_ref, sems.at[0]),
        pltpu.make_async_copy(order_in, order_ref, sems.at[1]),
    ]
    for copy in copies:
        copy.start()
    for copy in copies:
        copy.wait()
    rhs_count, points = right_ref.shape
    for start in range(0, points, LANES):
        at = jnp.broadcast_to(order_ref[:, start : start + LANES], (rhs_count, LANES))
        chunk = at // LANES
        lane = at % LANES
        result = jnp.zeros((rhs_count, LANES), F32)
        for source in range(points // LANES):
            values = right_ref[:, source * LANES : (source + 1) * LANES]
            picked = jnp.take_along_axis(values, lane, axis=1)
            result = jnp.where(chunk == source, picked, result)
        curve_ref[:, start : start + LANES] = result
        rounded_ref[:, start : start + LANES] = result.astype(BF16)


def device_place(block_len, field_ref, sub_count):
    blocks_dev = field_ref.shape[1] // block_len
    sub_index = lax.axis_index("sub")
    return sub_index, blocks_dev, sub_index * blocks_dev, blocks_dev * sub_count


def list_stride(slot_count):
    return -(-(2 * slot_count + LONG_GROUP) // LANES) * LANES


def lists_kernel(sub_count, blocks_dev, slot_count, pairs_ref, out_ref, padded, lists_ref, sem):
    width = padded.shape[1]
    stride = list_stride(slot_count)
    sub_index = lax.axis_index("sub")
    tile_blocks = blocks_dev * sub_count
    first_block = lax.axis_index("tile") * tile_blocks
    padded[...] = jnp.full(padded.shape, -1.0, F32)
    padded[0:2, 0:slot_count] = pairs_ref[...].astype(F32)
    by_lane = padded[...]
    by_row = jnp.transpose(by_lane)

    def sides(row, col, axis):
        live = jnp.concatenate([row, row], axis) >= 0.0
        row = row.astype(jnp.int32) - first_block
        col = col.astype(jnp.int32) - first_block
        source = jnp.concatenate([row, col], axis)
        target = jnp.concatenate([col, row], axis)
        return live, source, target

    live, source, target = sides(by_row[:, 0:1], by_row[:, 1:2], 0)
    kind = jnp.where(target >= tile_blocks, AHEAD, LATE)
    first_own = sub_index * blocks_dev
    is_early = (source >= first_own) & (source < first_own + blocks_dev)
    kind = jnp.where(is_early, EARLY, kind)
    kind = jnp.where(source >= tile_blocks, FROM_AHEAD, kind)
    kind = jnp.where(live, kind, -1)
    hot = (kind == lax.broadcasted_iota(jnp.int32, (2 * width, LANES), 1)).astype(F32)
    below = lax.broadcasted_iota(jnp.int32, (2 * width, 2 * width), 0) > lax.broadcasted_iota(
        jnp.int32, (2 * width, 2 * width), 1
    )
    ranks = times(below.astype(F32).astype(BF16), hot.astype(BF16))
    rank = jnp.sum(ranks * hot, axis=1, keepdims=True).astype(jnp.int32)
    counts = jnp.sum(hot, axis=0, keepdims=True)
    at = jnp.where(live, kind * stride + rank, -1)
    spread = at == lax.broadcasted_iota(jnp.int32, (2 * width, len(KINDS) * stride), 1)
    live, source, target = sides(by_lane[0:1, :], by_lane[1:2, :], 1)
    lane = lax.broadcasted_iota(jnp.int32, (1, 2 * width), 1)
    block = jnp.where(lane < width, lane, lane - width + slot_count)
    fields = jnp.concatenate(
        [jnp.where(live, value, 0).astype(F32) for value in (block, source, target)]
        + [jnp.zeros((5, 2 * width), F32)],
        0,
    )
    found = times(fields.astype(BF16), spread.astype(F32).astype(BF16))
    entries = found[0:1] + 256.0 * found[1:2] + 65536.0 * found[2:3]
    entries = entries.astype(jnp.int32)
    idle = (tile_blocks + blocks_dev) * 65536
    idle_source = {
        EARLY: sub_index * blocks_dev,
        AHEAD: tile_blocks - blocks_dev,
        LATE: 0,
        FROM_AHEAD: tile_blocks,
    }
    place = lax.broadcasted_iota(jnp.int32, (1, stride), 1)
    for index in KINDS:
        span = slice(index * stride, (index + 1) * stride)
        count = counts[:, index : index + 1].astype(jnp.int32)
        lists_ref[:, span] = jnp.where(place < count, entries[:, span], idle + 256 * idle_source[index])
    lists_ref[:, len(KINDS) * stride : len(KINDS) * stride + LANES] = counts.astype(jnp.int32)
    by_column = jnp.sum(hot[:width], axis=0, keepdims=True)
    lists_ref[:, len(KINDS) * stride + LANES :] = by_column.astype(jnp.int32)
    copy = pltpu.make_async_copy(lists_ref, out_ref, sem)
    copy.start()
    copy.wait()


def turn_kernel(pairs_blocks_ref, after_ref, blocks_ref, sem):
    slot_count = pairs_blocks_ref.shape[0]
    copy = pltpu.make_async_copy(pairs_blocks_ref, blocks_ref.at[pl.ds(0, slot_count)], sem)
    copy.start()

    square = blocks_ref.shape[1:]
    identity = lax.broadcasted_iota(jnp.int32, square, 0) == lax.broadcasted_iota(jnp.int32, square, 1)
    identity = identity.astype(F32).astype(BF16)

    def one_group(group, carry):
        for step in range(TURN_GROUP):
            slot = group * TURN_GROUP + step
            block = pairs_blocks_ref[slot]
            if step < TURN_GROUP - TURN_PRODUCTS:
                turned = jnp.transpose(block)
            else:
                turned = times_transposed(identity, block).astype(BF16)
            blocks_ref[slot_count + slot] = turned
        return carry

    lax.fori_loop(0, slot_count // TURN_GROUP, one_group, 0)
    copy.wait()


def add_products(lists_ref, blocks_ref, slot_count, field, total, index, size, source_from=0, target_from=0):
    stride = list_stride(slot_count)
    idle = lists_ref[0, index * stride + stride - 1] >> 16
    count = lists_ref[0, len(KINDS) * stride + index]
    column_count = lists_ref[0, len(KINDS) * stride + LANES + index]

    def add_part(first, end, kind, plain, cuts):
        def one_group(group, carry):
            results = []
            for step in range(size):
                place = first + group * size + step
                entry = lists_ref[0, index * stride + place]
                block, source, target = entry & 255, (entry >> 8) & 255, entry >> 16
                if plain:
                    block = jnp.where(block >= slot_count, block - slot_count, block)
                if cuts:
                    target = jnp.where(place < end, target, idle)
                value = kind(field[source - source_from].astype(BF16), blocks_ref[block])
                results.append((target - target_from, value))
            for at, value in results:
                total[at] += value
            return carry

        lax.fori_loop(0, (end - first + size - 1) // size, one_group, 0)

    if blocks_ref.shape[0] > slot_count:
        add_part(0, count, times, False, False)
    else:
        add_part(0, column_count, times, True, True)
        add_part(column_count, count, times_transposed, True, False)


def raised(value, exponent):
    result = value
    for _ in range(exponent - 1):
        result = result * value
    return result


def widen(tile, columns):
    return jnp.concatenate([tile] * (columns // LANES), axis=1)


def lay_out(row_ref, field, first, blocks_dev, block_len, factor=None):
    for block in range(blocks_dev):
        piece = row_ref[:, block * block_len : (block + 1) * block_len].astype(F32)
        field[first + block] = piece if factor is None else piece * factor


def own_products(diag_ref, noise_ref, own_ref, rounded, block):
    block_len = diag_ref.shape[1]
    span = slice(block * block_len, (block + 1) * block_len)
    return noise_ref[:, span] * own_ref[:, span] + times(rounded, diag_ref[block])


def early_kernel(index, sub_count, slot_count, lists_ref, blocks_ref, *refs):
    *refs, rounded_ref, total, field = refs
    block_len = blocks_ref.shape[1]
    blocks_dev = rounded_ref.shape[1] // block_len
    own_first = lax.axis_index("sub") * blocks_dev
    lay_out(rounded_ref, field, own_first, blocks_dev, block_len)
    for block in range(total.shape[0]):
        total[block] = jnp.zeros(total.shape[1:], F32)
    if index:
        for block in range(blocks_dev):
            total[own_first + block] = own_products(*refs, field[own_first + block].astype(BF16), block)
    add_products(lists_ref, blocks_ref, slot_count, field, total, EARLY, LONG_GROUP)


def own_kernel(after_ref, diag_ref, noise_ref, own_ref, rounded_ref, sum_ref, unit_ref):
    blocks_dev, block_len = diag_ref.shape[:2]
    largest = diag_ref[0].astype(F32)
    for block in range(1, blocks_dev):
        largest = jnp.maximum(largest, diag_ref[block].astype(F32))
    unit_ref[...] = jnp.full(unit_ref.shape, jnp.maximum(jnp.max(largest) * block_len, 1.0))
    for block in range(blocks_dev):
        span = slice(block * block_len, (block + 1) * block_len)
        sum_ref[:, span] = own_products(diag_ref, noise_ref, own_ref, rounded_ref[:, span], block)


def ahead_kernel(index, sub_count, slot_count, lists_ref, blocks_ref, begun_ref, *refs):
    if index == 1:
        *refs, ratios_ref, total = refs
        row_refs, (even_ref, odd_ref, field_ref) = refs[:-3], refs[-3:]
        points_dev = even_ref.shape[1] - LANES
        units = [row_ref[:, points_dev:].astype(F32) for row_ref in row_refs]
        tile_unit = functools.reduce(jnp.maximum, units)
        ratios = [unit / tile_unit for unit in units]
        ratios_ref[...] = jnp.concatenate(ratios + [tile_unit], axis=1)
    else:
        row_refs, (even_ref, odd_ref, field_ref, total) = refs[:-4], refs[-4:]
        points_dev = even_ref.shape[1]
        if index:
            ratios_ref, *row_refs = row_refs
            ratios = [ratios_ref[:, step * LANES : (step + 1) * LANES] for step in range(sub_count)]
    block_len = blocks_ref.shape[1]
    blocks_dev = points_dev // block_len
    tile_blocks = blocks_dev * sub_count
    sub_index = lax.axis_index("sub")
    for step, row_ref in enumerate(row_refs):
        factor = widen(raised(ratios[step], index), block_len) if index else None
        lay_out(row_ref, field_ref, (sub_index ^ step) * blocks_dev, blocks_dev, block_len, factor)
    for block in range(blocks_dev):
        value = begun_ref[tile_blocks + block]
        total[block] = value * widen(raised(ratios[0], index), block_len) if index else value
    total[blocks_dev] = jnp.zeros(total.shape[1:], F32)
    add_products(lists_ref, blocks_ref, slot_count, field_ref, total, AHEAD, SHORT_GROUP, 0, tile_blocks)
    is_odd = lax.axis_index("tile") % 2 == 1
    for block in range(blocks_dev):
        span = slice(block * block_len, (block + 1) * block_len)
        products = total[block]
        first_row = field_ref[block]
        even_ref[:, span] = jnp.where(is_odd, first_row, products).astype(BF16)
        odd_ref[:, span] = jnp.where(is_odd, products, first_row).astype(BF16)
    if index == 1:
        even_ref[:, points_dev:] = tile_unit.astype(BF16)
        odd_ref[:, points_dev:] = tile_unit.astype(BF16)


def late_kernel(index, slot_count, lists_ref, blocks_ref, begun_ref, field_ref, *refs):
    total = refs[-1]
    if index:
        factor = widen(raised(refs[0][:, :LANES], index), total.shape[2])
        for block in range(total.shape[0]):
            total[block] = begun_ref[block] * factor
    else:
        total[...] = begun_ref[...]
    add_products(lists_ref, blocks_ref, slot_count, field_ref, total, LATE, LONG_GROUP)


def neighbours(is_odd, even, odd):
    return jnp.where(is_odd, even, odd), jnp.where(is_odd, odd, even)


def curvature_kernel(
    begun_ref, field_ref, even_ref, odd_ref, moments_in_ref, unit_ref, ratios_ref, sides_ref, moments_ref
):
    index = ITERS - 1
    block_len = begun_ref.shape[2]
    blocks_dev = even_ref.shape[1] // block_len
    is_odd = lax.axis_index("tile") % 2 == 1
    unit = unit_ref[...]
    scale = widen(1.0 / (raised(ratios_ref[:, :LANES], 2 * index) * unit), block_len)
    before = widen(2.0 * raised(sides_ref[:, :LANES], index), block_len)
    product = jnp.zeros(begun_ref.shape[1:], F32)
    for block in range(field_ref.shape[0]):
        value = begun_ref[block]
        if block < blocks_dev:
            span = slice(block * block_len, (block + 1) * block_len)
            arrived, _ = neighbours(is_odd, even_ref[:, span].astype(F32), odd_ref[:, span].astype(F32))
            value += arrived * before
        product += field_ref[block] * (value * scale)
    last = jnp.sum(product, axis=1, keepdims=True)
    moments = moments_in_ref[...]
    lane = lax.broadcasted_iota(jnp.int32, moments.shape, 1)
    moments = jnp.where(lane == 2 * ITERS - 1, last, moments)
    moments_ref[...] = jnp.where(lane == 2 * ITERS, unit, moments)


def lost_weight(moments):
    inner = [moments[:, order : order + 1] for order in range(4)]
    first = inner[1] / inner[0]
    norm = inner[2] - first * inner[1]
    second = (inner[3] - 2.0 * first * inner[2] + first * first * inner[1]) / norm
    trace = first + 2.0 * second
    return jnp.where((norm > 0.0) & (trace > 0.0) & (trace < 30.0), -trace, 0.0)


def part_kernel(
    index, sub_count, slot_count, lists_ref, blocks_ref, begun_ref, field_ref, even_ref, odd_ref,
    moments_in_ref, *refs
):
    *refs, total, ahead = refs
    if index == 1:
        ratios_ref, *refs, sides_ref = refs
    elif index:
        ratios_ref, sides_ref, *refs = refs
    if index + 1 == ITERS:
        lost_refs, refs = refs[: sub_count - 1], refs[sub_count - 1 :]
    part_refs, kept_refs = refs[:sub_count], refs[sub_count:]
    if index + 1 < ITERS:
        moments_ref, *kept_refs = kept_refs
        moments_ref[...] = moments_in_ref[...]
    block_len = blocks_ref.shape[1]
    sub_index, blocks_dev, own_first, tile_blocks = device_place(block_len, part_refs[0], sub_count)
    is_odd = lax.axis_index("tile") % 2 == 1
    if index == 1:
        points_dev = blocks_dev * block_len
        even = even_ref[:, points_dev:].astype(F32)
        odd = odd_ref[:, points_dev:].astype(F32)
        tile_unit = ratios_ref[:, sub_count * LANES :]
        sides = [side / tile_unit for side in neighbours(is_odd, even, odd)]
        sides_ref[...] = jnp.concatenate(sides, axis=1)
    elif index:
        sides = [sides_ref[:, :LANES], sides_ref[:, LANES:]]
    if index:
        before, after = [widen(raised(side, index), block_len) for side in sides]
    for block in range(blocks_dev):
        span = slice(block * block_len, (block + 1) * block_len)
        even = even_ref[:, span].astype(F32)
        odd = odd_ref[:, span].astype(F32)
        products, first_row = neighbours(is_odd, even, odd)
        ahead[block] = first_row * after if index else first_row
        total[block] = begun_ref[block] + (products * before if index else products)
    for block in range(blocks_dev, tile_blocks):
        total[block] = begun_ref[block]
    total[begun_ref.shape[0] - 1] = jnp.zeros(total.shape[1:], F32)
    add_products(lists_ref, blocks_ref, slot_count, ahead, total, FROM_AHEAD, SHORT_GROUP, tile_blocks, 0)
    if index + 1 == ITERS:
        weight = lost_weight(moments_in_ref[...]) * ratios_ref[:, :1]
    for step in range(sub_count):
        first = (sub_index ^ step) * blocks_dev
        for block in range(blocks_dev):
            span = slice(block * block_len, (block + 1) * block_len)
            value = total[first + block]
            if step and index + 1 == ITERS:
                value += weight * lost_refs[step - 1][:, span]
            rounded = value.astype(part_refs[step].dtype)
            part_refs[step][:, span] = rounded
            if step and kept_refs:
                kept_refs[step - 1][:, span] = value - rounded.astype(F32)


def join_kernel(index, after_ref, unit_ref, ratios_ref, own_ref, old_ref, moments_in_ref, *refs):
    part_refs = refs[:-3]
    next_ref, rounded_ref, moments_ref = refs[-3:]
    points_dev = own_ref.shape[1]
    value = own_ref[...]
    for part_ref in part_refs:
        value += part_ref[...].astype(F32)
    unit = unit_ref[...]
    divisor = raised(ratios_ref[:, :LANES], index) * unit if index else unit
    value = value * widen(1.0 / divisor, points_dev)
    next_ref[...] = value
    rounded_ref[:, :points_dev] = value.astype(BF16)
    if index == 0:
        rounded_ref[:, points_dev:] = unit.astype(BF16)
    old = old_ref[...]
    lane = lax.broadcasted_iota(jnp.int32, moments_ref.shape, 1)
    moments = moments_in_ref[...] if index else jnp.zeros(moments_ref.shape, F32)
    found = {2 * index + 1: old * value, 2 * index + 2: value * value}
    if index == 0:
        found[0] = old * old
    for order, product in found.items():
        moments = jnp.where(lane == order, jnp.sum(product, axis=1, keepdims=True), moments)
    moments_ref[...] = moments


def add_moments_kernel(first_ref, second_ref, sum_ref):
    unit_lane = 2 * ITERS
    lane = lax.broadcasted_iota(jnp.int32, sum_ref.shape, 1)
    units = [ref[:, unit_lane : unit_lane + 1] for ref in (first_ref, second_ref)]
    larger = jnp.maximum(units[0], units[1])
    result = jnp.zeros(sum_ref.shape, F32)
    for ref, unit in zip((first_ref, second_ref), units):
        ratio = unit / larger
        value = ref[...]
        for order in range(1, unit_lane):
            value = jnp.where(lane >= order, value * ratio, value)
        result += value
    sum_ref[...] = jnp.where(lane == unit_lane, larger, result)


def finish_kernel(sub_count, moments_ref, unit_ref, ratios_ref, *refs):
    part_refs, basis_refs = refs[:sub_count], refs[sub_count:-5]
    outs, (solution_ref, residual_ref, sems) = refs[-5:-3], refs[-3:]
    moments = [moments_ref[:, order : order + 1] for order in range(2 * ITERS)]
    largest = moments_ref[:, 2 * ITERS : 2 * ITERS + 1]
    unit = unit_ref[:, :1]
    ratio = unit / largest

    def inner(first, second, shift):
        value = 0.0
        for i, a in enumerate(first):
            for j, b in enumerate(second):
                value = value + a * b * moments[i + j + shift]
        return value

    one = jnp.ones_like(moments[0])
    zero = jnp.zeros_like(one)
    direction, residual = [one], [one]
    answer = [zero] * ITERS
    norm_now = moments[0]
    for iteration in range(ITERS):
        step_size = norm_now / inner(direction, direction, 1)
        for power, weight in enumerate(direction):
            answer[power] = answer[power] + step_size * weight
        residual = residual + [zero]
        for power, weight in enumerate(direction):
            residual[power + 1] = residual[power + 1] - step_size * weight
        if iteration + 1 < ITERS:
            norm_next = inner(residual, residual, 0)
            direction = [
                value + (norm_next / norm_now) * old
                for value, old in zip(residual, direction + [zero])
            ]
            norm_now = norm_next
    for order in range(1, ITERS + 1):
        scale = raised(ratio, order)
        if order < ITERS:
            answer[order] = answer[order] * scale
        else:
            scale = scale / (raised(ratios_ref[:, :1], ITERS - 1) * unit)
        residual[order] = residual[order] * scale
    answer = [weight / largest for weight in answer]
    size = solution_ref.shape[1] // QUARTERS
    copies = []
    for quarter in range(QUARTERS):
        span = slice(quarter * size, (quarter + 1) * size)
        fields = [basis_ref[:, span] for basis_ref in basis_refs]
        fields.append(sum(part_ref[:, span].astype(F32) for part_ref in part_refs))
        for index, (ref, weights) in enumerate(((solution_ref, answer), (residual_ref, residual))):
            ref[:, span] = sum(weight * field for weight, field in zip(weights, fields))
            copy = pltpu.make_async_copy(ref.at[:, span], outs[index].at[:, span], sems.at[index, quarter])
            copy.start()
            copies.append(copy)
    for copy in copies:
        copy.wait()


def shape(rows, columns, kind):
    return jax.ShapeDtypeStruct((rows, columns), kind)


def exchange(block, axis, step):
    count = lax.axis_size(axis)
    return lax.ppermute(block, axis, [(i, i ^ step) for i in range(count)])


def swap(block, axis, first):
    count = lax.axis_size(axis)
    route = []
    for i in range(first, count - 1, 2):
        route += [(i, i + 1), (i + 1, i)]
    return lax.ppermute(block, axis, route)


def call(kernel, outs, ins, name, cost=0, **options):
    single = not isinstance(outs, tuple)
    specs = [SMEM if value.dtype == jnp.int32 else VMEM for value in ins]
    options.setdefault("in_specs", specs)
    options.setdefault("out_specs", VMEM if single else (VMEM,) * len(outs))
    return pl.pallas_call(
        kernel,
        out_shape=outs,
        compiler_params=PARAMS,
        name=name,
        cost_estimate=pl.CostEstimate(flops=int(cost * 1e9), bytes_accessed=0, transcendentals=0),
        **options,
    )(*ins)


def on_device(right_side, point_order, noise_var, block_pairs, pair_blocks, diag_blocks):
    sub_count = lax.axis_size("sub")
    tile_count = lax.axis_size("tile")
    rhs_count, points_dev = right_side.shape
    blocks_dev, block_len = diag_blocks.shape[:2]
    extended = (sub_count + 1) * blocks_dev
    noise = noise_var[None, :]
    full = shape(rhs_count, points_dev, F32)
    half = shape(rhs_count, points_dev, BF16)
    scalars = shape(rhs_count, LANES, F32)
    sums = jax.ShapeDtypeStruct((extended + 1, rhs_count, block_len), F32)

    def scratch(blocks):
        return pltpu.VMEM((blocks, rhs_count, block_len), F32)

    slot_count = pair_blocks.shape[0]
    width = -(-slot_count // LANES) * LANES
    assert 2 * width <= 256 and extended < 256 and slot_count % TURN_GROUP == 0
    lists_shape = (1, len(KINDS) * list_stride(slot_count) + 2 * LANES)
    lists = call(
        functools.partial(lists_kernel, sub_count, blocks_dev, slot_count),
        pltpu.SMEM(lists_shape, jnp.int32),
        (block_pairs.T,),
        "lists",
        1,
        in_specs=[VMEM],
        out_specs=SMEM,
        scratch_shapes=[
            pltpu.VMEM((8, width), F32),
            pltpu.VMEM(lists_shape, jnp.int32),
            pltpu.SemaphoreType.DMA(()),
        ],
    )
    field, rounded = call(
        order_kernel,
        (full, half),
        [pltpu.with_memory_space_constraint(value, pltpu.HBM) for value in (right_side, point_order)],
        "curve_order",
        10,
        in_specs=[pl.BlockSpec(memory_space=pltpu.HBM)] * 2,
        scratch_shapes=[
            pltpu.VMEM(right_side.shape, F32),
            pltpu.VMEM(point_order.shape, jnp.int32),
            pltpu.SemaphoreType.DMA((2,)),
        ],
    )
    blocks = pair_blocks
    basis = [field]
    moments = jnp.zeros(scalars.shape, F32)
    ratios = sides = ()
    for index in range(ITERS):
        is_last = index + 1 == ITERS
        rows = [exchange(rounded, "sub", step) for step in range(1, sub_count)]
        begun = call(
            functools.partial(early_kernel, index, sub_count, slot_count),
            sums,
            (lists, blocks, *((diag_blocks, noise, field) if index else ()), rounded),
            "early",
            3,
            scratch_shapes=[scratch(extended)],
        )
        message = shape(rhs_count, points_dev + LANES, BF16) if index == 1 else half
        even, odd, tile_field, *found = call(
            functools.partial(ahead_kernel, index, sub_count, slot_count),
            (message, message, jax.ShapeDtypeStruct((sub_count * blocks_dev, rhs_count, block_len), F32))
            + ((shape(rhs_count, (sub_count + 1) * LANES, F32),) if index == 1 else ()),
            (lists, blocks, begun, *ratios, rounded, *rows),
            "ahead",
            1,
            scratch_shapes=[scratch(blocks_dev + 1)],
        )
        ratios = ratios or tuple(found)
        even = swap(even, "tile", 0)
        odd = swap(odd, "tile", 1)
        begun = call(
            functools.partial(late_kernel, index, slot_count),
            sums,
            (lists, blocks, begun, tile_field, *ratios),
            "late",
            3,
        )
        if is_last:
            curved = call(
                curvature_kernel,
                scalars,
                (begun, tile_field, even, odd, moments, unit, *ratios, *sides),
                "curvature",
            )
        part = shape(rhs_count, points_dev, F32 if is_last else BF16)
        found = call(
            functools.partial(part_kernel, index, sub_count, slot_count),
            (full,)
            + (part,) * (sub_count - 1)
            + (() if is_last else (scalars,))
            + ((full,) * (sub_count - 1) if index + 2 == ITERS else ())
            + ((shape(rhs_count, 2 * LANES, F32),) if index == 1 else ()),
            (lists, blocks, begun, tile_field, even, odd, moments, *ratios, *sides, *(lost if is_last else ())),
            "parts",
            1,
            scratch_shapes=[scratch(extended + 1), scratch(blocks_dev)],
        )
        parts = list(found[:sub_count])
        if not is_last:
            moments = found[sub_count]
        if index == 1:
            sides = (found[-1],)
        lost = found[sub_count + 1 : 2 * sub_count]
        if is_last:
            break
        if index == 0:
            blocks = call(
                turn_kernel,
                pltpu.VMEM((2 * slot_count, block_len, block_len), BF16),
                (pair_blocks, moments),
                "turn",
                4,
                scratch_shapes=[pltpu.SemaphoreType.DMA(())],
            )
            own_sum, unit = call(
                own_kernel, (full, scalars), (moments, diag_blocks, noise, field, rounded), "own", 0.5
            )
        arrived = [exchange(parts[step], "sub", step) for step in range(sub_count - 1, 0, -1)]
        if index == 0:
            arrived.append(own_sum)
        field, rounded, moments = call(
            functools.partial(join_kernel, index),
            (full, half if index else shape(rhs_count, points_dev + LANES, BF16), scalars),
            (blocks, unit, *(ratios or (unit,)), parts[0], field, moments, *arrived),
            "join",
        )
        basis.append(field)
    moments = curved
    arrived = []
    for axis, count in (("tile", tile_count), ("sub", sub_count)):
        step = 1
        while step < count:
            moments = call(add_moments_kernel, scalars, (moments, exchange(moments, axis, step)), "add_moments")
            if len(arrived) < sub_count - 1:
                far = sub_count - 1 - len(arrived)
                arrived.append(exchange(parts[far], "sub", far))
                moments, *parts = lax.optimization_barrier((moments, *parts))
            step *= 2
    for far in range(sub_count - 1 - len(arrived), 0, -1):
        arrived.append(exchange(parts[far], "sub", far))
    return call(
        functools.partial(finish_kernel, sub_count),
        (full, full),
        (moments, unit, *ratios, parts[0], *arrived, *basis),
        "finish",
        out_specs=(pl.BlockSpec(memory_space=pltpu.HBM),) * 2,
        scratch_shapes=[
            pltpu.VMEM(right_side.shape, F32),
            pltpu.VMEM(right_side.shape, F32),
            pltpu.SemaphoreType.DMA((2, QUARTERS)),
        ],
    )


def solution(mesh):
    placed = (
        P(None, ("tile", "sub")),
        P(("tile", "sub"), None),
        P(("tile", "sub")),
        P(("tile", "sub"), None),
        P(("tile", "sub"), None, None),
        P(("tile", "sub"), None, None),
    )
    return jax.shard_map(
        on_device,
        mesh=mesh,
        in_specs=placed,
        out_specs=(P(None, ("tile", "sub")), P(None, ("tile", "sub"))),
        check_vma=False,
    )
```

```python
import functools

import jax
import jax.numpy as jnp
from jax import lax
from jax.experimental import pallas as pl
from jax.experimental.pallas import tpu as pltpu
from jax.sharding import PartitionSpec as P

ITERS = 3
LANES = 128
LONG_GROUP = 16
SHORT_GROUP = 8
TURN_GROUP = 32
TURN_PRODUCTS = 10
QUARTERS = 4
F32 = jnp.float32
BF16 = jnp.bfloat16
VMEM = pl.BlockSpec(memory_space=pltpu.VMEM)
SMEM = pl.BlockSpec(memory_space=pltpu.SMEM)
EARLY, AHEAD, LATE, FROM_AHEAD = KINDS = range(4)
PARAMS = pltpu.CompilerParams(vmem_limit_bytes=4 * 1024 * 1024)


def times(field, block):
    return lax.dot_general(field, block, (((1,), (0,)), ((), ())), preferred_element_type=F32)


def times_transposed(field, block):
    return lax.dot_general(field, block, (((1,), (1,)), ((), ())), preferred_element_type=F32)


def order_kernel(right_in, order_in, curve_ref, rounded_ref, right_ref, order_ref, sems):
    copies = [
        pltpu.make_async_copy(right_in, right_ref, sems.at[0]),
        pltpu.make_async_copy(order_in, order_ref, sems.at[1]),
    ]
    for copy in copies:
        copy.start()
    for copy in copies:
        copy.wait()
    rhs_count, points = right_ref.shape
    for start in range(0, points, LANES):
        at = jnp.broadcast_to(order_ref[:, start : start + LANES], (rhs_count, LANES))
        chunk = at // LANES
        lane = at % LANES
        result = jnp.zeros((rhs_count, LANES), F32)
        for source in range(points // LANES):
            values = right_ref[:, source * LANES : (source + 1) * LANES]
            picked = jnp.take_along_axis(values, lane, axis=1)
            result = jnp.where(chunk == source, picked, result)
        curve_ref[:, start : start + LANES] = result
        rounded_ref[:, start : start + LANES] = result.astype(BF16)


def device_place(block_len, field_ref, sub_count):
    blocks_dev = field_ref.shape[1] // block_len
    sub_index = lax.axis_index("sub")
    return sub_index, blocks_dev, sub_index * blocks_dev, blocks_dev * sub_count


def list_stride(slot_count):
    return -(-(2 * slot_count + LONG_GROUP) // LANES) * LANES


def lists_kernel(sub_count, blocks_dev, slot_count, pairs_ref, out_ref, padded, lists_ref, sem):
    width = padded.shape[1]
    stride = list_stride(slot_count)
    sub_index = lax.axis_index("sub")
    tile_blocks = blocks_dev * sub_count
    first_block = lax.axis_index("tile") * tile_blocks
    padded[...] = jnp.full(padded.shape, -1.0, F32)
    padded[0:2, 0:slot_count] = pairs_ref[...].astype(F32)
    by_lane = padded[...]
    by_row = jnp.transpose(by_lane)

    def sides(row, col, axis):
        live = jnp.concatenate([row, row], axis) >= 0.0
        row = row.astype(jnp.int32) - first_block
        col = col.astype(jnp.int32) - first_block
        source = jnp.concatenate([row, col], axis)
        target = jnp.concatenate([col, row], axis)
        return live, source, target

    live, source, target = sides(by_row[:, 0:1], by_row[:, 1:2], 0)
    kind = jnp.where(target >= tile_blocks, AHEAD, LATE)
    first_own = sub_index * blocks_dev
    is_early = (source >= first_own) & (source < first_own + blocks_dev)
    kind = jnp.where(is_early, EARLY, kind)
    kind = jnp.where(source >= tile_blocks, FROM_AHEAD, kind)
    kind = jnp.where(live, kind, -1)
    hot = (kind == lax.broadcasted_iota(jnp.int32, (2 * width, LANES), 1)).astype(F32)
    below = lax.broadcasted_iota(jnp.int32, (2 * width, 2 * width), 0) > lax.broadcasted_iota(
        jnp.int32, (2 * width, 2 * width), 1
    )
    ranks = times(below.astype(F32).astype(BF16), hot.astype(BF16))
    rank = jnp.sum(ranks * hot, axis=1, keepdims=True).astype(jnp.int32)
    counts = jnp.sum(hot, axis=0, keepdims=True)
    at = jnp.where(live, kind * stride + rank, -1)
    spread = at == lax.broadcasted_iota(jnp.int32, (2 * width, len(KINDS) * stride), 1)
    live, source, target = sides(by_lane[0:1, :], by_lane[1:2, :], 1)
    lane = lax.broadcasted_iota(jnp.int32, (1, 2 * width), 1)
    block = jnp.where(lane < width, lane, lane - width + slot_count)
    fields = jnp.concatenate(
        [jnp.where(live, value, 0).astype(F32) for value in (block, source, target)]
        + [jnp.zeros((5, 2 * width), F32)],
        0,
    )
    found = times(fields.astype(BF16), spread.astype(F32).astype(BF16))
    entries = found[0:1] + 256.0 * found[1:2] + 65536.0 * found[2:3]
    entries = entries.astype(jnp.int32)
    idle = (tile_blocks + blocks_dev) * 65536
    idle_source = {
        EARLY: sub_index * blocks_dev,
        AHEAD: tile_blocks - blocks_dev,
        LATE: 0,
        FROM_AHEAD: tile_blocks,
    }
    place = lax.broadcasted_iota(jnp.int32, (1, stride), 1)
    for index in KINDS:
        span = slice(index * stride, (index + 1) * stride)
        count = counts[:, index : index + 1].astype(jnp.int32)
        lists_ref[:, span] = jnp.where(place < count, entries[:, span], idle + 256 * idle_source[index])
    lists_ref[:, len(KINDS) * stride : len(KINDS) * stride + LANES] = counts.astype(jnp.int32)
    by_column = jnp.sum(hot[:width], axis=0, keepdims=True)
    lists_ref[:, len(KINDS) * stride + LANES :] = by_column.astype(jnp.int32)
    copy = pltpu.make_async_copy(lists_ref, out_ref, sem)
    copy.start()
    copy.wait()


def turn_kernel(pairs_blocks_ref, after_ref, blocks_ref, sem):
    slot_count = pairs_blocks_ref.shape[0]
    copy = pltpu.make_async_copy(pairs_blocks_ref, blocks_ref.at[pl.ds(0, slot_count)], sem)
    copy.start()

    square = blocks_ref.shape[1:]
    identity = lax.broadcasted_iota(jnp.int32, square, 0) == lax.broadcasted_iota(jnp.int32, square, 1)
    identity = identity.astype(F32).astype(BF16)

    def one_group(group, carry):
        for step in range(TURN_GROUP):
            slot = group * TURN_GROUP + step
            block = pairs_blocks_ref[slot]
            if step < TURN_GROUP - TURN_PRODUCTS:
                turned = jnp.transpose(block)
            else:
                turned = times_transposed(identity, block).astype(BF16)
            blocks_ref[slot_count + slot] = turned
        return carry

    lax.fori_loop(0, slot_count // TURN_GROUP, one_group, 0)
    copy.wait()


def add_products(lists_ref, blocks_ref, slot_count, field, total, index, size, source_from=0, target_from=0):
    stride = list_stride(slot_count)
    idle = lists_ref[0, index * stride + stride - 1] >> 16
    count = lists_ref[0, len(KINDS) * stride + index]
    column_count = lists_ref[0, len(KINDS) * stride + LANES + index]

    def add_part(first, end, kind, plain, cuts):
        def one_group(group, carry):
            results = []
            for step in range(size):
                place = first + group * size + step
                entry = lists_ref[0, index * stride + place]
                block, source, target = entry & 255, (entry >> 8) & 255, entry >> 16
                if plain:
                    block = jnp.where(block >= slot_count, block - slot_count, block)
                if cuts:
                    target = jnp.where(place < end, target, idle)
                value = kind(field[source - source_from].astype(BF16), blocks_ref[block])
                results.append((target - target_from, value))
            for at, value in results:
                total[at] += value
            return carry

        lax.fori_loop(0, (end - first + size - 1) // size, one_group, 0)

    if blocks_ref.shape[0] > slot_count:
        add_part(0, count, times, False, False)
    else:
        add_part(0, column_count, times, True, True)
        add_part(column_count, count, times_transposed, True, False)


def raised(value, exponent):
    result = value
    for _ in range(exponent - 1):
        result = result * value
    return result


def widen(tile, columns):
    return jnp.concatenate([tile] * (columns // LANES), axis=1)


def lay_out(row_ref, field, first, blocks_dev, block_len, factor=None):
    for block in range(blocks_dev):
        piece = row_ref[:, block * block_len : (block + 1) * block_len].astype(F32)
        field[first + block] = piece if factor is None else piece * factor


def own_products(diag_ref, noise_ref, own_ref, rounded, block):
    block_len = diag_ref.shape[1]
    span = slice(block * block_len, (block + 1) * block_len)
    return noise_ref[:, span] * own_ref[:, span] + times(rounded, diag_ref[block])


def early_kernel(index, sub_count, slot_count, lists_ref, blocks_ref, *refs):
    *refs, rounded_ref, total, field = refs
    block_len = blocks_ref.shape[1]
    blocks_dev = rounded_ref.shape[1] // block_len
    own_first = lax.axis_index("sub") * blocks_dev
    lay_out(rounded_ref, field, own_first, blocks_dev, block_len)
    for block in range(total.shape[0]):
        total[block] = jnp.zeros(total.shape[1:], F32)
    if index:
        for block in range(blocks_dev):
            total[own_first + block] = own_products(*refs, field[own_first + block].astype(BF16), block)
    add_products(lists_ref, blocks_ref, slot_count, field, total, EARLY, LONG_GROUP)


def own_kernel(after_ref, diag_ref, noise_ref, own_ref, rounded_ref, sum_ref, unit_ref):
    blocks_dev, block_len = diag_ref.shape[:2]
    largest = diag_ref[0].astype(F32)
    for block in range(1, blocks_dev):
        largest = jnp.maximum(largest, diag_ref[block].astype(F32))
    unit_ref[...] = jnp.full(unit_ref.shape, jnp.maximum(jnp.max(largest) * block_len, 1.0))
    for block in range(blocks_dev):
        span = slice(block * block_len, (block + 1) * block_len)
        sum_ref[:, span] = own_products(diag_ref, noise_ref, own_ref, rounded_ref[:, span], block)


def ahead_kernel(index, sub_count, slot_count, lists_ref, blocks_ref, begun_ref, *refs):
    if index == 1:
        *refs, ratios_ref, total = refs
        row_refs, (even_ref, odd_ref, field_ref) = refs[:-3], refs[-3:]
        points_dev = even_ref.shape[1] - LANES
        units = [row_ref[:, points_dev:].astype(F32) for row_ref in row_refs]
        tile_unit = functools.reduce(jnp.maximum, units)
        ratios = [unit / tile_unit for unit in units]
        ratios_ref[...] = jnp.concatenate(ratios + [tile_unit], axis=1)
    else:
        row_refs, (even_ref, odd_ref, field_ref, total) = refs[:-4], refs[-4:]
        points_dev = even_ref.shape[1]
        if index:
            ratios_ref, *row_refs = row_refs
            ratios = [ratios_ref[:, step * LANES : (step + 1) * LANES] for step in range(sub_count)]
    block_len = blocks_ref.shape[1]
    blocks_dev = points_dev // block_len
    tile_blocks = blocks_dev * sub_count
    sub_index = lax.axis_index("sub")
    for step, row_ref in enumerate(row_refs):
        factor = widen(raised(ratios[step], index), block_len) if index else None
        lay_out(row_ref, field_ref, (sub_index ^ step) * blocks_dev, blocks_dev, block_len, factor)
    for block in range(blocks_dev):
        value = begun_ref[tile_blocks + block]
        total[block] = value * widen(raised(ratios[0], index), block_len) if index else value
    total[blocks_dev] = jnp.zeros(total.shape[1:], F32)
    add_products(lists_ref, blocks_ref, slot_count, field_ref, total, AHEAD, SHORT_GROUP, 0, tile_blocks)
    is_odd = lax.axis_index("tile") % 2 == 1
    for block in range(blocks_dev):
        span = slice(block * block_len, (block + 1) * block_len)
        products = total[block]
        first_row = field_ref[block]
        even_ref[:, span] = jnp.where(is_odd, first_row, products).astype(BF16)
        odd_ref[:, span] = jnp.where(is_odd, products, first_row).astype(BF16)
    if index == 1:
        even_ref[:, points_dev:] = tile_unit.astype(BF16)
        odd_ref[:, points_dev:] = tile_unit.astype(BF16)


def late_kernel(index, slot_count, lists_ref, blocks_ref, begun_ref, field_ref, *refs):
    total = refs[-1]
    if index:
        factor = widen(raised(refs[0][:, :LANES], index), total.shape[2])
        for block in range(total.shape[0]):
            total[block] = begun_ref[block] * factor
    else:
        total[...] = begun_ref[...]
    add_products(lists_ref, blocks_ref, slot_count, field_ref, total, LATE, LONG_GROUP)


def neighbours(is_odd, even, odd):
    return jnp.where(is_odd, even, odd), jnp.where(is_odd, odd, even)


def curvature_kernel(
    begun_ref, field_ref, even_ref, odd_ref, moments_in_ref, unit_ref, ratios_ref, sides_ref, moments_ref
):
    index = ITERS - 1
    block_len = begun_ref.shape[2]
    blocks_dev = even_ref.shape[1] // block_len
    is_odd = lax.axis_index("tile") % 2 == 1
    unit = unit_ref[...]
    scale = widen(1.0 / (raised(ratios_ref[:, :LANES], 2 * index) * unit), block_len)
    before = widen(2.0 * raised(sides_ref[:, :LANES], index), block_len)
    product = jnp.zeros(begun_ref.shape[1:], F32)
    for block in range(field_ref.shape[0]):
        value = begun_ref[block]
        if block < blocks_dev:
            span = slice(block * block_len, (block + 1) * block_len)
            arrived, _ = neighbours(is_odd, even_ref[:, span].astype(F32), odd_ref[:, span].astype(F32))
            value += arrived * before
        product += field_ref[block] * (value * scale)
    last = jnp.sum(product, axis=1, keepdims=True)
    moments = moments_in_ref[...]
    lane = lax.broadcasted_iota(jnp.int32, moments.shape, 1)
    moments = jnp.where(lane == 2 * ITERS - 1, last, moments)
    moments_ref[...] = jnp.where(lane == 2 * ITERS, unit, moments)


def lost_weight(moments):
    inner = [moments[:, order : order + 1] for order in range(4)]
    first = inner[1] / inner[0]
    norm = inner[2] - first * inner[1]
    second = (inner[3] - 2.0 * first * inner[2] + first * first * inner[1]) / norm
    trace = first + 2.0 * second
    return jnp.where((norm > 0.0) & (trace > 0.0) & (trace < 30.0), -trace, 0.0)


def part_kernel(
    index, sub_count, slot_count, lists_ref, blocks_ref, begun_ref, field_ref, even_ref, odd_ref,
    moments_in_ref, *refs
):
    *refs, total, ahead = refs
    if index == 1:
        ratios_ref, *refs, sides_ref = refs
    elif index:
        ratios_ref, sides_ref, *refs = refs
    if index + 1 == ITERS:
        lost_refs, refs = refs[: sub_count - 1], refs[sub_count - 1 :]
    part_refs, kept_refs = refs[:sub_count], refs[sub_count:]
    if index + 1 < ITERS:
        moments_ref, *kept_refs = kept_refs
        moments_ref[...] = moments_in_ref[...]
    block_len = blocks_ref.shape[1]
    sub_index, blocks_dev, own_first, tile_blocks = device_place(block_len, part_refs[0], sub_count)
    is_odd = lax.axis_index("tile") % 2 == 1
    if index == 1:
        points_dev = blocks_dev * block_len
        even = even_ref[:, points_dev:].astype(F32)
        odd = odd_ref[:, points_dev:].astype(F32)
        tile_unit = ratios_ref[:, sub_count * LANES :]
        sides = [side / tile_unit for side in neighbours(is_odd, even, odd)]
        sides_ref[...] = jnp.concatenate(sides, axis=1)
    elif index:
        sides = [sides_ref[:, :LANES], sides_ref[:, LANES:]]
    if index:
        before, after = [widen(raised(side, index), block_len) for side in sides]
    for block in range(blocks_dev):
        span = slice(block * block_len, (block + 1) * block_len)
        even = even_ref[:, span].astype(F32)
        odd = odd_ref[:, span].astype(F32)
        products, first_row = neighbours(is_odd, even, odd)
        ahead[block] = first_row * after if index else first_row
        total[block] = begun_ref[block] + (products * before if index else products)
    for block in range(blocks_dev, tile_blocks):
        total[block] = begun_ref[block]
    total[begun_ref.shape[0] - 1] = jnp.zeros(total.shape[1:], F32)
    add_products(lists_ref, blocks_ref, slot_count, ahead, total, FROM_AHEAD, SHORT_GROUP, tile_blocks, 0)
    if index + 1 == ITERS:
        weight = lost_weight(moments_in_ref[...]) * ratios_ref[:, :1]
    for step in range(sub_count):
        first = (sub_index ^ step) * blocks_dev
        for block in range(blocks_dev):
            span = slice(block * block_len, (block + 1) * block_len)
            value = total[first + block]
            if step and index + 1 == ITERS:
                value += weight * lost_refs[step - 1][:, span]
            rounded = value.astype(part_refs[step].dtype)
            part_refs[step][:, span] = rounded
            if step and kept_refs:
                kept_refs[step - 1][:, span] = value - rounded.astype(F32)


def join_kernel(index, after_ref, unit_ref, ratios_ref, own_ref, old_ref, moments_in_ref, *refs):
    part_refs = refs[:-3]
    next_ref, rounded_ref, moments_ref = refs[-3:]
    points_dev = own_ref.shape[1]
    value = own_ref[...]
    for part_ref in part_refs:
        value += part_ref[...].astype(F32)
    unit = unit_ref[...]
    divisor = raised(ratios_ref[:, :LANES], index) * unit if index else unit
    value = value * widen(1.0 / divisor, points_dev)
    next_ref[...] = value
    rounded_ref[:, :points_dev] = value.astype(BF16)
    if index == 0:
        rounded_ref[:, points_dev:] = unit.astype(BF16)
    old = old_ref[...]
    lane = lax.broadcasted_iota(jnp.int32, moments_ref.shape, 1)
    moments = moments_in_ref[...] if index else jnp.zeros(moments_ref.shape, F32)
    found = {2 * index + 1: old * value, 2 * index + 2: value * value}
    if index == 0:
        found[0] = old * old
    for order, product in found.items():
        moments = jnp.where(lane == order, jnp.sum(product, axis=1, keepdims=True), moments)
    moments_ref[...] = moments


def add_moments_kernel(first_ref, second_ref, sum_ref):
    unit_lane = 2 * ITERS
    lane = lax.broadcasted_iota(jnp.int32, sum_ref.shape, 1)
    units = [ref[:, unit_lane : unit_lane + 1] for ref in (first_ref, second_ref)]
    larger = jnp.maximum(units[0], units[1])
    result = jnp.zeros(sum_ref.shape, F32)
    for ref, unit in zip((first_ref, second_ref), units):
        ratio = unit / larger
        value = ref[...]
        for order in range(1, unit_lane):
            value = jnp.where(lane >= order, value * ratio, value)
        result += value
    sum_ref[...] = jnp.where(lane == unit_lane, larger, result)


def finish_kernel(sub_count, moments_ref, unit_ref, ratios_ref, *refs):
    part_refs, basis_refs = refs[:sub_count], refs[sub_count:-5]
    outs, (solution_ref, residual_ref, sems) = refs[-5:-3], refs[-3:]
    moments = [moments_ref[:, order : order + 1] for order in range(2 * ITERS)]
    largest = moments_ref[:, 2 * ITERS : 2 * ITERS + 1]
    unit = unit_ref[:, :1]
    ratio = unit / largest

    def inner(first, second, shift):
        value = 0.0
        for i, a in enumerate(first):
            for j, b in enumerate(second):
                value = value + a * b * moments[i + j + shift]
        return value

    one = jnp.ones_like(moments[0])
    zero = jnp.zeros_like(one)
    direction, residual = [one], [one]
    answer = [zero] * ITERS
    norm_now = moments[0]
    for iteration in range(ITERS):
        step_size = norm_now / inner(direction, direction, 1)
        for power, weight in enumerate(direction):
            answer[power] = answer[power] + step_size * weight
        residual = residual + [zero]
        for power, weight in enumerate(direction):
            residual[power + 1] = residual[power + 1] - step_size * weight
        if iteration + 1 < ITERS:
            norm_next = inner(residual, residual, 0)
            direction = [
                value + (norm_next / norm_now) * old
                for value, old in zip(residual, direction + [zero])
            ]
            norm_now = norm_next
    for order in range(1, ITERS + 1):
        scale = raised(ratio, order)
        if order < ITERS:
            answer[order] = answer[order] * scale
        else:
            scale = scale / (raised(ratios_ref[:, :1], ITERS - 1) * unit)
        residual[order] = residual[order] * scale
    answer = [weight / largest for weight in answer]
    size = solution_ref.shape[1] // QUARTERS
    copies = []
    for quarter in range(QUARTERS):
        span = slice(quarter * size, (quarter + 1) * size)
        fields = [basis_ref[:, span] for basis_ref in basis_refs]
        fields.append(sum(part_ref[:, span].astype(F32) for part_ref in part_refs))
        for index, (ref, weights) in enumerate(((solution_ref, answer), (residual_ref, residual))):
            ref[:, span] = sum(weight * field for weight, field in zip(weights, fields))
            copy = pltpu.make_async_copy(ref.at[:, span], outs[index].at[:, span], sems.at[index, quarter])
            copy.start()
            copies.append(copy)
    for copy in copies:
        copy.wait()


def shape(rows, columns, kind):
    return jax.ShapeDtypeStruct((rows, columns), kind)


def exchange(block, axis, step):
    count = lax.axis_size(axis)
    return lax.ppermute(block, axis, [(i, i ^ step) for i in range(count)])


def swap(block, axis, first):
    count = lax.axis_size(axis)
    route = []
    for i in range(first, count - 1, 2):
        route += [(i, i + 1), (i + 1, i)]
    return lax.ppermute(block, axis, route)


def call(kernel, outs, ins, name, cost=0, **options):
    single = not isinstance(outs, tuple)
    specs = [SMEM if value.dtype == jnp.int32 else VMEM for value in ins]
    options.setdefault("in_specs", specs)
    options.setdefault("out_specs", VMEM if single else (VMEM,) * len(outs))
    return pl.pallas_call(
        kernel,
        out_shape=outs,
        compiler_params=PARAMS,
        name=name,
        cost_estimate=pl.CostEstimate(flops=int(cost * 1e9), bytes_accessed=0, transcendentals=0),
        **options,
    )(*ins)


def on_device(right_side, point_order, noise_var, block_pairs, pair_blocks, diag_blocks):
    sub_count = lax.axis_size("sub")
    tile_count = lax.axis_size("tile")
    rhs_count, points_dev = right_side.shape
    blocks_dev, block_len = diag_blocks.shape[:2]
    extended = (sub_count + 1) * blocks_dev
    noise = noise_var[None, :]
    full = shape(rhs_count, points_dev, F32)
    half = shape(rhs_count, points_dev, BF16)
    scalars = shape(rhs_count, LANES, F32)
    sums = jax.ShapeDtypeStruct((extended + 1, rhs_count, block_len), F32)

    def scratch(blocks):
        return pltpu.VMEM((blocks, rhs_count, block_len), F32)

    slot_count = pair_blocks.shape[0]
    width = -(-slot_count // LANES) * LANES
    assert 2 * width <= 256 and extended < 256 and slot_count % TURN_GROUP == 0
    lists_shape = (1, len(KINDS) * list_stride(slot_count) + 2 * LANES)
    lists = call(
        functools.partial(lists_kernel, sub_count, blocks_dev, slot_count),
        pltpu.SMEM(lists_shape, jnp.int32),
        (block_pairs.T,),
        "lists",
        1,
        in_specs=[VMEM],
        out_specs=SMEM,
        scratch_shapes=[
            pltpu.VMEM((8, width), F32),
            pltpu.VMEM(lists_shape, jnp.int32),
            pltpu.SemaphoreType.DMA(()),
        ],
    )
    field, rounded = call(
        order_kernel,
        (full, half),
        [pltpu.with_memory_space_constraint(value, pltpu.HBM) for value in (right_side, point_order)],
        "curve_order",
        10,
        in_specs=[pl.BlockSpec(memory_space=pltpu.HBM)] * 2,
        scratch_shapes=[
            pltpu.VMEM(right_side.shape, F32),
            pltpu.VMEM(point_order.shape, jnp.int32),
            pltpu.SemaphoreType.DMA((2,)),
        ],
    )
    blocks = pair_blocks
    basis = [field]
    moments = jnp.zeros(scalars.shape, F32)
    ratios = sides = ()
    for index in range(ITERS):
        is_last = index + 1 == ITERS
        rows = [exchange(rounded, "sub", step) for step in range(1, sub_count)]
        begun = call(
            functools.partial(early_kernel, index, sub_count, slot_count),
            sums,
            (lists, blocks, *((diag_blocks, noise, field) if index else ()), rounded),
            "early",
            3,
            scratch_shapes=[scratch(extended)],
        )
        message = shape(rhs_count, points_dev + LANES, BF16) if index == 1 else half
        even, odd, tile_field, *found = call(
            functools.partial(ahead_kernel, index, sub_count, slot_count),
            (message, message, jax.ShapeDtypeStruct((sub_count * blocks_dev, rhs_count, block_len), F32))
            + ((shape(rhs_count, (sub_count + 1) * LANES, F32),) if index == 1 else ()),
            (lists, blocks, begun, *ratios, rounded, *rows),
            "ahead",
            1,
            scratch_shapes=[scratch(blocks_dev + 1)],
        )
        ratios = ratios or tuple(found)
        even = swap(even, "tile", 0)
        odd = swap(odd, "tile", 1)
        begun = call(
            functools.partial(late_kernel, index, slot_count),
            sums,
            (lists, blocks, begun, tile_field, *ratios),
            "late",
            3,
        )
        if is_last:
            curved = call(
                curvature_kernel,
                scalars,
                (begun, tile_field, even, odd, moments, unit, *ratios, *sides),
                "curvature",
            )
        part = shape(rhs_count, points_dev, F32 if is_last else BF16)
        found = call(
            functools.partial(part_kernel, index, sub_count, slot_count),
            (full,)
            + (part,) * (sub_count - 1)
            + (() if is_last else (scalars,))
            + ((full,) * (sub_count - 1) if index + 2 == ITERS else ())
            + ((shape(rhs_count, 2 * LANES, F32),) if index == 1 else ()),
            (lists, blocks, begun, tile_field, even, odd, moments, *ratios, *sides, *(lost if is_last else ())),
            "parts",
            1,
            scratch_shapes=[scratch(extended + 1), scratch(blocks_dev)],
        )
        parts = list(found[:sub_count])
        if not is_last:
            moments = found[sub_count]
        if index == 1:
            sides = (found[-1],)
        lost = found[sub_count + 1 : 2 * sub_count]
        if is_last:
            break
        if index == 0:
            blocks = call(
                turn_kernel,
                pltpu.VMEM((2 * slot_count, block_len, block_len), BF16),
                (pair_blocks, moments),
                "turn",
                4,
                scratch_shapes=[pltpu.SemaphoreType.DMA(())],
            )
            own_sum, unit = call(
                own_kernel, (full, scalars), (moments, diag_blocks, noise, field, rounded), "own", 0.5
            )
        arrived = [exchange(parts[step], "sub", step) for step in range(sub_count - 1, 0, -1)]
        if index == 0:
            arrived.append(own_sum)
        field, rounded, moments = call(
            functools.partial(join_kernel, index),
            (full, half if index else shape(rhs_count, points_dev + LANES, BF16), scalars),
            (blocks, unit, *(ratios or (unit,)), parts[0], field, moments, *arrived),
            "join",
        )
        basis.append(field)
    moments = curved
    arrived = []
    for axis, count in (("sub", sub_count), ("tile", tile_count)):
        step = 1
        while step < count:
            moments = call(add_moments_kernel, scalars, (moments, exchange(moments, axis, step)), "add_moments")
            if len(arrived) < sub_count - 1:
                far = sub_count - 1 - len(arrived)
                arrived.append(exchange(parts[far], "sub", far))
                moments, *parts = lax.optimization_barrier((moments, *parts))
            step *= 2
    for far in range(sub_count - 1 - len(arrived), 0, -1):
        arrived.append(exchange(parts[far], "sub", far))
    return call(
        functools.partial(finish_kernel, sub_count),
        (full, full),
        (moments, unit, *ratios, parts[0], *arrived, *basis),
        "finish",
        out_specs=(pl.BlockSpec(memory_space=pltpu.HBM),) * 2,
        scratch_shapes=[
            pltpu.VMEM(right_side.shape, F32),
            pltpu.VMEM(right_side.shape, F32),
            pltpu.SemaphoreType.DMA((2, QUARTERS)),
        ],
    )


def solution(mesh):
    placed = (
        P(None, ("tile", "sub")),
        P(("tile", "sub"), None),
        P(("tile", "sub")),
        P(("tile", "sub"), None),
        P(("tile", "sub"), None, None),
        P(("tile", "sub"), None, None),
    )
    return jax.shard_map(
        on_device,
        mesh=mesh,
        in_specs=placed,
        out_specs=(P(None, ("tile", "sub")), P(None, ("tile", "sub"))),
        check_vma=False,
    )
```
